32 devices in a mesh: phase: 4 (over y, x), batch: 8 (over z, core).
Axes of the slice: x: 2, y: 2, z: 4, core: 2. Of those that a mesh axis runs over, the one named last changes fastest.
Arguments:
- features: bfloat16 [256000, 256], P('batch'), may hold values from -6 to 6
- weights: bfloat16 [4, 213504], P('phase')
- crop_kind: int32 [8, 4, 5], replicated, may hold values from 0 to 3, as said below
- positives: int32 [8, 4, 5], P('batch'), may hold values from 0 to 16383
- negatives: int32 [8, 4, 5, 4096], P('batch'), may hold values from 0 to 16383
- bank: float32 [16384, 128], replicated, may hold values from -0.5 to 0.5
- normalizer: float32 [1], replicated, may hold values from 1024 to 262144
Outputs:
- weight_grads: float32 [4, 213504], P('phase')
- input_grad: bfloat16 [256000, 256], P(('batch', 'phase'))
The draws below stay inside these ranges and needn't reach their ends.
Inputs may be any that keep to these rules, and one draw needn't show every extreme that they name: `crop_kind`: 0 is an empty slot, 1, 2, 3 the crop classes; live slots come first; the input pixels of one device's micro-batch sum to at most 8000, and in every draw one device's micro-batch holds five class-1 crops filling 8000 exactly.
All inputs are finite; a program needn't handle non-finite values.
Results may differ from the reference program's by a relative error of at most 0.017.
Values may be sent and summed in bfloat16 or wider, within the bound.
A program may use at most 320 MiB of HBM per device.

```python
import math
from functools import partial
import jax
import jax.numpy as jnp
import numpy as np
from jax import lax

CIN = 256
MID = 128
COUT = 512
EMB = 128
SIDE_UNIT = 4
SLOTS = 5
MICRO = 4
NEG = 4096
BANK = 16384
PIX = 8000
GRAD_LEN = 213504
TOTAL_PIX = 256000
N_BATCH = 8


PATTERNS = np.array([[3, 0, 0, 0, 0], [3, 1, 0, 0, 0], [2, 2, 0, 0, 0], [2, 1, 1, 0, 0], [1, 1, 1, 1, 1], [2, 2, 1, 0, 0], [1, 1, 1, 1, 0], [2, 1, 1, 1, 0]], dtype=np.int32)


def layout_drawn(section):
    if section == 0:
        return (('conv_in', (CIN, MID), 0), ('gain_in', (MID,), 1), ('bias_in', (MID,), 2), ('conv_mid', (9 * MID, MID), 0), ('gain_mid', (MID,), 1), ('bias_mid', (MID,), 2))
    if section == 1:
        return (('conv_out', (MID, COUT), 0), ('gain_out', (COUT,), 1), ('bias_out', (COUT,), 2), ('shortcut', (CIN, COUT), 0), ('gain_short', (COUT,), 1), ('bias_short', (COUT,), 2))
    if section == 2:
        return (('conv_in', (COUT, MID), 0), ('gain_in', (MID,), 1), ('bias_in', (MID,), 2), ('conv_mid', (9 * MID, MID), 0), ('gain_mid', (MID,), 1), ('bias_mid', (MID,), 2))
    return (('conv_out', (MID, COUT), 0), ('gain_out', (COUT,), 1), ('bias_out', (COUT,), 2), ('head', (COUT, EMB), 0))


def draw_piece(key, shape, kind):
    if kind == 0:
        return jax.random.normal(key, shape, jnp.float32) * shape[0] ** (-0.5)
    if kind == 1:
        return 0.6 + 0.8 * jax.random.uniform(key, shape, jnp.float32)
    return 0.3 * jax.random.normal(key, shape, jnp.float32)


def draw_weights(key, part):
    key = jax.random.fold_in(key, 11)
    rows_list = []
    for section in range(4):
        pieces = []
        for number, entry in enumerate(layout_drawn(section)):
            name, shape, kind = entry
            pieces.append(draw_piece(jax.random.fold_in(key, 16 * section + number), shape, kind).reshape(-1))
        vector = jnp.concatenate(pieces)
        filler = 0.05 * jax.random.normal(jax.random.fold_in(key, 100 + section), (GRAD_LEN - vector.shape[0],), jnp.float32)
        rows_list.append(jnp.concatenate([vector, filler]))
    return jnp.stack(rows_list).astype(jnp.bfloat16)


def draw_crop_kind(key, part):
    key = jax.random.fold_in(key, 5)
    first, second, third = jax.random.split(key, 3)
    table = jnp.asarray(PATTERNS)
    picks = jax.random.randint(first, (N_BATCH, MICRO), 0, 8)
    kinds = table[picks]
    batch_pick = jax.random.randint(second, (), 0, N_BATCH)
    micro_pick = jax.random.randint(third, (), 0, MICRO)
    chosen = (jnp.arange(N_BATCH)[:, None] == batch_pick) & (jnp.arange(MICRO)[None, :] == micro_pick)
    return jnp.where(chosen[:, :, None], table[4][None, None, :], kinds).astype(jnp.int32)


def with_ends(drawn, own_key, low, top_value):
    index_at = [jax.random.randint(jax.random.fold_in(own_key, axis), (), 0, length) for axis, length in enumerate(drawn.shape)]
    widest = drawn.shape.index(max(drawn.shape))
    beside = index_at[:widest] + [(index_at[widest] + 1) % drawn.shape[widest]] + index_at[widest + 1:]
    return drawn.at[tuple(index_at)].set(low).at[tuple(beside)].set(top_value)


def level_of(stream_key, dims, cuts, low, largest):
    factor_of, own = 1.0, jax.random.fold_in(stream_key, 6)
    for axis_at, parts in cuts:
        heights = jnp.exp(jax.random.uniform(jax.random.fold_in(own, axis_at), (parts,), jnp.float32, low / len(cuts), largest / len(cuts)))
        factor_of = factor_of * jnp.repeat(heights, dims[axis_at] // parts).reshape([-1 if axis == axis_at else 1 for axis in range(len(dims))])
    return factor_of


def centred(rng, shape, scale, bound, cuts=(), held_as=jnp.bfloat16):
    level = level_of(rng, shape, cuts, -0.22, 0.18) if cuts else 1.0
    drawn = jax.random.normal(rng, shape, jnp.float32) * scale * level
    return jnp.minimum(jnp.maximum(drawn, -bound), bound).astype(held_as)


def setup_inputs(seed: int = 0) -> dict:
    splits = jax.random.split(jax.random.key(seed), 8)
    features = centred(splits[0], (TOTAL_PIX, CIN), 1.0, 6.0, ((0, 8),))
    weights = draw_weights(jax.random.fold_in(splits[7], 71), 0)
    crop_kind = draw_crop_kind(jax.random.fold_in(splits[7], 71), 0)
    positives = with_ends(jax.random.randint(splits[3], (N_BATCH, MICRO, SLOTS), 0, BANK), jax.random.fold_in(splits[3], 1), 0, BANK - 1).astype(jnp.int32)
    negatives = with_ends(jax.random.randint(splits[4], (N_BATCH, MICRO, SLOTS, NEG), 0, BANK), jax.random.fold_in(splits[4], 1), 0, BANK - 1).astype(jnp.int32)
    bank = centred(splits[5], (BANK, EMB), EMB ** -0.5, 0.5, (), jnp.float32)
    normalizer = jnp.clip(jnp.exp(jax.random.uniform(splits[6], (1,), jnp.float32, math.log(1024.0), math.log(262144.0))), 1024.0, 262144.0)
    return {"features": features, "weights": weights, "crop_kind": crop_kind, "positives": positives, "negatives": negatives, "bank": bank, "normalizer": normalizer}


@jax.custom_vjp
def low(v):
    return lax.optimization_barrier(v.astype(jnp.bfloat16)).astype(jnp.float32)

@jax.custom_vjp
def low_back(v):
    return v

def low_keep(v):
    return (low(v), None)

def low_pass(kept, grad):
    return (grad,)

def back_keep(v):
    return (v, None)

def back_low(kept, grad):
    return (low(grad),)
low.defvjp(low_keep, low_pass)
low_back.defvjp(back_keep, back_low)
SOFTMAX_TEMPER = 0.07
EPSILON = 1e-05

def layout(section):
    if section == 0:
        return (('conv_in', (CIN, MID), 0), ('gain_in', (MID,), 1), ('bias_in', (MID,), 2), ('conv_mid', (9 * MID, MID), 0), ('gain_mid', (MID,), 1), ('bias_mid', (MID,), 2))
    if section == 1:
        return (('conv_out', (MID, COUT), 0), ('gain_out', (COUT,), 1), ('bias_out', (COUT,), 2), ('shortcut', (CIN, COUT), 0), ('gain_short', (COUT,), 1), ('bias_short', (COUT,), 2))
    if section == 2:
        return (('conv_in', (COUT, MID), 0), ('gain_in', (MID,), 1), ('bias_in', (MID,), 2), ('conv_mid', (9 * MID, MID), 0), ('gain_mid', (MID,), 1), ('bias_mid', (MID,), 2))
    return (('conv_out', (MID, COUT), 0), ('gain_out', (COUT,), 1), ('bias_out', (COUT,), 2), ('head', (COUT, EMB), 0))

def unpack(flat, section):
    pieces = {}
    offset = 0
    for name, shape, kind in layout(section):
        count = 1
        for extent in shape:
            count = count * extent
        pieces[name] = flat[offset:offset + count].reshape(shape)
        offset = offset + count
    return pieces

def side_lengths(kinds):
    return (SIDE_UNIT * jnp.where(kinds == 1, 5, jnp.where(kinds == 2, 7, jnp.where(kinds == 3, 9, 0)))).astype(jnp.int32)

def geometry(kinds, out_rows):
    sides = side_lengths(kinds)
    areas = sides * sides
    starts = jnp.cumsum(areas, dtype=jnp.int32) - areas
    rows = jnp.arange(out_rows, dtype=jnp.int32)
    inside = ((rows[:, None] >= starts[None, :]) & (rows[:, None] < (starts + areas)[None, :])).astype(jnp.int32)
    live = lax.optimization_barrier(jnp.sum(inside, axis=1, dtype=jnp.int32)) > 0
    width = jnp.maximum(lax.optimization_barrier(jnp.sum(inside * sides[None, :], axis=1, dtype=jnp.int32)), 1)
    local = rows - lax.optimization_barrier(jnp.sum(inside * starts[None, :], axis=1, dtype=jnp.int32))
    base = rows - local
    return (inside, live, width, local // width, local % width, base)

def input_live(kinds, in_rows):
    sides = side_lengths(kinds)
    total = jnp.sum(sides * sides, dtype=jnp.int32)
    return jnp.arange(in_rows, dtype=jnp.int32) < 4 * total

def taps(width, row_pos, col_pos, base, live, stride):
    full = stride * width
    index_list = []
    valid_list = []
    for shift_row in range(3):
        for shift_col in range(3):
            pos_row = stride * row_pos + shift_row - 1
            pos_col = stride * col_pos + shift_col - 1
            valid = live & (pos_row >= 0) & (pos_row < full) & (pos_col >= 0) & (pos_col < full)
            index_list.append(jnp.where(valid, stride * stride * base + pos_row * full + pos_col, 0).astype(jnp.int32))
            valid_list.append(valid)
    return (jnp.stack(index_list, axis=1), jnp.stack(valid_list, axis=1))

def shortcut_index(width, row_pos, col_pos, base, live):
    return jnp.where(live, 4 * base + 4 * row_pos * width + 2 * col_pos, 0).astype(jnp.int32)

def gather_taps(source, index, valid):
    picked = jnp.take(source, index.reshape(-1), axis=0).reshape(index.shape[0], 9, source.shape[1])
    picked = picked * valid[:, :, None].astype(source.dtype)
    return picked.reshape(index.shape[0], 9 * source.shape[1])

def blended_output(pattern, left, right):
    return jnp.einsum(pattern, left, right, precision=lax.Precision.HIGHEST)

def batch_norm(values, live, gain, bias):
    mask = live.astype(jnp.float32)[..., None]
    count = jnp.sum(mask)
    mean = lax.optimization_barrier(jnp.sum(values * mask, axis=(0, 1))) / count
    square = lax.optimization_barrier(jnp.sum(values * values * mask, axis=(0, 1))) / count
    inverse = lax.rsqrt(square - mean * mean + EPSILON)
    return (values - mean) * inverse * gain + bias

def micro_loss(params, feats, kinds, pos_ids, neg_ids, bank, log_offset):
    out_rows = PIX // 4
    inside, live, width, row_pos, col_pos, base = jax.vmap(partial(geometry, out_rows=out_rows))(kinds)
    live_in = jax.vmap(partial(input_live, in_rows=PIX))(kinds)
    wide_index, wide_valid = jax.vmap(partial(taps, stride=2))(width, row_pos, col_pos, base, live)
    near_index, near_valid = jax.vmap(partial(taps, stride=1))(width, row_pos, col_pos, base, live)
    sub_index = jax.vmap(shortcut_index)(width, row_pos, col_pos, base, live)
    first, second, third, fourth = params
    conv_first = low_back(blended_output('brc,cd->brd', feats, first['conv_in']))
    hidden_one = low(jax.nn.silu(batch_norm(conv_first, live_in, first['gain_in'], first['bias_in'])))
    columns = jax.vmap(gather_taps)(hidden_one, wide_index, wide_valid)
    conv_second = low_back(blended_output('brc,cd->brd', columns, first['conv_mid']))
    hidden_two = low(low_back(jax.nn.silu(batch_norm(conv_second, live, first['gain_mid'], first['bias_mid']))))
    conv_third = low_back(blended_output('brc,cd->brd', hidden_two, second['conv_out']))
    branch = batch_norm(conv_third, live, second['gain_out'], second['bias_out'])
    picked = jax.vmap(partial(jnp.take, axis=0))(feats, sub_index) * live.astype(jnp.float32)[..., None]
    picked = low_back(picked)
    conv_short = low_back(blended_output('brc,cd->brd', picked, second['shortcut']))
    short = batch_norm(conv_short, live, second['gain_short'], second['bias_short'])
    block = low(low_back(jax.nn.silu(branch + short)))
    conv_fourth = low_back(blended_output('brc,cd->brd', block, third['conv_in']))
    hidden_three = low(jax.nn.silu(batch_norm(conv_fourth, live, third['gain_in'], third['bias_in'])))
    columns_near = jax.vmap(gather_taps)(hidden_three, near_index, near_valid)
    conv_fifth = low_back(blended_output('brc,cd->brd', columns_near, third['conv_mid']))
    hidden_four = low(low_back(jax.nn.silu(batch_norm(conv_fifth, live, third['gain_mid'], third['bias_mid']))))
    carried = low_back(block)
    conv_sixth = low_back(blended_output('brc,cd->brd', hidden_four, fourth['conv_out']))
    final = jax.nn.silu(batch_norm(conv_sixth, live, fourth['gain_out'], fourth['bias_out']) + carried)
    sides = side_lengths(kinds).astype(jnp.float32)
    share = inside.astype(jnp.float32) / jnp.maximum(sides * sides, 1.0)[:, None, :]
    pooled = blended_output('brs,brc->bsc', share, final)
    embed = blended_output('bsc,ce->bse', pooled, fourth['head'])
    unit_features = embed * lax.rsqrt(lax.optimization_barrier(jnp.sum(embed * embed, axis=-1, keepdims=True)) + 1e-06)
    logit_scores = blended_output('ngo,yo->ngy', unit_features, bank) / SOFTMAX_TEMPER
    positive = jnp.take_along_axis(logit_scores, pos_ids[..., None], axis=2)[..., 0]
    negative = jnp.take_along_axis(logit_scores, neg_ids, axis=2)
    per_crop = jax.nn.softplus(log_offset - positive) + lax.optimization_barrier(jnp.sum(jax.nn.softplus(negative - log_offset), axis=-1))
    return jnp.sum(per_crop * (kinds > 0).astype(jnp.float32))

def reference(features, weights, crop_kind, positives, negatives, bank, normalizer):
    feats = features.astype(jnp.float32).reshape(N_BATCH, MICRO, PIX, CIN)
    flat = weights.astype(jnp.float32)
    log_offset = jnp.log(normalizer[0] * NEG / BANK)

    def total_loss(flat_params, all_feats):
        params = [unpack(flat_params[section], section) for section in range(4)]
        total = jnp.zeros((), jnp.float32)
        for micro in range(MICRO):
            total = total + micro_loss(params, all_feats[:, micro], crop_kind[:, micro], positives[:, micro], negatives[:, micro], bank, log_offset)
        return total
    value, pullback = jax.vjp(total_loss, flat, feats)
    grad_flat, grad_feats = pullback(jnp.ones((), jnp.float32))
    return (grad_flat, grad_feats.reshape(N_BATCH * MICRO * PIX, CIN).astype(jnp.bfloat16))
```

```python
import functools
import math
import types

import jax
import jax.numpy as jnp
from jax import lax
from jax.experimental import pallas as pl
from jax.experimental.pallas import tpu as pltpu
from jax.sharding import PartitionSpec as P

CIN = 256
MID = 128
COUT = 512
EMB = 128
SIDE_UNIT = 4
MICRO = 4
NEG = 4096
BANK = 16384
GRAD_LEN = 213504
LANES = 128
SOFTMAX_TEMPER = 0.07
EPSILON = 1e-05

PAD = 48
ROW = GRAD_LEN // LANES
ROWS = -(-ROW // 16) * 16
BLOCK = 16
TABLE = 512
UNROLL = 5
EARLY = 272
AHEAD = 80
MESH = pl.DeviceIdType.MESH
F32 = jnp.float32
BF16 = jnp.bfloat16

IN_GAIN, IN_BIAS, MID_AT = CIN, CIN + 1, CIN + 2
MID_GAIN, MID_BIAS = MID_AT + 9 * MID, MID_AT + 9 * MID + 1
THIRD_GAIN, THIRD_BIAS, THIRD_MID = COUT, COUT + 1, COUT + 2
THIRD_MID_GAIN, THIRD_MID_BIAS = THIRD_MID + 9 * MID, THIRD_MID + 9 * MID + 1
OUT_GAIN, OUT_BIAS, AFTER_OUT = 512, 516, 520
SHORT_GAIN, SHORT_BIAS = AFTER_OUT + 1024, AFTER_OUT + 1028

EXCHANGES = 12
SPANS = {2: 16, 5: 8, 6: 8, 9: 16}
STARTS = {2: 0, 5: 16, 6: 24, 9: 32}
SPAN_ROWS = 48

PIECES = ((3, 1032), (2, 1668), (1, 1552), (0, 9 * MID), (0, 260))
LAST, THIRD, SECOND, FIRST_MID, FIRST_IN = range(5)

L1, L2, L3, LS, L4, L5, L6 = range(7)
HALF_SCALE, HALF_SHIFT, INVERSE, NEG_MEAN, GRAD_A, GRAD_E, GRAD_D = range(7)


def dense(left, right):
    return jnp.dot(left, right, preferred_element_type=F32)


def across(left, right):
    return lax.dot_general(left, right, (((1,), (1,)), ((), ())), preferred_element_type=F32)


def outer(left, right):
    return lax.dot_general(left, right, (((0,), (0,)), ((), ())), preferred_element_type=F32)


def folded(values):
    rows, width = values.shape
    return values.reshape(rows // 8, 8, width).sum(axis=0)


def silu_half(half):
    return half + half * jnp.tanh(half)


def slope_half(half):
    bend = jnp.tanh(half)
    return 0.5 * (1.0 + bend + half * (1.0 - bend * bend))


def split(values):
    high = values.astype(BF16)
    return high, (values - high.astype(F32)).astype(BF16)


def line_levels(lines):
    return [lines] if lines <= 8 else [lines // 8, 8]


def kernel(names, batches, phases, in_rows, slots, *refs):
    k = types.SimpleNamespace(**dict(zip(names, refs, strict=True)))
    out_rows = in_rows // 4
    plane = out_rows + 2 * PAD
    chunk = out_rows // 5
    part = out_rows // 25
    blocks = out_rows // BLOCK
    per = part // BLOCK
    me = lax.axis_index("batch")
    stage = lax.axis_index("phase")
    core = lax.rem(me, 2)
    line = lax.div(me, 2)
    lines = batches // 2
    group = 2 * phases
    mine = 2 * stage + core
    levels = line_levels(lines)
    half_bank = BANK // 2
    quarter = in_rows // 4
    feat, t1, big0, big1, big2, src = k.feat, k.t1, k.big0, k.big1, k.big2, k.src
    tab, masks, wst, wts, gw, wide2, gn = k.tab, k.masks, k.wst, k.wts, k.gw, k.wide2, k.gn

    def batch_peer(i):
        return {"batch": lax.rem(me + i, batches)}

    def phase_peer(i):
        return {"phase": lax.rem(stage + i, phases)}

    def remote(source, target, send_sem, recv_sem, device):
        return pltpu.make_async_remote_copy(
            src_ref=source,
            dst_ref=target,
            send_sem=send_sem,
            recv_sem=recv_sem,
            device_id=device,
            device_id_type=MESH,
        )

    def wait_for(sem, region):
        pltpu.make_async_copy(region, region, sem).wait()

    barrier = pltpu.get_barrier_semaphore()

    def greet(i, carry):
        pl.semaphore_signal(barrier, inc=1, device_id=batch_peer(i), device_id_type=MESH)
        return carry

    lax.fori_loop(1, batches, greet, 0)
    for i in range(1, phases):
        for other in (me, 2 * line + 1 - core):
            pl.semaphore_signal(
                barrier,
                inc=1,
                device_id={"phase": lax.rem(stage + i, phases), "batch": other},
                device_id_type=MESH,
            )

    raw_copy = pltpu.make_async_copy(k.weights_at, k.raw, k.raw_sem)
    raw_copy.start()
    feat_copies = []
    for i in range(4):
        copy = pltpu.make_async_copy(
            k.features_at.at[pl.ds(pl.multiple_of(stage * in_rows + i * quarter, 16), quarter)],
            feat.at[pl.ds(i * quarter, quarter)],
            k.feat_sem.at[i],
        )
        copy.start()
        feat_copies.append(copy)
    neg_copy = pltpu.make_async_copy(k.negatives_at.at[0], k.neg, k.neg_sem)
    neg_copy.start()
    bank_copies = [
        pltpu.make_async_copy(
            k.bank_at.at[pl.ds(i * half_bank, half_bank)],
            big0.at[pl.ds(0, half_bank)],
            k.bank_sem.at[i],
        )
        for i in range(2)
    ]

    def side_of(kind):
        return SIDE_UNIT * jnp.where(
            kind == 1, 5, jnp.where(kind == 2, 7, jnp.where(kind == 3, 9, 0))
        )

    sides = [side_of(k.kinds[slot, stage, me]) for slot in range(slots)]
    ends = []
    for side in sides:
        ends.append(side * side + (ends[-1] if ends else 0))
    starts = [0, *ends[:-1]]
    rows_live = ends[-1]

    def all_areas(i, carry):
        for slot in range(slots):
            side = side_of(k.kinds[slot, stage, i])
            carry = carry + side * side
        return carry

    live_pixels = lax.fori_loop(0, batches, all_areas, 0)
    inverse_count = 1.0 / jnp.full((1, LANES), live_pixels, jnp.int32).astype(F32)[:, 0:1]

    def place(first):
        base = jnp.zeros_like(first)
        width = jnp.zeros_like(first)
        slot = jnp.full_like(first, 7)
        for number in range(slots):
            inside = (first >= starts[number]) & (first < ends[number])
            base = jnp.where(inside, starts[number], base)
            width = jnp.where(inside, sides[number], width)
            slot = jnp.where(inside, number, slot)
        return base, width, slot

    def divided(value, side):
        factor = jnp.zeros_like(side)
        for kind in (5, 7, 9):
            factor = jnp.where(side == SIDE_UNIT * kind, 65536 // (SIDE_UNIT * kind) + 1, factor)
        return lax.shift_right_logical(value * factor, jnp.full_like(value, 16))

    index = lax.broadcasted_iota(jnp.int32, (1, TABLE), 1)
    first = BLOCK * index
    base, width, slot = place(first)
    live = width > 0
    local = jnp.where(live, first - base, 0)
    row = divided(local, width)
    left = jnp.where(live, (row + 1) * width - local, BLOCK)
    begin = jnp.where(live, 4 * base + 2 * (local + row * width), 4 * first)
    jump = jnp.where(left < BLOCK, 2 * width, 0)
    window_at = lax.shift_right_logical(
        index * (65536 // per + 1), jnp.full_like(index, 16)
    ) * (4 * part) - AHEAD
    in_window = begin - jnp.maximum(window_at, 0)
    pixel = BLOCK // 4 * index
    in_base, in_width, unused_slot = place(pixel)
    in_live = in_width > 0
    in_side = jnp.maximum(in_width, 1)
    in_local = 4 * (pixel - in_base)
    in_row = divided(2 * (pixel - in_base), in_width)
    in_left = jnp.where(in_live, (2 * in_side - (in_local - in_row * 2 * in_side)) >> 1, 8)
    upper = in_row >> 1
    odd = in_row - 2 * upper
    lower = (in_row + 1) >> 1
    here = in_base + upper * in_side + (in_side - in_left)
    below = in_base + lower * in_side - in_left
    at_here = jnp.where(in_live, PAD + here + odd * (2 * plane), PAD + out_rows - BLOCK)
    at_below = jnp.where(in_left < 8, PAD + below + (1 - odd) * (2 * plane), at_here)
    even_here = jnp.where(in_live & (odd == 0), PAD + here, 0)
    even_below = jnp.where(in_live & (in_left < 8) & (odd == 1), PAD + below, 0)
    columns = (width, local, begin, left, jump, slot, 2 * width)
    columns = columns + (at_here, at_below, in_left, even_here, even_below, in_window)
    for number, column in enumerate(columns):
        k.tabv[number : number + 1, :] = column
    tab_copy = pltpu.make_async_copy(k.tabv, tab, k.tab_sem)
    tab_copy.start()

    raw_copy.wait()

    def to_rows(first, last):
        def body(i, carry):
            found = []
            for u in range(16):
                at = pl.multiple_of((i * 16 + u) * LANES, LANES)
                found.append(k.raw[0:1, pl.ds(at, LANES)].astype(F32))
            for u, values in enumerate(found):
                wst[pl.ds(i * 16 + u, 1), :] = values
            return carry

        lax.fori_loop(first // 16, last // 16, body, 0)
        done = last // 16 * 16
        for at in range(done, last):
            wst[at : at + 1, :] = k.raw[0:1, at * LANES : (at + 1) * LANES].astype(F32)
        if done < last:
            wst[last : done + 16, :] = jnp.zeros((done + 16 - last, LANES), F32)

        def convert(i, carry):
            rows = pl.ds(pl.multiple_of(i * 16, 16), 16)
            wts[stage, rows, :] = wst[rows, :].astype(BF16)
            return carry

        lax.fori_loop(first // 16, -(-last // 16), convert, 0, unroll=2)

    weight_spans = ((0, EARLY), (EARLY, ROWS - EARLY))

    def send_weights(number):
        at, rows = weight_spans[number]
        region = wts.at[stage, pl.ds(at, rows)]
        copies = []
        for i in range(1, phases):
            copy = remote(
                region,
                region,
                k.weight_send.at[number, i],
                k.weight_recv.at[number, stage],
                phase_peer(i),
            )
            copy.start()
            copies.append(copy)
        return copies

    def need_weights(number, section):
        at, rows = weight_spans[number]

        @pl.when(stage != section)
        def unused_wait():
            wait_for(k.weight_recv.at[number, section], wts.at[section, pl.ds(at, rows)])

    to_rows(0, EARLY)
    pl.semaphore_wait(barrier, batches - 1 + 2 * (phases - 1))
    weight_copies = send_weights(0)

    def outgoing(number):
        if number in SPANS:
            return k.send.at[pl.ds(STARTS[number], SPANS[number])]
        return k.send_narrow.at[number]

    def incoming(number, which):
        if number in SPANS:
            return k.recv.at[which, pl.ds(STARTS[number], SPANS[number])]
        return k.recv_narrow.at[number, which]

    def share(number):
        def give(i, carry):
            remote(
                outgoing(number),
                incoming(number, me),
                k.stat_send.at[number],
                k.stat_recv.at[number],
                batch_peer(i),
            ).start()
            return carry

        lax.fori_loop(1, batches, give, 0, unroll=batches <= 8)
        incoming(number, me)[...] = outgoing(number)[...]

    def collect(number):
        wait_for(k.stat_recv.at[number], incoming(number, pl.ds(0, batches - 1)))

        def add(i, carry):
            return carry + incoming(number, i)[...]

        rows = SPANS.get(number, 2)
        k.total[pl.ds(0, rows), :] = lax.fori_loop(
            1, batches, add, incoming(number, 0)[...], unroll=batches <= 8
        )

    padded = [-(-rows // (16 * group)) * 16 * group for unused, rows in PIECES]
    piece_at = [sum(padded[:i]) for i in range(len(padded))]
    section_at = [0, 0, 0, 0, padded[FIRST_MID]]
    part_of = [rows // group for rows in padded]

    def summed(rows, target, *sources):
        total = sources[0](0, rows).astype(F32)
        for source in sources[1:]:
            total = total + source(0, rows).astype(F32)
        target(0, rows, total.astype(BF16))

    def reader(ref, start):
        return lambda at, step: ref[pl.ds(pl.multiple_of(start + at, 16), step), :]

    def writer(ref, start):
        def write(at, step, values):
            ref[pl.ds(pl.multiple_of(start + at, 16), step), :] = values

        return write

    def give_scatter(number):
        rows, at = part_of[number], piece_at[number]

        def give(i, carry):
            other = lax.rem(mine + i, group)
            remote(
                k.gb.at[pl.ds(at + other * rows, rows)],
                k.got_scatter.at[i - 1, pl.ds(at // group, rows)],
                k.scatter_send.at[number],
                k.scatter_recv.at[number],
                {"phase": lax.div(other, 2), "batch": 2 * line + lax.rem(other, 2)},
            ).start()
            return carry

        lax.fori_loop(1, group, give, 0)

    def give_line(number):
        rows, at = part_of[number], piece_at[number]
        within = at // group
        wait_for(k.scatter_recv.at[number], k.got_scatter.at[:, pl.ds(within, rows)])

        def other(i):
            return lambda start, step: k.got_scatter[i, pl.ds(within + start, step), :]

        summed(
            rows,
            writer(k.line_sum.at[0], within),
            reader(k.gb, at + mine * rows),
            *[other(i) for i in range(group - 1)],
        )
        send_level(number, 0)

    def level_of(level):
        size, stride = levels[level], math.prod(levels[:level])
        return size, stride, sum(levels[:level]) - level, lax.rem(lax.div(line, stride), size)

    def send_level(number, level):
        size, stride, slot, digit = level_of(level)
        rows, within = part_of[number], piece_at[number] // group

        def give(i, carry):
            other = line + (lax.rem(digit + i, size) - digit) * stride
            remote(
                k.line_sum.at[level, pl.ds(within, rows)],
                k.got_line.at[slot + i - 1, pl.ds(within, rows)],
                k.line_send.at[level, number],
                k.line_recv.at[level, number],
                {"batch": 2 * other + core},
            ).start()
            return carry

        lax.fori_loop(1, size, give, 0)

    def add_level(number, level, target):
        size, stride, slot, digit = level_of(level)
        rows, within = part_of[number], piece_at[number] // group
        arrived = k.got_line.at[pl.ds(slot, size - 1), pl.ds(within, rows)]
        wait_for(k.line_recv.at[level, number], arrived)

        own = k.line_sum[level, pl.ds(within, rows), :].astype(F32)
        total = jnp.zeros((rows, LANES), F32)
        for which in range(size):
            at = jnp.minimum(lax.rem(digit - which - 1 + size, size), size - 2)
            found = k.got_line[slot + at, pl.ds(within, rows), :].astype(F32)
            total = total + jnp.where(which == digit, own, found)
        target[pl.ds(within, rows), :] = total.astype(BF16)

    def give_home(number):
        section = PIECES[number][0]
        rows, at = part_of[number], piece_at[number]
        within = at // group
        for level in range(len(levels) - 1):
            add_level(number, level, k.line_sum.at[level + 1])
            send_level(number, level + 1)
        add_level(number, len(levels) - 1, k.home)
        target = k.got_all.at[pl.ds(section_at[number] + mine * rows, rows)]

        def give(other):
            remote(
                k.home.at[pl.ds(within, rows)],
                target,
                k.home_send.at[number],
                k.home_recv.at[number],
                {"phase": section, "batch": 2 * line + other},
            ).start()

        @pl.when(stage != section)
        def unused_both():
            give(0)
            give(1)

        @pl.when(stage == section)
        def unused_one():
            give(1 - core)
            target[...] = k.home[pl.ds(within, rows), :]

    def take_all(number):
        rows, within = part_of[number], section_at[number]

        @pl.when(stage == PIECES[number][0])
        def unused_take():
            wait_for(k.home_recv.at[number], k.got_all.at[pl.ds(within, (group - 1) * rows)])

    def end_sends(number):
        rows, at = part_of[number], piece_at[number]
        within = at // group
        wait_for(k.scatter_send.at[number], k.got_scatter.at[:, pl.ds(within, rows)])
        for level in range(len(levels)):
            size, unused_stride, slot, unused_digit = level_of(level)
            sent = k.got_line.at[pl.ds(slot, size - 1), pl.ds(within, rows)]
            wait_for(k.line_send.at[level, number], sent)

        @pl.when(stage != PIECES[number][0])
        def unused_away():
            wait_for(k.home_send.at[number], k.got_all.at[pl.ds(0, 2 * rows)])

        @pl.when(stage == PIECES[number][0])
        def unused_home():
            wait_for(k.home_send.at[number], k.got_all.at[pl.ds(0, rows)])

    def stage_piece(number):
        rows, used, at = padded[number], PIECES[number][1], piece_at[number]
        if used < rows:
            wst[used:rows, :] = jnp.zeros((rows - used, LANES), F32)

        def convert(i, carry):
            start = pl.multiple_of(i * 64, 64)
            k.gb[pl.ds(at + start, 64), :] = wst[pl.ds(start, 64), :].astype(BF16)
            return carry

        lax.fori_loop(0, rows // 64, convert, 0)
        give_scatter(number)

    def put_narrow(number, row, vector):
        k.send_narrow[number, row : row + 1, :] = vector

    def put_wide(number, row, vectors):
        for j, vector in enumerate(vectors):
            at = STARTS[number] + 4 * row + j
            k.send[at : at + 1, :] = vector

    def put_small(row, vector):
        k.small[row : row + 1, :] = vector

    def narrow(row):
        return k.total[row : row + 1, :]

    def wide(row):
        return jnp.concatenate([k.total[4 * row + j : 4 * row + j + 1, :] for j in range(4)], axis=1)

    def reduced(values):
        return jnp.sum(values, axis=0, keepdims=True)

    def gain_narrow(row):
        return k.gains[row : row + 1, :]

    def gain_wide(row):
        return jnp.concatenate([k.gains[row + j : row + j + 1, :] for j in range(4)], axis=1)

    def put_coef(layer, what, vector):
        row = 8 * layer + what
        k.coef[row : row + 1, 0 : vector.shape[1]] = vector

    def lanes(j):
        return slice(j * LANES, (j + 1) * LANES)

    def get_coef(layer, what, j=0):
        row = 8 * layer + what
        return k.coef[row : row + 1, lanes(j)]

    def finish(layer, sums, squares, gain, bias, count_inverse):
        mean = sums * count_inverse
        inverse = lax.rsqrt(squares * count_inverse - mean * mean + EPSILON)
        scale = inverse * gain
        put_coef(layer, INVERSE, inverse)
        put_coef(layer, NEG_MEAN, -mean * inverse)
        put_coef(layer, HALF_SCALE, 0.5 * scale)
        put_coef(layer, HALF_SHIFT, 0.5 * (bias - mean * scale))

    def normed_sum(layer, sums, products, j=0):
        return products * get_coef(layer, INVERSE, j) + sums * get_coef(layer, NEG_MEAN, j)

    def finish_back(layer, sums, dots, gain, count_inverse):
        width = sums.shape[1]
        row = 8 * layer
        inverse = k.coef[row + INVERSE : row + INVERSE + 1, 0:width]
        scale = inverse * gain
        slant = scale * dots * count_inverse
        put_coef(layer, GRAD_A, scale)
        put_coef(layer, GRAD_E, slant * inverse)
        put_coef(
            layer,
            GRAD_D,
            scale * sums * count_inverse
            + slant * k.coef[row + NEG_MEAN : row + NEG_MEAN + 1, 0:width],
        )

    def put_late(stores):
        for ref, at, value in stores:
            ref[at] = value

    def each_part(body, carry=0, parts=1):
        def step(i, inner):
            stores = []
            for u in range(parts):
                inner, found = body(pl.multiple_of((i * parts + u) * part, 16), inner)
                stores = stores + found
            put_late(stores)
            return inner

        return lax.fori_loop(0, 25 // parts, step, carry, unroll=UNROLL if parts == 1 else 1)

    def each_chunk(body, carry=0):
        def step(i, inner):
            return body(pl.multiple_of(i * chunk, 16), inner)

        return lax.fori_loop(0, 5, step, carry, unroll=UNROLL)

    def each_block(body):
        def step(i, carry):
            stores = []
            for u in range(per):
                number = i * per + u
                stores = stores + body(number, pl.multiple_of(number * BLOCK, 16))
            put_late(stores)
            return carry

        lax.fori_loop(0, blocks // per, step, 0, unroll=UNROLL)

    def zeros(width=MID):
        return jnp.zeros((8, width), F32)

    def live_rows(start, rows):
        return lax.broadcasted_iota(jnp.int32, (rows, LANES), 0) + start < rows_live

    def near_rows(rows, number):
        return lax.broadcasted_iota(jnp.int32, (rows, LANES), 0) < number

    def live_block(width):
        return jnp.broadcast_to(jnp.where(width > 0, 1.0, 0.0), (BLOCK, LANES)).astype(BF16)

    def at_block(buffer, j, start, rows):
        return buffer[pl.ds(j * out_rows + start, rows), :]

    def wide_store(buffer, start, values):
        rows = values.shape[0]
        for j in range(4):
            buffer[pl.ds(j * out_rows + start, rows), :] = values[:, lanes(j)]

    def added(carry, values):
        return carry[0] + folded(values), carry[1] + folded(values * values)

    def product_sums(left, right, store):
        width = right.shape[1]

        def body(start, carry):
            values = dense(left[pl.ds(start, chunk), :], right[...])
            store(start, values)
            return added(carry, values)

        return each_chunk(body, (zeros(width), zeros(width)))

    def store_narrow(target):
        def store(start, values):
            target[pl.ds(start, values.shape[0]), :] = values

        return store

    def send_narrow(number, sums):
        put_narrow(number, 0, reduced(sums[0]))
        put_narrow(number, 1, reduced(sums[1]))
        share(number)

    def by_lanes(vector):
        return [vector[:, lanes(j)] for j in range(4)]

    def stage_section(section):
        def step(i, carry):
            start = pl.multiple_of(i * (ROWS // 7), 16)
            wst[pl.ds(start, ROWS // 7), :] = wts[section, pl.ds(start, ROWS // 7), :].astype(F32)
            return carry

        lax.fori_loop(0, 7, step, 0)

    def unpack_wide(at, rows, target):
        for j in range(4):
            for r in range(rows // LANES):
                piece = wst[pl.ds(at + 4 * LANES * r + j, LANES, stride=4), :]
                target[r * LANES : (r + 1) * LANES, lanes(j)] = piece.astype(BF16)

    def take_gain(row, at, rows=1):
        k.gains[row : row + rows, :] = wst[at : at + rows, :]

    def turned(piece):
        return piece.astype(BF16).T

    tab_copy.wait()
    src[0:PAD, :] = jnp.zeros((PAD, LANES), F32)
    src[PAD + out_rows : plane, :] = jnp.zeros((PAD, LANES), F32)
    for number in range(4):
        big0[number * plane : number * plane + PAD, :] = jnp.zeros((PAD, LANES), F32)

    def make_masks(number, start):
        width, local = tab[0, number], tab[1, number]
        pixel = lax.broadcasted_iota(jnp.int32, (BLOCK, LANES), 0).astype(F32) + local.astype(F32)
        side = jnp.maximum(width, 1).astype(F32)
        row = jnp.floor((pixel + 0.5) / side)
        column = pixel - row * side
        one = jnp.where(width > 0, 1.0, 0.0)
        found = (row > 0.5, row < side - 1.5, column > 0.5, column < side - 1.5)
        return [
            (
                masks,
                (which, pl.ds(start, BLOCK), slice(None)),
                jnp.where(condition, one, 0.0).astype(BF16),
            )
            for which, condition in enumerate(found)
        ]

    each_block(make_masks)
    to_rows(EARLY, ROW)
    weight_copies = weight_copies + send_weights(1)
    for copy in feat_copies:
        copy.wait()

    window_rows = AHEAD + 4 * part

    def shortcut_pixels(i, carry):
        low = pl.multiple_of(jnp.maximum(i * 4 * part - AHEAD, 0), 16)
        stores = []
        for half in range(2):
            gn[half * window_rows : (half + 1) * window_rows, :] = feat[
                pl.ds(low, window_rows), lanes(half)
            ].astype(F32)
        for u in range(per):
            number = i * per + u
            start = pl.multiple_of(number * BLOCK, 16)
            first = tab[12, number]
            second = first + tab[4, number]
            near = near_rows(BLOCK, tab[3, number])
            one = jnp.where(tab[0, number] > 0, 1.0, 0.0)
            for half in range(2):
                picked = jnp.where(
                    near,
                    gn[pl.ds(half * window_rows + first, BLOCK, stride=2), :],
                    gn[pl.ds(half * window_rows + second, BLOCK, stride=2), :],
                )
                stores.append(
                    (k.xs, (pl.ds(start, BLOCK), lanes(half)), (picked * one).astype(BF16))
                )
        put_late(stores)
        return carry

    lax.fori_loop(0, 25, shortcut_pixels, 0)

    need_weights(0, 0)
    def open_first(step, carry):
        start = pl.multiple_of(step * chunk, 16)
        values = dense(feat[pl.ds(start, chunk), :], wts[0, 0:CIN, :])
        t1[pl.ds(start, chunk), :] = values
        rows = lax.broadcasted_iota(jnp.int32, values.shape, 0) + start
        return added(carry, jnp.where(rows < 4 * rows_live, values, 0.0))

    sums = lax.fori_loop(0, in_rows // chunk, open_first, (zeros(), zeros()), unroll=UNROLL)
    send_narrow(0, sums)

    need_weights(1, 0)
    stage_section(0)
    take_gain(0, IN_GAIN, 2)
    take_gain(2, MID_GAIN, 2)
    k.wmid1[...] = wst[MID_AT : MID_AT + 9 * MID, :].astype(BF16)

    def first_products(block):
        rows = slice(block * out_rows, (block + 1) * out_rows)
        live = (
            lax.broadcasted_iota(jnp.int32, (out_rows, MID), 0) + block * out_rows < 4 * rows_live
        )
        k.turn[0:LANES, :] = turned(jnp.where(live, t1[rows, :], 0.0))
        live = lax.broadcasted_iota(jnp.int32, (16, out_rows), 1) + block * out_rows < 4 * rows_live
        k.turn[LANES : LANES + 16, :] = jnp.where(live, 1.0, 0.0).astype(BF16)
        found = dense(k.turn[...], feat[rows, :])
        for half in range(2):
            at = slice(half * LANES, (half + 1) * LANES)
            product = found[0:LANES, lanes(half)].T
            total = jnp.broadcast_to(found[LANES : LANES + 1, lanes(half)], (LANES, LANES)).T
            k.first_t[at, :] = product if block == 0 else k.first_t[at, :] + product
            k.first_s[at, :] = total if block == 0 else k.first_s[at, :] + total

    first_products(0)
    collect(0)
    finish(L1, narrow(0), narrow(1), gain_narrow(0), gain_narrow(1), 0.25 * inverse_count)

    def first_hidden(number, start):
        scale, shift = get_coef(L1, HALF_SCALE), get_coef(L1, HALF_SHIFT)
        near = near_rows(BLOCK, tab[3, number])
        stores = []
        for row in range(2):
            for column in range(2):
                first = tab[2, number] + column + (tab[6, number] if row else 0)
                values = jnp.where(
                    near,
                    t1[pl.ds(first, BLOCK, stride=2), :],
                    t1[pl.ds(first + tab[4, number], BLOCK, stride=2), :],
                )
                at = pl.ds((2 * row + column) * plane + PAD + start, BLOCK)
                stores.append((big0, (at, slice(None)), silu_half(values * scale + shift)))
        return stores

    each_block(first_hidden)

    def wide_columns(number, start):
        width = tab[0, number]
        here = pl.ds(start, BLOCK)
        top, left, live = masks[0, here, :], masks[2, here, :], live_block(width)
        corner = top * left
        stores = []
        for tap in range(9):
            i, j = tap // 3, tap % 3
            at = (2 * (0 if i == 1 else 1) + (0 if j == 1 else 1)) * plane + PAD + start
            at = at - (width if i == 0 else 0) - (1 if j == 0 else 0)
            mask = (corner if j == 0 else top) if i == 0 else (left if j == 0 else live)
            values = big0[pl.ds(at, BLOCK), :].astype(BF16) * mask
            stores.append((k.cols1, (here, lanes(tap)), values))
        return stores

    each_block(wide_columns)
    send_narrow(1, product_sums(k.cols1, k.wmid1, store_narrow(k.t2)))

    bank_copies[0].start()
    need_weights(0, 1)
    need_weights(1, 1)
    stage_section(1)
    take_gain(8, OUT_GAIN, 8)
    take_gain(16, SHORT_GAIN, 8)
    unpack_wide(0, MID, k.wout2)
    unpack_wide(AFTER_OUT, CIN, k.wshort)
    short_sums = product_sums(k.xs, k.wshort, functools.partial(wide_store, big2))
    put_wide(2, 2, by_lanes(reduced(short_sums[0])))
    put_wide(2, 3, by_lanes(reduced(short_sums[1])))

    def close_narrow(layer, source, target):
        def body(start, carry):
            half = source[pl.ds(start, part), :] * get_coef(layer, HALF_SCALE) + get_coef(
                layer, HALF_SHIFT
            )
            values = jnp.where(live_rows(start, part), silu_half(half), 0.0).astype(BF16)
            return carry, [(target, (pl.ds(start, part), slice(None)), values)]

        each_part(body, parts=5)

    collect(1)
    finish(L2, narrow(0), narrow(1), gain_narrow(2), gain_narrow(3), inverse_count)
    close_narrow(L2, k.t2, k.h2)

    sums = product_sums(k.h2, k.wout2, functools.partial(wide_store, big1))
    put_wide(2, 0, by_lanes(reduced(sums[0])))
    put_wide(2, 1, by_lanes(reduced(sums[1])))
    share(2)

    def bank_to_bf16(half):
        bank_copies[half].wait()

        def body(i, carry):
            start = pl.multiple_of(i * 128, 128)
            for j in range(2):
                wide2[pl.ds(start, 128), lanes(2 * half + j)] = big0[
                    pl.ds(j * (BANK // 4) + start, 128), :
                ].astype(BF16)
            return carry

        lax.fori_loop(0, BANK // 4 // 128, body, 0)

    need_weights(0, 2)
    need_weights(1, 2)
    stage_section(2)
    take_gain(4, THIRD_GAIN, 2)
    take_gain(6, THIRD_MID_GAIN, 2)
    k.wmid3[...] = wst[THIRD_MID : THIRD_MID + 9 * MID, :].astype(BF16)
    bank_to_bf16(0)
    bank_copies[1].start()
    collect(2)
    finish(L3, wide(0), wide(1), gain_wide(8), gain_wide(12), inverse_count)
    finish(LS, wide(2), wide(3), gain_wide(16), gain_wide(20), inverse_count)

    def second_half(j, start):
        return (
            at_block(big1, j, start, part) * get_coef(L3, HALF_SCALE, j)
            + at_block(big2, j, start, part) * get_coef(LS, HALF_SCALE, j)
            + (get_coef(L3, HALF_SHIFT, j) + get_coef(LS, HALF_SHIFT, j))
        )

    def close_second(start, carry):
        live = live_rows(start, part)
        stores = []
        for j in range(4):
            values = jnp.where(live, silu_half(second_half(j, start)), 0.0).astype(BF16)
            stores.append((k.y, (pl.ds(start, part), lanes(j)), values))
        return carry, stores

    each_part(close_second)

    send_narrow(3, product_sums(k.y, wts.at[2, pl.ds(0, COUT)], store_narrow(k.t4)))
    need_weights(0, 3)
    need_weights(1, 3)
    stage_section(3)
    take_gain(24, OUT_GAIN, 8)
    unpack_wide(0, MID, k.wout4)
    bank_to_bf16(1)
    first_products(1)
    collect(3)
    finish(L4, narrow(0), narrow(1), gain_narrow(4), gain_narrow(5), inverse_count)

    def third_hidden(start, carry):
        half = k.t4[pl.ds(start, part), :] * get_coef(L4, HALF_SCALE) + get_coef(L4, HALF_SHIFT)
        return carry, [(src, (pl.ds(PAD + start, part), slice(None)), silu_half(half))]

    each_part(third_hidden, parts=5)

    def near_columns(number, start, target, target_start):
        width = tab[0, number]
        here = pl.ds(start, BLOCK)
        top, bottom, left, right = (masks[which, here, :] for which in range(4))
        live = live_block(width)
        stores = []
        for tap in range(9):
            i, j = tap // 3, tap % 3
            at = PAD + start + (i - 1) * width + (j - 1)
            mask = (top, live, bottom)[i]
            if j != 1:
                beside = left if j == 0 else right
                mask = beside if i == 1 else mask * beside
            values = src[pl.ds(at, BLOCK), :].astype(BF16) * mask
            stores.append((target, (pl.ds(target_start, BLOCK), lanes(tap)), values))
        return stores

    each_block(lambda number, start: near_columns(number, start, k.cols2, start))
    send_narrow(4, product_sums(k.cols2, k.wmid3, store_narrow(k.t5)))

    neg_copy.wait()
    gn[0 : 8 * LANES, :] = jnp.zeros((8 * LANES, LANES), F32)
    neg_piece = 512
    for slot in range(slots):

        def count(i, carry, slot=slot):
            at = pl.multiple_of(i * neg_piece, neg_piece)
            found = k.neg[slot, pl.ds(stage, 1), pl.ds(at, neg_piece)]
            spot = lax.broadcasted_iota(jnp.int32, (LANES, neg_piece), 0)
            upper = lax.shift_right_logical(found, 7)
            high = jnp.where(spot == upper, 1.0, 0.0).astype(BF16)
            low = jnp.where(spot == found - LANES * upper, 1.0, 0.0).astype(BF16)
            return carry + across(high, low)

        found = lax.fori_loop(
            0, NEG // neg_piece, count, jnp.zeros((LANES, LANES), F32), unroll=True
        )
        gn[pl.ds(slot, LANES, stride=8), :] = found
    collect(4)
    finish(L5, narrow(0), narrow(1), gain_narrow(6), gain_narrow(7), inverse_count)
    close_narrow(L5, k.t5, k.h4)

    sums = product_sums(k.h4, k.wout4, functools.partial(wide_store, big0))
    put_wide(5, 0, by_lanes(reduced(sums[0])))
    put_wide(5, 1, by_lanes(reduced(sums[1])))
    share(5)
    for j in range(4):
        k.wout4_t[j * LANES : (j + 1) * LANES, :] = turned(k.wout4[:, lanes(j)])
    for tap in range(9):
        k.wmid3_t[(8 - tap) * MID : (9 - tap) * MID, :] = turned(
            k.wmid3[tap * MID : (tap + 1) * MID, :]
        )
    for r in range(4):
        k.win3_t[:, lanes(r)] = turned(wts[2, r * LANES : (r + 1) * LANES, :])
    first_products(2)
    collect(5)
    finish(L6, wide(0), wide(1), gain_wide(24), gain_wide(28), inverse_count)

    def last_half(j, start):
        return (
            at_block(big0, j, start, part) * get_coef(L6, HALF_SCALE, j)
            + get_coef(L6, HALF_SHIFT, j)
            + 0.5 * k.y[pl.ds(start, part), lanes(j)].astype(F32)
        )

    def close_last(start, carry):
        return carry, [
            (gw, (pl.ds(start, part), lanes(j)), silu_half(last_half(j, start)).astype(BF16))
            for j in range(4)
        ]

    each_part(close_last)

    def pool(start, carry):
        rows = lax.broadcasted_iota(jnp.int32, (8, chunk), 1) + start
        owner = jnp.zeros((8, chunk), jnp.int32)
        for end in ends:
            owner = owner + jnp.where(rows >= end, 1, 0)
        mine = owner == lax.broadcasted_iota(jnp.int32, (8, chunk), 0)
        mine = jnp.where(mine, 1.0, 0.0).astype(BF16)
        return carry + dense(mine, gw[pl.ds(start, chunk), :])

    slot_row = lax.broadcasted_iota(jnp.int32, (8, LANES), 0)
    area = jnp.zeros((8, LANES), jnp.int32)
    positive = jnp.full((8, LANES), -1, jnp.int32)
    for slot in range(slots):
        area = jnp.where(slot_row == slot, sides[slot] * sides[slot], area)
        positive = jnp.where(slot_row == slot, k.positives[0, stage, slot], positive)
    inverse_area = jnp.where(area > 0, 1.0 / jnp.maximum(area, 1).astype(F32), 0.0)
    inverse_area_wide = jnp.concatenate([inverse_area] * 4, axis=1)
    half_offset = 0.5 * jnp.log(jnp.full((8, LANES), k.normalizer[0] * NEG / BANK))
    pooled = each_chunk(pool, zeros(COUT)) * inverse_area_wide

    head = wst[AFTER_OUT : AFTER_OUT + COUT, :].astype(BF16)
    pooled_high, pooled_low = split(pooled)
    embed = dense(pooled_high, head) + dense(pooled_low, head)
    scale = lax.rsqrt(jnp.sum(embed * embed, axis=1, keepdims=True) + 1e-06)
    unit = embed * scale
    unit_parts = jnp.concatenate(split(unit), axis=0)
    lane = lax.broadcasted_iota(jnp.int32, (8, LANES), 1)
    parts = []
    for block in range(4):
        scores = across(unit_parts, wide2[:, lanes(block)])
        scores = scores[0:8, :] + scores[8:16, :]
        pieces = []
        for j in range(BANK // 4 // LANES):
            high = block * (BANK // 4 // LANES) + j
            half = scores[:, lanes(j)] * (0.5 / SOFTMAX_TEMPER) - half_offset
            sigma = 0.5 + 0.5 * jnp.tanh(half)
            chosen = jnp.where(positive == lane + high * LANES, 1.0, 0.0)
            pieces.append((gn[high * 8 : high * 8 + 8, :] + chosen) * sigma - chosen)
        parts = parts + list(split(jnp.concatenate(pieces, axis=1)))
    found = dense(jnp.concatenate(parts, axis=0), wide2[...])
    unit_grad = zeros(EMB)
    for block in range(4):
        for row in (16 * block, 16 * block + 8):
            unit_grad = unit_grad + found[row : row + 8, lanes(block)]
    unit_grad = jnp.where(inverse_area > 0.0, unit_grad, 0.0) * (1.0 / SOFTMAX_TEMPER)
    embed_grad = scale * unit_grad - embed * (
        scale * scale * scale * jnp.sum(embed * unit_grad, axis=1, keepdims=True)
    )
    grad_high, grad_low = split(embed_grad)
    pooled_grad = across(grad_high, head) + across(grad_low, head)
    pooled_grad = pooled_grad * inverse_area_wide
    for j in range(4):
        k.spread[8 * j : 8 * j + 8, :] = pooled_grad[:, lanes(j)]

    def last_slope(step, carry):
        start = pl.multiple_of(step * part, 16)
        owners = [tab[5, step * per + u] for u in range(per)]
        found, stores = [], []
        for j in range(4):
            upstream = jnp.concatenate(
                [
                    jnp.broadcast_to(k.spread[pl.ds(8 * j + owner, 1), :], (BLOCK, LANES))
                    for owner in owners
                ],
                axis=0,
            )
            upstream = upstream * slope_half(last_half(j, start))
            stores.append((gw, (pl.ds(start, part), lanes(j)), upstream.astype(BF16)))
            found.append(
                (
                    carry[j][0] + folded(upstream),
                    carry[j][1] + folded(upstream * at_block(big0, j, start, part)),
                )
            )
        put_late(stores)
        return tuple(found)

    pair = (zeros(), zeros())
    sums = lax.fori_loop(0, 25, last_slope, (pair,) * 4, unroll=UNROLL)
    bias_grads = [reduced(sums[j][0]) for j in range(4)]
    gain_grads = [normed_sum(L6, bias_grads[j], reduced(sums[j][1]), j) for j in range(4)]
    put_wide(6, 0, bias_grads)
    put_wide(6, 1, gain_grads)
    share(6)
    for j in range(4):
        wst[OUT_GAIN + j : OUT_GAIN + j + 1, :] = gain_grads[j]
        wst[OUT_BIAS + j : OUT_BIAS + j + 1, :] = bias_grads[j]
    wst[AFTER_OUT : AFTER_OUT + COUT, :] = (
        outer(pooled_high, grad_high) + outer(pooled_high, grad_low) + outer(pooled_low, grad_high)
    )
    for j in range(4):
        k.wout2_t[j * LANES : (j + 1) * LANES, :] = turned(k.wout2[:, lanes(j)])
        for r in range(2):
            k.wshort_t[j * LANES : (j + 1) * LANES, lanes(r)] = turned(
                k.wshort[r * LANES : (r + 1) * LANES, lanes(j)]
            )
    def put_turned(source, target, values):
        at = (target // 2) * 4 * MID + source * MID
        k.wmid1_t[at : at + MID, lanes(target % 2)] = values

    for tap in range(9):
        i, j = tap // 3, tap % 3
        source = 2 * (1 if i == 0 else 0) + (1 if j == 0 else 0)
        target = 2 * (0 if i == 1 else 1) + (0 if j == 1 else 1)
        put_turned(source, target, turned(k.wmid1[tap * MID : (tap + 1) * MID, :]))
    for source in range(4):
        for target in range(4):
            if source & target != source:
                put_turned(source, target, jnp.zeros((MID, MID), BF16))
    first_products(3)
    collect(6)
    finish_back(L6, wide(0), wide(1), gain_wide(24), inverse_count)

    def back_value(layer, upstream, values, j=0):
        return (
            upstream * get_coef(layer, GRAD_A, j)
            - values * get_coef(layer, GRAD_E, j)
            - get_coef(layer, GRAD_D, j)
        )

    def back_sixth(start, carry):
        here = pl.ds(start, part)
        live = live_rows(start, part)
        stores = []
        for j in range(4):
            values = back_value(
                L6, gw[here, lanes(j)].astype(F32), at_block(big0, j, start, part), j
            )
            stores.append((wide2, (here, lanes(j)), jnp.where(live, values, 0.0).astype(BF16)))
        return carry, stores

    each_part(back_sixth)

    def back_narrow(layer, upstream, values, carry):
        half = values * get_coef(layer, HALF_SCALE) + get_coef(layer, HALF_SHIFT)
        upstream = upstream * slope_half(half)
        return upstream, (carry[0] + folded(upstream), carry[1] + folded(upstream * values))

    def back_rows(layer, values):
        def body(start, carry):
            here = pl.ds(start, part)
            upstream, carry = back_narrow(layer, gn[here, :], values[here, :], carry)
            return carry, [(gn, (here, slice(None)), upstream)]

        return each_part(body, (zeros(), zeros()), parts=5)

    def send_back(number, row, layer, sums):
        bias_grad = reduced(sums[0])
        gain_grad = normed_sum(layer, bias_grad, reduced(sums[1]))
        put_narrow(number, 0, bias_grad)
        put_narrow(number, 1, gain_grad)
        share(number)
        put_small(row, gain_grad)
        put_small(row + 1, bias_grad)

    def rounded_product(left, right):
        def body(start, carry):
            here = pl.ds(start, chunk)
            gn[here, :] = dense(left[here, :], right[...]).astype(BF16).astype(F32)
            return carry

        each_chunk(body)

    rounded_product(wide2, k.wout4_t)
    send_back(7, 2, L5, back_rows(L5, k.t5))

    def put_wide_matrix(at, values):
        for r in range(values.shape[0] // LANES):
            for j in range(4):
                wst[pl.ds(at + 4 * LANES * r + j, LANES, stride=4), :] = values[
                    r * LANES : (r + 1) * LANES, lanes(j)
                ]

    def turned_rows(ref, lane=0):
        return turned(ref[:, lane * LANES : (lane + 1) * LANES])

    k.turn[0:LANES, :] = turned_rows(k.h4)
    put_wide_matrix(0, dense(k.turn[0:LANES, :], wide2[0:out_rows, :]))
    stage_piece(LAST)
    collect(7)
    finish_back(L5, narrow(0), narrow(1), gain_narrow(6), inverse_count)

    def back_close(layer, values):
        def body(start, carry):
            here = pl.ds(start, part)
            found = back_value(layer, gn[here, :], values[here, :])
            found = jnp.where(live_rows(start, part), found, 0.0).astype(BF16)
            return carry, [
                (k.dtn, (here, slice(None)), found),
                (src, (pl.ds(PAD + start, part), slice(None)), found.astype(F32)),
            ]

        each_part(body, parts=5)

    back_close(L5, k.t5)

    def open_back_fourth(step, carry):
        chunk_start = pl.multiple_of(step * chunk, 16)

        def fill(i, inner):
            stores = []
            for u in range(per):
                at = pl.multiple_of((i * per + u) * BLOCK, 16)
                number = step * (chunk // BLOCK) + i * per + u
                stores = stores + near_columns(number, chunk_start + at, k.colt, at)
            put_late(stores)
            return inner

        lax.fori_loop(0, chunk // BLOCK // per, fill, 0, unroll=UNROLL)
        gn[pl.ds(chunk_start, chunk), :] = dense(k.colt[...], k.wmid3_t[...])
        return carry

    lax.fori_loop(0, 5, open_back_fourth, 0)
    send_back(8, 0, L4, back_rows(L4, k.t4))

    def columns_grad(columns, store):
        k.turn[0:LANES, :] = turned_rows(k.dtn)
        for group in range(3):
            found = dense(k.turn[0:LANES, :], columns[:, 3 * group * LANES : 3 * (group + 1) * LANES])
            for j in range(3):
                store(3 * group + j, found[:, lanes(j)].T)

    def store_third(tap, values):
        wst[THIRD_MID + tap * MID : THIRD_MID + (tap + 1) * MID, :] = values

    columns_grad(k.cols2, store_third)
    give_line(LAST)
    collect(8)
    finish_back(L4, narrow(0), narrow(1), gain_narrow(4), inverse_count)
    back_close(L4, k.t4)

    def back_block(start, carry):
        here = pl.ds(start, part)
        arrived = dense(k.dtn[here, :], k.win3_t[...])
        found, stores = [], []
        for j in range(4):
            upstream = arrived[:, lanes(j)] + gw[here, lanes(j)].astype(F32)
            upstream = upstream.astype(BF16).astype(F32) * slope_half(second_half(j, start))
            stores.append((gw, (here, lanes(j)), upstream.astype(BF16)))
            found.append(
                (
                    carry[j][0] + folded(upstream),
                    carry[j][1] + folded(upstream * at_block(big1, j, start, part)),
                    carry[j][2] + folded(upstream * at_block(big2, j, start, part)),
                )
            )
        return tuple(found), stores

    sums = each_part(back_block, ((zeros(), zeros(), zeros()),) * 4)
    bias_grads, gain_grads, short_grads = (
        [reduced(sums[j][which]) for j in range(4)] for which in range(3)
    )
    gain_grads = [normed_sum(L3, bias_grads[j], gain_grads[j], j) for j in range(4)]
    short_grads = [normed_sum(LS, bias_grads[j], short_grads[j], j) for j in range(4)]
    put_wide(9, 0, bias_grads)
    put_wide(9, 1, gain_grads)
    put_wide(9, 2, short_grads)
    share(9)
    k.turn[0:LANES, :] = turned_rows(k.dtn)
    found = dense(k.turn[0:LANES, :], k.y[...])
    for j in range(4):
        wst[j * LANES : (j + 1) * LANES, :] = found[:, lanes(j)].T
    wst[THIRD_GAIN : THIRD_BIAS + 1, :] = k.small[0:2, :]
    wst[THIRD_MID_GAIN : THIRD_MID_BIAS + 1, :] = k.small[2:4, :]
    stage_piece(THIRD)
    give_home(LAST)
    collect(9)
    finish_back(L3, wide(0), wide(1), gain_wide(8), inverse_count)
    finish_back(LS, wide(0), wide(2), gain_wide(16), inverse_count)

    def back_third(start, carry):
        here = pl.ds(start, part)
        below = pl.ds(out_rows + start, part)
        live = live_rows(start, part)
        stores = []
        for j in range(4):
            upstream = gw[here, lanes(j)].astype(F32)
            found = back_value(L3, upstream, at_block(big1, j, start, part), j)
            stores.append((wide2, (here, lanes(j)), jnp.where(live, found, 0.0).astype(BF16)))
            found = back_value(LS, upstream, at_block(big2, j, start, part), j)
            stores.append((wide2, (below, lanes(j)), jnp.where(live, found, 0.0).astype(BF16)))
        return carry, stores

    each_part(back_third)
    rounded_product(wide2, k.wout2_t)
    send_back(10, 6, L2, back_rows(L2, k.t2))
    for j in range(4):
        wst[OUT_GAIN + j : OUT_GAIN + j + 1, :] = gain_grads[j]
        wst[OUT_BIAS + j : OUT_BIAS + j + 1, :] = bias_grads[j]
        wst[SHORT_GAIN + j : SHORT_GAIN + j + 1, :] = short_grads[j]
        wst[SHORT_BIAS + j : SHORT_BIAS + j + 1, :] = bias_grads[j]
    k.turn[0:LANES, :] = turned_rows(k.h2)
    put_wide_matrix(0, dense(k.turn[0:LANES, :], wide2[0:out_rows, :]))
    for half in range(2):
        k.turn[0:LANES, :] = turned_rows(k.xs, half)
        put_wide_matrix(
            AFTER_OUT + half * 4 * LANES, dense(k.turn[0:LANES, :], wide2[out_rows : 2 * out_rows, :])
        )
    stage_piece(SECOND)
    give_line(THIRD)

    def back_picked(start, carry):
        found = dense(wide2[pl.ds(out_rows + start, chunk), :], k.wshort_t[...])
        found = found.astype(BF16).astype(F32)
        for half in range(2):
            big2[pl.ds(half * plane + PAD + start, chunk), :] = found[:, lanes(half)]
        return carry

    each_chunk(back_picked)
    for half in range(2):
        big2[half * plane : half * plane + PAD, :] = jnp.zeros((PAD, LANES), F32)
    collect(10)
    finish_back(L2, narrow(0), narrow(1), gain_narrow(2), inverse_count)
    back_close(L2, k.t2)


    def back_planes(step, carry):
        chunk_start = pl.multiple_of(step * chunk, 16)

        def fill(i, inner):
            stores = []
            for u in range(per):
                at = pl.multiple_of((i * per + u) * BLOCK, 16)
                start = chunk_start + at
                here = pl.ds(start, BLOCK)
                width = tab[0, step * (chunk // BLOCK) + i * per + u]
                bottom, right, live = masks[1, here, :], masks[3, here, :], live_block(width)
                shifts = ((0, live), (1, right), (width, bottom), (width + 1, bottom * right))
                for number, (shift, mask) in enumerate(shifts):
                    values = src[pl.ds(PAD + start + shift, BLOCK), :].astype(BF16) * mask
                    stores.append((k.colt, (pl.ds(at, BLOCK), lanes(number)), values))
            put_late(stores)
            return inner

        lax.fori_loop(0, chunk // BLOCK // per, fill, 0, unroll=UNROLL)
        even = dense(k.colt[:, 0 : 2 * MID], k.wmid1_t[0 : 2 * MID, :])
        odd = dense(k.colt[:, 0 : 4 * MID], k.wmid1_t[4 * MID : 8 * MID, :])
        for number in range(4):
            found = (even, odd)[number // 2][:, lanes(number % 2)]
            big0[pl.ds(number * plane + PAD + chunk_start, chunk), :] = found
        return carry

    lax.fori_loop(0, 5, back_planes, 0)

    in_unroll = 10

    def back_first(i, carry):
        stores = []
        for u in range(in_unroll):
            number = i * in_unroll + u
            first, second = tab[7, number], tab[8, number]
            near = near_rows(8, tab[9, number])
            for column in range(2):
                at = pl.ds(number * BLOCK + column, 8, stride=2)
                hidden = jnp.where(
                    near,
                    big0[pl.ds(first + column * plane, 8), :],
                    big0[pl.ds(second + column * plane, 8), :],
                )
                upstream, carry = back_narrow(L1, hidden, t1[at, :], carry)
                stores.append((big1, (at, slice(None)), upstream))
        put_late(stores)
        return carry

    sums = lax.fori_loop(
        0, in_rows // BLOCK // in_unroll, back_first, (zeros(), zeros()), unroll=UNROLL
    )
    send_back(11, 4, L1, sums)
    def store_first(tap, values):
        at = piece_at[FIRST_MID] + tap * MID
        k.gb[at : at + MID, :] = values.astype(BF16)

    columns_grad(k.cols1, store_first)
    if padded[FIRST_MID] > 9 * MID:
        at = piece_at[FIRST_MID]
        k.gb[at + 9 * MID : at + padded[FIRST_MID], :] = jnp.zeros(
            (padded[FIRST_MID] - 9 * MID, LANES), BF16
        )
    give_scatter(FIRST_MID)
    give_line(SECOND)
    give_home(THIRD)

    found = jnp.zeros((MID, CIN), F32)
    for block in range(4):
        rows = slice(block * out_rows, (block + 1) * out_rows)
        k.turn[0:LANES, :] = turned(big1[rows, :])
        found = found + dense(k.turn[0:LANES, :], feat[rows, :])
    first_g = [found[:, lanes(half)].T for half in range(2)]
    gn[0 : 2 * window_rows, :] = jnp.zeros((2 * window_rows, LANES), F32)
    for half in range(2):
        k.win1_t[:, lanes(half)] = turned(wts[0, half * LANES : (half + 1) * LANES, :])
    collect(11)
    finish_back(L1, narrow(0), narrow(1), gain_narrow(0), 0.25 * inverse_count)

    at = piece_at[FIRST_IN]
    for half in range(2):
        rows = slice(half * LANES, (half + 1) * LANES)
        values = first_g[half] * get_coef(L1, GRAD_A) - k.first_t[rows, :] * get_coef(L1, GRAD_E)
        values = values - k.first_s[rows, :] * get_coef(L1, GRAD_D)
        k.gb[at + half * LANES : at + (half + 1) * LANES, :] = values.astype(BF16)
    k.gb[at + CIN : at + CIN + 16, :] = jnp.concatenate(
        [k.small[4:8, :], jnp.zeros((12, LANES), F32)], axis=0
    ).astype(BF16)
    k.gb[at + CIN + 16 : at + padded[FIRST_IN], :] = jnp.zeros(
        (padded[FIRST_IN] - CIN - 16, LANES), BF16
    )
    give_scatter(FIRST_IN)
    give_line(FIRST_MID)
    give_home(SECOND)

    for block in range(4):

        def close_back_first(start, carry, block=block):
            rows = pl.ds(block * out_rows + start, part)
            found = back_value(L1, big1[rows, :], t1[rows, :])
            row = lax.broadcasted_iota(jnp.int32, (part, MID), 0) + (block * out_rows + start)
            found = jnp.where(row < 4 * rows_live, found, 0.0).astype(BF16)
            return carry, [(gw, (pl.ds(start, part), lanes(block)), found)]

        each_part(close_back_first, parts=5)

    give_line(FIRST_IN)
    give_home(FIRST_MID)

    def input_grad(step, carry):
        block, start = lax.div(step, 5), pl.multiple_of(lax.rem(step, 5) * chunk, 16)
        stores = []
        for u in range(chunk // BLOCK):
            number = step * (chunk // BLOCK) + u
            near = near_rows(8, tab[9, number])
            for half in range(2):
                values = jnp.where(
                    near,
                    big2[pl.ds(tab[10, number] + half * plane, 8), :],
                    big2[pl.ds(tab[11, number] + half * plane, 8), :],
                )
                at = slice(half * window_rows + u * BLOCK, half * window_rows + (u + 1) * BLOCK, 2)
                stores.append((gn, (at, slice(None)), values))
        put_late(stores)
        lane = pl.ds(pl.multiple_of(block * LANES, LANES), LANES)
        found = dense(gw[pl.ds(start, chunk), lane], k.win1_t[...])
        rows = pl.ds(pl.multiple_of(step * chunk, 16), chunk)
        for half in range(2):
            feat[rows, lanes(half)] = (
                found[:, lanes(half)] + gn[half * window_rows : half * window_rows + chunk, :]
            ).astype(BF16)
        return carry

    lax.fori_loop(0, 10, input_grad, 0)
    give_home(FIRST_IN)
    lax.fori_loop(10, 20, input_grad, 0)
    input_copy = pltpu.make_async_copy(feat, k.input_grad_at, k.out_sem.at[0])
    input_copy.start()

    for number in range(len(PIECES)):
        take_all(number)

    def ordered(target, source, rows):
        def body(i, carry):
            start = pl.multiple_of(i * 32, 32)
            wst[pl.ds(target + start, 32), :] = k.got_all[pl.ds(source + start, 32), :].astype(F32)
            return carry

        lax.fori_loop(0, rows // 32, body, 0)

    def blank(at):
        wst[at:ROWS, :] = jnp.zeros((ROWS - at, LANES), F32)

    for number in (LAST, THIRD, SECOND):

        @pl.when(stage == PIECES[number][0])
        def unused_ordered(number=number):
            rows = min(padded[number], ROWS // 32 * 32)
            if rows < ROWS:
                blank(rows)
            ordered(0, 0, rows)
            if rows < PIECES[number][1]:
                tail = k.got_all[rows : rows + 16, :].astype(F32)
                wst[rows : rows + 16, :] = tail

    @pl.when(stage == 0)
    def unused_first():
        at = section_at[FIRST_IN]
        blank(MID_BIAS + 1)
        ordered(0, at, CIN)
        gains = k.got_all[at + CIN : at + CIN + 16, :].astype(F32)
        wst[IN_GAIN : IN_BIAS + 1, :] = gains[0:2, :]
        wst[MID_GAIN : MID_BIAS + 1, :] = gains[2:4, :]
        ordered(MID_AT, 0, 9 * MID)

    out_copy = pltpu.make_async_copy(wst.at[pl.ds(0, ROWS)], k.weight_grads_at, k.grad_sem)
    out_copy.start()
    input_copy.wait()
    for copy in weight_copies:
        copy.wait_send()
    for number in range(EXCHANGES):
        wait_for(k.stat_send.at[number], incoming(number, pl.ds(0, batches - 1)))
    for number in range(len(PIECES)):
        end_sends(number)
    out_copy.wait()


def write_kernel(weight_rows, input_rows, weight_out, input_out):
    input_out[...] = input_rows[...]

    @pl.when(pl.program_id(0) == 0)
    def unused_weights():
        weight_out.reshape(ROW, LANES)[...] = weight_rows[0:ROW, :]


def shards(features, weights, crop_kind, positives, negatives, bank, normalizer):
    phases = lax.axis_size("phase")
    batches = lax.axis_size("batch")
    in_rows = features.shape[0] // MICRO
    out_rows = in_rows // 4
    plane = out_rows + 2 * PAD
    slots = crop_kind.shape[2]
    chunk = out_rows // 5
    part = out_rows // 25
    group = 2 * phases
    levels = line_levels(batches // 2)
    padded = [-(-rows // (16 * group)) * 16 * group for unused, rows in PIECES]
    widest = max(*padded[:3], padded[3] + padded[4])
    eighth = sum(padded) // group
    staged = max(ROWS, *padded[:3])
    any_space = pl.BlockSpec(memory_space=pl.ANY)
    smem = pl.BlockSpec(memory_space=pltpu.SMEM)

    def held(*shape, dtype=F32):
        return pltpu.VMEM(shape, dtype)

    def sems(*shape):
        return pltpu.SemaphoreType.DMA(shape)

    def low(*shape):
        return held(*shape, dtype=BF16)

    inputs = {
        "features_at": (features, any_space),
        "weights_at": (weights, any_space),
        "negatives_at": (jnp.transpose(negatives, (0, 2, 1, 3)), any_space),
        "bank_at": (bank, any_space),
        "kinds": (jnp.transpose(crop_kind, (2, 1, 0)), smem),
        "positives": (positives, smem),
        "normalizer": (normalizer, smem),
    }
    outputs = {
        "weight_grads_at": jax.ShapeDtypeStruct((ROWS, LANES), F32),
        "input_grad_at": jax.ShapeDtypeStruct((in_rows, CIN), BF16),
    }
    scratch = {
        "feat": low(in_rows, CIN),
        "t1": held(in_rows, MID),
        "big0": held(4 * plane, MID),
        "big1": held(in_rows, MID),
        "big2": held(4 * plane, MID),
        "cols1": low(out_rows, 9 * MID),
        "cols2": low(out_rows, 9 * MID),
        "colt": low(chunk, 9 * MID),
        "src": held(plane, MID),
        "t2": held(out_rows, MID),
        "t4": held(out_rows, MID),
        "t5": held(out_rows, MID),
        "gn": held(out_rows, MID),
        "h2": low(out_rows, MID),
        "h4": low(out_rows, MID),
        "xs": low(out_rows, CIN),
        "y": low(out_rows, COUT),
        "gw": low(out_rows, COUT),
        "wide2": low(BANK // 4, COUT),
        "dtn": low(out_rows, MID),
        "turn": low(LANES + 16, out_rows),
        "first_t": held(CIN, MID),
        "first_s": held(CIN, MID),
        "masks": low(4, out_rows, LANES),
        "raw": low(1, GRAD_LEN),
        "wts": low(phases, ROWS, LANES),
        "wst": held(staged, LANES),
        "wmid1": low(9 * MID, MID),
        "wmid3": low(9 * MID, MID),
        "wout2": low(MID, COUT),
        "wshort": low(CIN, COUT),
        "wout4": low(MID, COUT),
        "wout2_t": low(COUT, MID),
        "wshort_t": low(COUT, CIN),
        "wout4_t": low(COUT, MID),
        "wmid1_t": low(8 * MID, 2 * MID),
        "wmid3_t": low(9 * MID, MID),
        "win1_t": low(MID, CIN),
        "win3_t": low(MID, COUT),
        "gains": held(32, LANES),
        "small": held(8, LANES),
        "coef": held(56, COUT),
        "spread": held(32, LANES),
        "neg": held(slots, MICRO, NEG, dtype=jnp.int32),
        "tabv": held(16, TABLE, dtype=jnp.int32),
        "tab": pltpu.SMEM((16, TABLE), jnp.int32),
        "send": held(SPAN_ROWS, LANES),
        "send_narrow": held(EXCHANGES, 2, LANES),
        "recv_narrow": held(EXCHANGES, batches, 2, LANES),
        "recv": held(batches, SPAN_ROWS, LANES),
        "total": held(16, LANES),
        "gb": low(sum(padded), LANES),
        "got_scatter": low(group - 1, eighth, LANES),
        "line_sum": low(len(levels), eighth, LANES),
        "got_line": low(sum(levels) - len(levels), eighth, LANES),
        "home": low(eighth, LANES),
        "got_all": low(widest, LANES),
        "raw_sem": pltpu.SemaphoreType.DMA,
        "feat_sem": sems(4),
        "bank_sem": sems(2),
        "neg_sem": pltpu.SemaphoreType.DMA,
        "tab_sem": pltpu.SemaphoreType.DMA,
        "weight_send": sems(2, phases),
        "weight_recv": sems(2, phases),
        "stat_send": sems(EXCHANGES),
        "stat_recv": sems(EXCHANGES),
        "scatter_send": sems(len(PIECES)),
        "scatter_recv": sems(len(PIECES)),
        "line_send": sems(len(levels), len(PIECES)),
        "line_recv": sems(len(levels), len(PIECES)),
        "home_send": sems(len(PIECES)),
        "home_recv": sems(len(PIECES)),
        "out_sem": sems(4),
        "grad_sem": pltpu.SemaphoreType.DMA,
    }
    names = (*inputs, *outputs, *scratch)
    weight_rows, input_rows = pl.pallas_call(
        functools.partial(kernel, names, batches, phases, in_rows, slots),
        out_shape=tuple(outputs.values()),
        in_specs=[spec for unused, spec in inputs.values()],
        out_specs=(any_space, any_space),
        scratch_shapes=list(scratch.values()),
        compiler_params=pltpu.CompilerParams(
            collective_id=0, has_side_effects=True, vmem_limit_bytes=64 * 1024 * 1024
        ),
    )(*[value for value, unused in inputs.values()])
    steps = 4
    rows = pl.BlockSpec((in_rows // steps, CIN), lambda i: (i, 0))
    weight_grads, input_grad = pl.pallas_call(
        write_kernel,
        grid=(steps,),
        out_shape=(
            jax.ShapeDtypeStruct((1, GRAD_LEN), F32),
            jax.ShapeDtypeStruct((in_rows, CIN), BF16),
        ),
        in_specs=[pl.BlockSpec((ROWS, LANES), lambda i: (0, 0)), rows],
        out_specs=(pl.BlockSpec((1, GRAD_LEN), lambda i: (0, 0)), rows),
        compiler_params=pltpu.CompilerParams(vmem_limit_bytes=64 * 1024 * 1024),
    )(weight_rows, input_rows)
    return (weight_grads, input_grad)


def solution(mesh):
    placed = (
        P("batch", None),
        P("phase", None),
        P(),
        P("batch", None, None),
        P("batch", None, None, None),
        P(),
        P(),
    )
    return jax.shard_map(
        shards,
        mesh=mesh,
        in_specs=placed,
        out_specs=(P("phase", None), P(("batch", "phase"), None)),
        check_vma=False,
    )
```

```python
import functools
import math
import types

import jax
import jax.numpy as jnp
from jax import lax
from jax.experimental import pallas as pl
from jax.experimental.pallas import tpu as pltpu
from jax.sharding import PartitionSpec as P

CIN = 256
MID = 128
COUT = 512
EMB = 128
SIDE_UNIT = 4
MICRO = 4
NEG = 4096
BANK = 16384
GRAD_LEN = 213504
LANES = 128
SOFTMAX_TEMPER = 0.07
EPSILON = 1e-05

PAD = 48
ROW = GRAD_LEN // LANES
ROWS = -(-ROW // 16) * 16
BLOCK = 16
TABLE = 512
UNROLL = 5
EARLY = 272
AHEAD = 80
MESH = pl.DeviceIdType.MESH
F32 = jnp.float32
BF16 = jnp.bfloat16

IN_GAIN, IN_BIAS, MID_AT = CIN, CIN + 1, CIN + 2
MID_GAIN, MID_BIAS = MID_AT + 9 * MID, MID_AT + 9 * MID + 1
THIRD_GAIN, THIRD_BIAS, THIRD_MID = COUT, COUT + 1, COUT + 2
THIRD_MID_GAIN, THIRD_MID_BIAS = THIRD_MID + 9 * MID, THIRD_MID + 9 * MID + 1
OUT_GAIN, OUT_BIAS, AFTER_OUT = 512, 516, 520
SHORT_GAIN, SHORT_BIAS = AFTER_OUT + 1024, AFTER_OUT + 1028

EXCHANGES = 12
SPANS = {2: 16, 5: 8, 6: 8, 9: 16}
STARTS = {2: 0, 5: 16, 6: 24, 9: 32}
SPAN_ROWS = 48

PIECES = ((3, 1032), (2, 1668), (1, 1552), (0, 9 * MID), (0, 260))
LAST, THIRD, SECOND, FIRST_MID, FIRST_IN = range(5)

L1, L2, L3, LS, L4, L5, L6 = range(7)
HALF_SCALE, HALF_SHIFT, INVERSE, NEG_MEAN, GRAD_A, GRAD_E, GRAD_D = range(7)


def dense(left, right):
    return jnp.dot(left, right, preferred_element_type=F32)


def across(left, right):
    return lax.dot_general(left, right, (((1,), (1,)), ((), ())), preferred_element_type=F32)


def outer(left, right):
    return lax.dot_general(left, right, (((0,), (0,)), ((), ())), preferred_element_type=F32)


def folded(values):
    rows, width = values.shape
    return values.reshape(rows // 8, 8, width).sum(axis=0)


def silu_half(half):
    return half + half * jnp.tanh(half)


def slope_half(half):
    bend = jnp.tanh(half)
    return 0.5 * (1.0 + bend + half * (1.0 - bend * bend))


def split(values):
    high = values.astype(BF16)
    return high, (values - high.astype(F32)).astype(BF16)


def line_levels(lines):
    return [lines] if lines <= 8 else [lines // 8, 8]


def kernel(names, batches, phases, in_rows, slots, *refs):
    k = types.SimpleNamespace(**dict(zip(names, refs, strict=True)))
    out_rows = in_rows // 4
    plane = out_rows + 2 * PAD
    chunk = out_rows // 5
    part = out_rows // 25
    blocks = out_rows // BLOCK
    per = part // BLOCK
    me = lax.axis_index("batch")
    stage = lax.axis_index("phase")
    core = lax.rem(me, 2)
    line = lax.div(me, 2)
    lines = batches // 2
    group = 2 * phases
    mine = 2 * stage + core
    levels = line_levels(lines)
    half_bank = BANK // 2
    quarter = in_rows // 4
    feat, t1, big0, big1, big2, src = k.feat, k.t1, k.big0, k.big1, k.big2, k.src
    tab, masks, wst, wts, gw, wide2, gn = k.tab, k.masks, k.wst, k.wts, k.gw, k.wide2, k.gn

    def batch_peer(i):
        return {"batch": lax.rem(me + i, batches)}

    def phase_peer(i):
        return {"phase": lax.rem(stage + i, phases)}

    def remote(source, target, send_sem, recv_sem, device):
        return pltpu.make_async_remote_copy(
            src_ref=source,
            dst_ref=target,
            send_sem=send_sem,
            recv_sem=recv_sem,
            device_id=device,
            device_id_type=MESH,
        )

    def wait_for(sem, region):
        pltpu.make_async_copy(region, region, sem).wait()

    barrier = pltpu.get_barrier_semaphore()

    def greet(i, carry):
        pl.semaphore_signal(barrier, inc=1, device_id=batch_peer(i), device_id_type=MESH)
        return carry

    lax.fori_loop(1, batches, greet, 0)
    for i in range(1, phases):
        for other in (me, 2 * line + 1 - core):
            pl.semaphore_signal(
                barrier,
                inc=1,
                device_id={"phase": lax.rem(stage + i, phases), "batch": other},
                device_id_type=MESH,
            )

    raw_copy = pltpu.make_async_copy(k.weights_at, k.raw, k.raw_sem)
    raw_copy.start()
    feat_copies = []
    for i in range(4):
        copy = pltpu.make_async_copy(
            k.features_at.at[pl.ds(pl.multiple_of(stage * in_rows + i * quarter, 16), quarter)],
            feat.at[pl.ds(i * quarter, quarter)],
            k.feat_sem.at[i],
        )
        copy.start()
        feat_copies.append(copy)
    neg_copy = pltpu.make_async_copy(k.negatives_at.at[0], k.neg, k.neg_sem)
    neg_copy.start()
    bank_copies = [
        pltpu.make_async_copy(
            k.bank_at.at[pl.ds(i * half_bank, half_bank)],
            big0.at[pl.ds(0, half_bank)],
            k.bank_sem.at[i],
        )
        for i in range(2)
    ]

    def side_of(kind):
        return SIDE_UNIT * jnp.where(
            kind == 1, 5, jnp.where(kind == 2, 7, jnp.where(kind == 3, 9, 0))
        )

    sides = [side_of(k.kinds[slot, stage, me]) for slot in range(slots)]
    ends = []
    for side in sides:
        ends.append(side * side + (ends[-1] if ends else 0))
    starts = [0, *ends[:-1]]
    rows_live = ends[-1]

    def all_areas(i, carry):
        for slot in range(slots):
            side = side_of(k.kinds[slot, stage, i])
            carry = carry + side * side
        return carry

    live_pixels = lax.fori_loop(0, batches, all_areas, 0)
    inverse_count = 1.0 / jnp.full((1, LANES), live_pixels, jnp.int32).astype(F32)[:, 0:1]

    def place(first):
        base = jnp.zeros_like(first)
        width = jnp.zeros_like(first)
        slot = jnp.full_like(first, 7)
        for number in range(slots):
            inside = (first >= starts[number]) & (first < ends[number])
            base = jnp.where(inside, starts[number], base)
            width = jnp.where(inside, sides[number], width)
            slot = jnp.where(inside, number, slot)
        return base, width, slot

    def divided(value, side):
        factor = jnp.zeros_like(side)
        for kind in (5, 7, 9):
            factor = jnp.where(side == SIDE_UNIT * kind, 65536 // (SIDE_UNIT * kind) + 1, factor)
        return lax.shift_right_logical(value * factor, jnp.full_like(value, 16))

    index = lax.broadcasted_iota(jnp.int32, (1, TABLE), 1)
    first = BLOCK * index
    base, width, slot = place(first)
    live = width > 0
    local = jnp.where(live, first - base, 0)
    row = divided(local, width)
    left = jnp.where(live, (row + 1) * width - local, BLOCK)
    begin = jnp.where(live, 4 * base + 2 * (local + row * width), 4 * first)
    jump = jnp.where(left < BLOCK, 2 * width, 0)
    window_at = lax.shift_right_logical(
        index * (65536 // per + 1), jnp.full_like(index, 16)
    ) * (4 * part) - AHEAD
    in_window = begin - jnp.maximum(window_at, 0)
    pixel = BLOCK // 4 * index
    in_base, in_width, unused_slot = place(pixel)
    in_live = in_width > 0
    in_side = jnp.maximum(in_width, 1)
    in_local = 4 * (pixel - in_base)
    in_row = divided(2 * (pixel - in_base), in_width)
    in_left = jnp.where(in_live, (2 * in_side - (in_local - in_row * 2 * in_side)) >> 1, 8)
    upper = in_row >> 1
    odd = in_row - 2 * upper
    lower = (in_row + 1) >> 1
    here = in_base + upper * in_side + (in_side - in_left)
    below = in_base + lower * in_side - in_left
    at_here = jnp.where(in_live, PAD + here + odd * (2 * plane), PAD + out_rows - BLOCK)
    at_below = jnp.where(in_left < 8, PAD + below + (1 - odd) * (2 * plane), at_here)
    even_here = jnp.where(in_live & (odd == 0), PAD + here, 0)
    even_below = jnp.where(in_live & (in_left < 8) & (odd == 1), PAD + below, 0)
    columns = (width, local, begin, left, jump, slot, 2 * width)
    columns = columns + (at_here, at_below, in_left, even_here, even_below, in_window)
    k.tabv[...] = jnp.zeros(k.tabv.shape, jnp.int32)
    for number, column in enumerate(columns):
        k.tabv[number : number + 1, :] = column
    tab_copy = pltpu.make_async_copy(k.tabv, tab, k.tab_sem)
    tab_copy.start()

    raw_copy.wait()

    def to_rows(first, last):
        def body(i, carry):
            found = []
            for u in range(16):
                at = pl.multiple_of((i * 16 + u) * LANES, LANES)
                found.append(k.raw[0:1, pl.ds(at, LANES)].astype(F32))
            for u, values in enumerate(found):
                wst[pl.ds(i * 16 + u, 1), :] = values
            return carry

        lax.fori_loop(first // 16, last // 16, body, 0)
        done = last // 16 * 16
        for at in range(done, last):
            wst[at : at + 1, :] = k.raw[0:1, at * LANES : (at + 1) * LANES].astype(F32)
        if done < last:
            wst[last : done + 16, :] = jnp.zeros((done + 16 - last, LANES), F32)

        def convert(i, carry):
            rows = pl.ds(pl.multiple_of(i * 16, 16), 16)
            wts[stage, rows, :] = wst[rows, :].astype(BF16)
            return carry

        lax.fori_loop(first // 16, -(-last // 16), convert, 0, unroll=2)

    weight_spans = ((0, EARLY), (EARLY, ROWS - EARLY))

    def send_weights(number):
        at, rows = weight_spans[number]
        region = wts.at[stage, pl.ds(at, rows)]
        copies = []
        for i in range(1, phases):
            copy = remote(
                region,
                region,
                k.weight_send.at[number, i],
                k.weight_recv.at[number, stage],
                phase_peer(i),
            )
            copy.start()
            copies.append(copy)
        return copies

    def need_weights(number, section):
        at, rows = weight_spans[number]

        @pl.when(stage != section)
        def unused_wait():
            wait_for(k.weight_recv.at[number, section], wts.at[section, pl.ds(at, rows)])

    to_rows(0, EARLY)
    pl.semaphore_wait(barrier, batches - 1 + 2 * (phases - 1))
    weight_copies = send_weights(0)

    def outgoing(number):
        if number in SPANS:
            return k.send.at[pl.ds(STARTS[number], SPANS[number])]
        return k.send_narrow.at[number]

    def incoming(number, which):
        if number in SPANS:
            return k.recv.at[which, pl.ds(STARTS[number], SPANS[number])]
        return k.recv_narrow.at[number, which]

    def share(number):
        def give(i, carry):
            remote(
                outgoing(number),
                incoming(number, me),
                k.stat_send.at[number],
                k.stat_recv.at[number],
                {"batch": lax.rem(batches - 1 - me + i, batches)},
            ).start()
            return carry

        mirrored = lax.rem(2 * me + 1, batches)

        def skip(i, carry):
            return give(i + jnp.where(i >= mirrored, 1, 0), carry)

        lax.fori_loop(0, batches - 1, skip, 0, unroll=batches <= 8)
        incoming(number, me)[...] = outgoing(number)[...]

    def collect(number):
        wait_for(k.stat_recv.at[number], incoming(number, pl.ds(0, batches - 1)))

        def add(i, carry):
            return carry + incoming(number, i)[...]

        rows = SPANS.get(number, 2)
        k.total[pl.ds(0, rows), :] = lax.fori_loop(
            1, batches, add, incoming(number, 0)[...], unroll=batches <= 8
        )

    padded = [-(-rows // (16 * group)) * 16 * group for unused, rows in PIECES]
    piece_at = [sum(padded[:i]) for i in range(len(padded))]
    section_at = [0, 0, 0, 0, padded[FIRST_MID]]
    part_of = [rows // group for rows in padded]

    def summed(rows, target, *sources):
        total = sources[0](0, rows).astype(F32)
        for source in sources[1:]:
            total = total + source(0, rows).astype(F32)
        target(0, rows, total.astype(BF16))

    def reader(ref, start):
        return lambda at, step: ref[pl.ds(pl.multiple_of(start + at, 16), step), :]

    def writer(ref, start):
        def write(at, step, values):
            ref[pl.ds(pl.multiple_of(start + at, 16), step), :] = values

        return write

    def give_scatter(number):
        rows, at = part_of[number], piece_at[number]

        def give(i, carry):
            other = lax.rem(mine + i, group)
            remote(
                k.gb.at[pl.ds(at + other * rows, rows)],
                k.got_scatter.at[i - 1, pl.ds(at // group, rows)],
                k.scatter_send.at[number],
                k.scatter_recv.at[number],
                {"phase": lax.div(other, 2), "batch": 2 * line + lax.rem(other, 2)},
            ).start()
            return carry

        lax.fori_loop(1, group, give, 0)

    def give_line(number):
        rows, at = part_of[number], piece_at[number]
        within = at // group
        wait_for(k.scatter_recv.at[number], k.got_scatter.at[:, pl.ds(within, rows)])

        def other(i):
            return lambda start, step: k.got_scatter[i, pl.ds(within + start, step), :]

        summed(
            rows,
            writer(k.line_sum.at[0], within),
            reader(k.gb, at + mine * rows),
            *[other(i) for i in range(group - 1)],
        )
        send_level(number, 0)

    def level_of(level):
        size, stride = levels[level], math.prod(levels[:level])
        return size, stride, sum(levels[:level]) - level, lax.rem(lax.div(line, stride), size)

    def send_level(number, level):
        size, stride, slot, digit = level_of(level)
        rows, within = part_of[number], piece_at[number] // group

        def give(i, carry):
            other = line + (lax.rem(digit + i, size) - digit) * stride
            remote(
                k.line_sum.at[level, pl.ds(within, rows)],
                k.got_line.at[slot + i - 1, pl.ds(within, rows)],
                k.line_send.at[level, number],
                k.line_recv.at[level, number],
                {"batch": 2 * other + core},
            ).start()
            return carry

        lax.fori_loop(1, size, give, 0)

    def add_level(number, level, target):
        size, stride, slot, digit = level_of(level)
        rows, within = part_of[number], piece_at[number] // group
        arrived = k.got_line.at[pl.ds(slot, size - 1), pl.ds(within, rows)]
        wait_for(k.line_recv.at[level, number], arrived)

        own = k.line_sum[level, pl.ds(within, rows), :].astype(F32)
        total = jnp.zeros((rows, LANES), F32)
        for which in range(size):
            at = jnp.minimum(lax.rem(digit - which - 1 + size, size), size - 2)
            found = k.got_line[slot + at, pl.ds(within, rows), :].astype(F32)
            total = total + jnp.where(which == digit, own, found)
        target[pl.ds(within, rows), :] = total.astype(BF16)

    def give_home(number):
        section = PIECES[number][0]
        rows, at = part_of[number], piece_at[number]
        within = at // group
        for level in range(len(levels) - 1):
            add_level(number, level, k.line_sum.at[level + 1])
            send_level(number, level + 1)
        add_level(number, len(levels) - 1, k.home)
        target = k.got_all.at[pl.ds(section_at[number] + mine * rows, rows)]

        def give(other):
            remote(
                k.home.at[pl.ds(within, rows)],
                target,
                k.home_send.at[number],
                k.home_recv.at[number],
                {"phase": section, "batch": 2 * line + other},
            ).start()

        @pl.when(stage != section)
        def unused_both():
            give(0)
            give(1)

        @pl.when(stage == section)
        def unused_one():
            give(1 - core)
            target[...] = k.home[pl.ds(within, rows), :]

    def take_all(number):
        rows, within = part_of[number], section_at[number]

        @pl.when(stage == PIECES[number][0])
        def unused_take():
            wait_for(k.home_recv.at[number], k.got_all.at[pl.ds(within, (group - 1) * rows)])

    def end_sends(number):
        rows, at = part_of[number], piece_at[number]
        within = at // group
        wait_for(k.scatter_send.at[number], k.got_scatter.at[:, pl.ds(within, rows)])
        for level in range(len(levels)):
            size, unused_stride, slot, unused_digit = level_of(level)
            sent = k.got_line.at[pl.ds(slot, size - 1), pl.ds(within, rows)]
            wait_for(k.line_send.at[level, number], sent)

        @pl.when(stage != PIECES[number][0])
        def unused_away():
            wait_for(k.home_send.at[number], k.got_all.at[pl.ds(0, 2 * rows)])

        @pl.when(stage == PIECES[number][0])
        def unused_home():
            wait_for(k.home_send.at[number], k.got_all.at[pl.ds(0, rows)])

    def stage_piece(number):
        rows, used, at = padded[number], PIECES[number][1], piece_at[number]
        if used < rows:
            wst[used:rows, :] = jnp.zeros((rows - used, LANES), F32)

        def convert(i, carry):
            start = pl.multiple_of(i * 64, 64)
            k.gb[pl.ds(at + start, 64), :] = wst[pl.ds(start, 64), :].astype(BF16)
            return carry

        lax.fori_loop(0, rows // 64, convert, 0)
        give_scatter(number)

    def put_narrow(number, row, vector):
        k.send_narrow[number, row : row + 1, :] = vector

    def put_wide(number, row, vectors):
        for j, vector in enumerate(vectors):
            at = STARTS[number] + 4 * row + j
            k.send[at : at + 1, :] = vector

    def put_small(row, vector):
        k.small[row : row + 1, :] = vector

    def narrow(row):
        return k.total[row : row + 1, :]

    def wide(row):
        return jnp.concatenate([k.total[4 * row + j : 4 * row + j + 1, :] for j in range(4)], axis=1)

    def reduced(values):
        return jnp.sum(values, axis=0, keepdims=True)

    def gain_narrow(row):
        return k.gains[row : row + 1, :]

    def gain_wide(row):
        return jnp.concatenate([k.gains[row + j : row + j + 1, :] for j in range(4)], axis=1)

    def put_coef(layer, what, vector):
        row = 8 * layer + what
        k.coef[row : row + 1, 0 : vector.shape[1]] = vector

    def lanes(j):
        return slice(j * LANES, (j + 1) * LANES)

    def get_coef(layer, what, j=0):
        row = 8 * layer + what
        return k.coef[row : row + 1, lanes(j)]

    def finish(layer, sums, squares, gain, bias, count_inverse):
        mean = sums * count_inverse
        inverse = lax.rsqrt(squares * count_inverse - mean * mean + EPSILON)
        scale = inverse * gain
        put_coef(layer, INVERSE, inverse)
        put_coef(layer, NEG_MEAN, -mean * inverse)
        put_coef(layer, HALF_SCALE, 0.5 * scale)
        put_coef(layer, HALF_SHIFT, 0.5 * (bias - mean * scale))

    def normed_sum(layer, sums, products, j=0):
        return products * get_coef(layer, INVERSE, j) + sums * get_coef(layer, NEG_MEAN, j)

    def finish_back(layer, sums, dots, gain, count_inverse):
        width = sums.shape[1]
        row = 8 * layer
        inverse = k.coef[row + INVERSE : row + INVERSE + 1, 0:width]
        scale = inverse * gain
        slant = scale * dots * count_inverse
        put_coef(layer, GRAD_A, scale)
        put_coef(layer, GRAD_E, slant * inverse)
        put_coef(
            layer,
            GRAD_D,
            scale * sums * count_inverse
            + slant * k.coef[row + NEG_MEAN : row + NEG_MEAN + 1, 0:width],
        )

    def put_late(stores):
        for ref, at, value in stores:
            ref[at] = value

    def each_part(body, carry=0, parts=1):
        def step(i, inner):
            stores = []
            for u in range(parts):
                inner, found = body(pl.multiple_of((i * parts + u) * part, 16), inner)
                stores = stores + found
            put_late(stores)
            return inner

        return lax.fori_loop(0, 25 // parts, step, carry, unroll=UNROLL if parts == 1 else 1)

    def each_chunk(body, carry=0):
        def step(i, inner):
            return body(pl.multiple_of(i * chunk, 16), inner)

        return lax.fori_loop(0, 5, step, carry, unroll=UNROLL)

    def each_block(body):
        def step(i, carry):
            stores = []
            for u in range(per):
                number = i * per + u
                stores = stores + body(number, pl.multiple_of(number * BLOCK, 16))
            put_late(stores)
            return carry

        lax.fori_loop(0, blocks // per, step, 0, unroll=UNROLL)

    def zeros(width=MID):
        return jnp.zeros((8, width), F32)

    def live_rows(start, rows):
        return lax.broadcasted_iota(jnp.int32, (rows, LANES), 0) + start < rows_live

    def near_rows(rows, number):
        return lax.broadcasted_iota(jnp.int32, (rows, LANES), 0) < number

    def live_block(width):
        return jnp.broadcast_to(jnp.where(width > 0, 1.0, 0.0), (BLOCK, LANES)).astype(BF16)

    def at_block(buffer, j, start, rows):
        return buffer[pl.ds(j * out_rows + start, rows), :]

    def wide_store(buffer, start, values):
        rows = values.shape[0]
        for j in range(4):
            buffer[pl.ds(j * out_rows + start, rows), :] = values[:, lanes(j)]

    def added(carry, values):
        return carry[0] + folded(values), carry[1] + folded(values * values)

    def product_sums(left, right, store, masked=False):
        width = right.shape[1]

        def body(start, carry):
            values = dense(left[pl.ds(start, chunk), :], right[...])
            store(start, values)
            if masked:
                values = jnp.where(live_rows(start, chunk), values, 0.0)
            return added(carry, values)

        return each_chunk(body, (zeros(width), zeros(width)))

    def store_narrow(target):
        def store(start, values):
            target[pl.ds(start, values.shape[0]), :] = values

        return store

    def send_narrow(number, sums):
        put_narrow(number, 0, reduced(sums[0]))
        put_narrow(number, 1, reduced(sums[1]))
        share(number)

    def by_lanes(vector):
        return [vector[:, lanes(j)] for j in range(4)]

    def stage_section(section):
        def step(i, carry):
            start = pl.multiple_of(i * (ROWS // 7), 16)
            wst[pl.ds(start, ROWS // 7), :] = wts[section, pl.ds(start, ROWS // 7), :].astype(F32)
            return carry

        lax.fori_loop(0, 7, step, 0)

    def unpack_wide(at, rows, target):
        for j in range(4):
            for r in range(rows // LANES):
                piece = wst[pl.ds(at + 4 * LANES * r + j, LANES, stride=4), :]
                target[r * LANES : (r + 1) * LANES, lanes(j)] = piece.astype(BF16)

    def take_gain(row, at, rows=1):
        k.gains[row : row + rows, :] = wst[at : at + rows, :]

    def turned(piece):
        return piece.astype(BF16).T

    tab_copy.wait()
    src[0:PAD, :] = jnp.zeros((PAD, LANES), F32)
    src[PAD + out_rows : plane, :] = jnp.zeros((PAD, LANES), F32)
    for number in range(4):
        big0[number * plane : number * plane + PAD, :] = jnp.zeros((PAD, LANES), F32)

    def make_masks(number, start):
        width, local = tab[0, number], tab[1, number]
        pixel = lax.broadcasted_iota(jnp.int32, (BLOCK, LANES), 0).astype(F32) + local.astype(F32)
        side = jnp.maximum(width, 1).astype(F32)
        row = jnp.floor((pixel + 0.5) / side)
        column = pixel - row * side
        one = jnp.where(width > 0, 1.0, 0.0)
        found = (row > 0.5, row < side - 1.5, column > 0.5, column < side - 1.5)
        return [
            (
                masks,
                (which, pl.ds(start, BLOCK), slice(None)),
                jnp.where(condition, one, 0.0).astype(BF16),
            )
            for which, condition in enumerate(found)
        ]

    each_block(make_masks)
    to_rows(EARLY, ROW)
    weight_copies = weight_copies + send_weights(1)
    for copy in feat_copies:
        copy.wait()

    window_rows = AHEAD + 4 * part

    def shortcut_pixels(i, carry):
        low = pl.multiple_of(jnp.maximum(i * 4 * part - AHEAD, 0), 16)
        stores = []
        for half in range(2):
            gn[half * window_rows : (half + 1) * window_rows, :] = feat[
                pl.ds(low, window_rows), lanes(half)
            ].astype(F32)
        for u in range(per):
            number = i * per + u
            start = pl.multiple_of(number * BLOCK, 16)
            first = tab[12, number]
            second = first + tab[4, number]
            near = near_rows(BLOCK, tab[3, number])
            one = jnp.where(tab[0, number] > 0, 1.0, 0.0)
            for half in range(2):
                picked = jnp.where(
                    near,
                    gn[pl.ds(half * window_rows + first, BLOCK, stride=2), :],
                    gn[pl.ds(half * window_rows + second, BLOCK, stride=2), :],
                )
                stores.append(
                    (k.xs, (pl.ds(start, BLOCK), lanes(half)), (picked * one).astype(BF16))
                )
        put_late(stores)
        return carry

    lax.fori_loop(0, 25, shortcut_pixels, 0)

    need_weights(0, 0)
    def open_first(step, carry):
        start = pl.multiple_of(step * chunk, 16)
        values = dense(feat[pl.ds(start, chunk), :], wts[0, 0:CIN, :])
        t1[pl.ds(start, chunk), :] = values
        rows = lax.broadcasted_iota(jnp.int32, values.shape, 0) + start
        return added(carry, jnp.where(rows < 4 * rows_live, values, 0.0))

    sums = lax.fori_loop(0, in_rows // chunk, open_first, (zeros(), zeros()), unroll=UNROLL)
    send_narrow(0, sums)

    need_weights(1, 0)
    stage_section(0)
    take_gain(0, IN_GAIN, 2)
    take_gain(2, MID_GAIN, 2)
    k.wmid1[...] = wst[MID_AT : MID_AT + 9 * MID, :].astype(BF16)

    def first_products(block):
        rows = slice(block * out_rows, (block + 1) * out_rows)
        live = (
            lax.broadcasted_iota(jnp.int32, (out_rows, MID), 0) + block * out_rows < 4 * rows_live
        )
        k.turn[0:LANES, :] = turned(jnp.where(live, t1[rows, :], 0.0))
        live = lax.broadcasted_iota(jnp.int32, (16, out_rows), 1) + block * out_rows < 4 * rows_live
        k.turn[LANES : LANES + 16, :] = jnp.where(live, 1.0, 0.0).astype(BF16)
        found = dense(k.turn[...], feat[rows, :])
        for half in range(2):
            at = slice(half * LANES, (half + 1) * LANES)
            product = found[0:LANES, lanes(half)].T
            total = jnp.broadcast_to(found[LANES : LANES + 1, lanes(half)], (LANES, LANES)).T
            k.first_t[at, :] = product if block == 0 else k.first_t[at, :] + product
            k.first_s[at, :] = total if block == 0 else k.first_s[at, :] + total

    first_products(0)
    collect(0)
    finish(L1, narrow(0), narrow(1), gain_narrow(0), gain_narrow(1), 0.25 * inverse_count)

    def first_hidden(number, start):
        scale, shift = get_coef(L1, HALF_SCALE), get_coef(L1, HALF_SHIFT)
        near = near_rows(BLOCK, tab[3, number])
        stores = []
        for row in range(2):
            for column in range(2):
                first = tab[2, number] + column + (tab[6, number] if row else 0)
                values = jnp.where(
                    near,
                    t1[pl.ds(first, BLOCK, stride=2), :],
                    t1[pl.ds(first + tab[4, number], BLOCK, stride=2), :],
                )
                at = pl.ds((2 * row + column) * plane + PAD + start, BLOCK)
                stores.append((big0, (at, slice(None)), silu_half(values * scale + shift)))
        return stores

    each_block(first_hidden)

    def wide_columns(number, start):
        width = tab[0, number]
        here = pl.ds(start, BLOCK)
        top, left, live = masks[0, here, :], masks[2, here, :], live_block(width)
        corner = top * left
        stores = []
        for tap in range(9):
            i, j = tap // 3, tap % 3
            at = (2 * (0 if i == 1 else 1) + (0 if j == 1 else 1)) * plane + PAD + start
            at = at - (width if i == 0 else 0) - (1 if j == 0 else 0)
            mask = (corner if j == 0 else top) if i == 0 else (left if j == 0 else live)
            values = big0[pl.ds(at, BLOCK), :].astype(BF16) * mask
            stores.append((k.cols1, (here, lanes(tap)), values))
        return stores

    each_block(wide_columns)
    send_narrow(1, product_sums(k.cols1, k.wmid1, store_narrow(k.t2)))

    bank_copies[0].start()
    need_weights(0, 1)
    need_weights(1, 1)
    stage_section(1)
    take_gain(8, OUT_GAIN, 8)
    take_gain(16, SHORT_GAIN, 8)
    unpack_wide(0, MID, k.wout2)
    unpack_wide(AFTER_OUT, CIN, k.wshort)
    short_sums = product_sums(k.xs, k.wshort, functools.partial(wide_store, big2))
    put_wide(2, 2, by_lanes(reduced(short_sums[0])))
    put_wide(2, 3, by_lanes(reduced(short_sums[1])))

    def close_narrow(layer, source, target):
        def body(start, carry):
            half = source[pl.ds(start, part), :] * get_coef(layer, HALF_SCALE) + get_coef(
                layer, HALF_SHIFT
            )
            values = jnp.where(live_rows(start, part), silu_half(half), 0.0).astype(BF16)
            return carry, [(target, (pl.ds(start, part), slice(None)), values)]

        each_part(body, parts=5)

    collect(1)
    finish(L2, narrow(0), narrow(1), gain_narrow(2), gain_narrow(3), inverse_count)
    close_narrow(L2, k.t2, k.h2)

    roomy = hasattr(k, "slope23")

    def worked_slope(layer, values):
        return slope_half(values * get_coef(layer, HALF_SCALE) + get_coef(layer, HALF_SHIFT))

    def keep_narrow_slope(layer, source, target):
        def body(start, carry):
            here = pl.ds(start, part)
            values = worked_slope(layer, source[here, :]).astype(BF16)
            return carry, [(target, (here, slice(None)), values)]

        each_part(body, parts=5)

    def second_slope(j, start):
        if roomy:
            return k.slope23[pl.ds(start, part), lanes(j)].astype(F32)
        return slope_half(second_half(j, start))

    def keep_second_slope():
        def body(start, carry):
            return carry, [
                (
                    k.slope23,
                    (pl.ds(start, part), lanes(j)),
                    slope_half(second_half(j, start)).astype(BF16),
                )
                for j in range(4)
            ]

        if roomy:
            each_part(body)

    def keep_first_slope():
        def body(start, carry):
            return carry, [
                (
                    k.cols2,
                    (pl.ds(start, part), lanes(block)),
                    worked_slope(L1, t1[pl.ds(block * out_rows + start, part), :]).astype(BF16),
                )
                for block in range(4)
            ]

        each_part(body)

    sums = product_sums(k.h2, k.wout2, functools.partial(wide_store, big1))
    put_wide(2, 0, by_lanes(reduced(sums[0])))
    put_wide(2, 1, by_lanes(reduced(sums[1])))
    share(2)

    def bank_to_bf16(half):
        bank_copies[half].wait()

        def body(i, carry):
            start = pl.multiple_of(i * 128, 128)
            for j in range(2):
                wide2[pl.ds(start, 128), lanes(2 * half + j)] = big0[
                    pl.ds(j * (BANK // 4) + start, 128), :
                ].astype(BF16)
            return carry

        lax.fori_loop(0, BANK // 4 // 128, body, 0)

    need_weights(0, 2)
    need_weights(1, 2)
    stage_section(2)
    take_gain(4, THIRD_GAIN, 2)
    take_gain(6, THIRD_MID_GAIN, 2)
    k.wmid3[...] = wst[THIRD_MID : THIRD_MID + 9 * MID, :].astype(BF16)
    bank_to_bf16(0)
    bank_copies[1].start()
    collect(2)
    finish(L3, wide(0), wide(1), gain_wide(8), gain_wide(12), inverse_count)
    finish(LS, wide(2), wide(3), gain_wide(16), gain_wide(20), inverse_count)

    def second_half(j, start):
        return (
            at_block(big1, j, start, part) * get_coef(L3, HALF_SCALE, j)
            + at_block(big2, j, start, part) * get_coef(LS, HALF_SCALE, j)
            + (get_coef(L3, HALF_SHIFT, j) + get_coef(LS, HALF_SHIFT, j))
        )

    def close_second(start, carry):
        stores = []
        for j in range(4):
            values = silu_half(second_half(j, start)).astype(BF16)
            stores.append((k.y, (pl.ds(start, part), lanes(j)), values))
        return carry, stores

    each_part(close_second)

    send_narrow(3, product_sums(k.y, wts.at[2, pl.ds(0, COUT)], store_narrow(k.t4), True))
    need_weights(0, 3)
    need_weights(1, 3)
    stage_section(3)
    take_gain(24, OUT_GAIN, 8)
    unpack_wide(0, MID, k.wout4)
    bank_to_bf16(1)
    first_products(1)
    keep_second_slope()
    collect(3)
    finish(L4, narrow(0), narrow(1), gain_narrow(4), gain_narrow(5), inverse_count)

    def third_hidden(start, carry):
        half = k.t4[pl.ds(start, part), :] * get_coef(L4, HALF_SCALE) + get_coef(L4, HALF_SHIFT)
        return carry, [(src, (pl.ds(PAD + start, part), slice(None)), silu_half(half))]

    each_part(third_hidden, parts=5)

    def near_columns(number, start, target, target_start):
        width = tab[0, number]
        here = pl.ds(start, BLOCK)
        top, bottom, left, right = (masks[which, here, :] for which in range(4))
        live = live_block(width)
        stores = []
        for tap in range(9):
            i, j = tap // 3, tap % 3
            at = PAD + start + (i - 1) * width + (j - 1)
            mask = (top, live, bottom)[i]
            if j != 1:
                beside = left if j == 0 else right
                mask = beside if i == 1 else mask * beside
            values = src[pl.ds(at, BLOCK), :].astype(BF16) * mask
            stores.append((target, (pl.ds(target_start, BLOCK), lanes(tap)), values))
        return stores

    each_block(lambda number, start: near_columns(number, start, k.cols2, start))
    send_narrow(4, product_sums(k.cols2, k.wmid3, store_narrow(k.t5)))

    neg_copy.wait()
    gn[0 : 8 * LANES, :] = jnp.zeros((8 * LANES, LANES), F32)
    neg_piece = 512
    for slot in range(slots):

        def count(i, carry, slot=slot):
            at = pl.multiple_of(i * neg_piece, neg_piece)
            found = k.neg[slot, pl.ds(stage, 1), pl.ds(at, neg_piece)]
            spot = lax.broadcasted_iota(jnp.int32, (LANES, neg_piece), 0)
            upper = lax.shift_right_logical(found, 7)
            high = jnp.where(spot == upper, 1.0, 0.0).astype(BF16)
            low = jnp.where(spot == found - LANES * upper, 1.0, 0.0).astype(BF16)
            return carry + across(high, low)

        found = lax.fori_loop(
            0, NEG // neg_piece, count, jnp.zeros((LANES, LANES), F32), unroll=True
        )
        gn[pl.ds(slot, LANES, stride=8), :] = found
    collect(4)
    finish(L5, narrow(0), narrow(1), gain_narrow(6), gain_narrow(7), inverse_count)
    close_narrow(L5, k.t5, k.h4)

    sums = product_sums(k.h4, k.wout4, functools.partial(wide_store, big0))
    put_wide(5, 0, by_lanes(reduced(sums[0])))
    put_wide(5, 1, by_lanes(reduced(sums[1])))
    share(5)
    for j in range(4):
        k.wout4_t[j * LANES : (j + 1) * LANES, :] = turned(k.wout4[:, lanes(j)])
    for tap in range(9):
        k.wmid3_t[(8 - tap) * MID : (9 - tap) * MID, :] = turned(
            k.wmid3[tap * MID : (tap + 1) * MID, :]
        )
    for r in range(4):
        k.win3_t[:, lanes(r)] = turned(wts[2, r * LANES : (r + 1) * LANES, :])
    first_products(2)
    keep_narrow_slope(L5, k.t5, k.dtn)
    collect(5)
    finish(L6, wide(0), wide(1), gain_wide(24), gain_wide(28), inverse_count)

    def last_half(j, start):
        return (
            at_block(big0, j, start, part) * get_coef(L6, HALF_SCALE, j)
            + get_coef(L6, HALF_SHIFT, j)
            + 0.5 * k.y[pl.ds(start, part), lanes(j)].astype(F32)
        )

    def close_last(start, carry):
        return carry, [
            (gw, (pl.ds(start, part), lanes(j)), silu_half(last_half(j, start)).astype(BF16))
            for j in range(4)
        ]

    each_part(close_last)

    def pool(start, carry):
        rows = lax.broadcasted_iota(jnp.int32, (8, chunk), 1) + start
        owner = jnp.zeros((8, chunk), jnp.int32)
        for end in ends:
            owner = owner + jnp.where(rows >= end, 1, 0)
        mine = owner == lax.broadcasted_iota(jnp.int32, (8, chunk), 0)
        mine = jnp.where(mine, 1.0, 0.0).astype(BF16)
        return carry + dense(mine, gw[pl.ds(start, chunk), :])

    slot_row = lax.broadcasted_iota(jnp.int32, (8, LANES), 0)
    area = jnp.zeros((8, LANES), jnp.int32)
    positive = jnp.full((8, LANES), -1, jnp.int32)
    for slot in range(slots):
        area = jnp.where(slot_row == slot, sides[slot] * sides[slot], area)
        positive = jnp.where(slot_row == slot, k.positives[0, stage, slot], positive)
    inverse_area = jnp.where(area > 0, 1.0 / jnp.maximum(area, 1).astype(F32), 0.0)
    inverse_area_wide = jnp.concatenate([inverse_area] * 4, axis=1)
    half_offset = 0.5 * jnp.log(jnp.full((8, LANES), k.normalizer[0] * NEG / BANK))
    pooled = each_chunk(pool, zeros(COUT)) * inverse_area_wide

    head = wst[AFTER_OUT : AFTER_OUT + COUT, :].astype(BF16)
    pooled_high, pooled_low = split(pooled)
    embed = dense(pooled_high, head) + dense(pooled_low, head)
    scale = lax.rsqrt(jnp.sum(embed * embed, axis=1, keepdims=True) + 1e-06)
    unit = embed * scale
    unit_parts = jnp.concatenate(split(unit), axis=0)
    lane = lax.broadcasted_iota(jnp.int32, (8, LANES), 1)
    parts = []
    for block in range(4):
        scores = across(unit_parts, wide2[:, lanes(block)])
        scores = scores[0:8, :] + scores[8:16, :]
        pieces = []
        for j in range(BANK // 4 // LANES):
            high = block * (BANK // 4 // LANES) + j
            half = scores[:, lanes(j)] * (0.5 / SOFTMAX_TEMPER) - half_offset
            sigma = 0.5 + 0.5 * jnp.tanh(half)
            chosen = jnp.where(positive == lane + high * LANES, 1.0, 0.0)
            pieces.append((gn[high * 8 : high * 8 + 8, :] + chosen) * sigma - chosen)
        parts = parts + list(split(jnp.concatenate(pieces, axis=1)))
    found = dense(jnp.concatenate(parts, axis=0), wide2[...])
    unit_grad = zeros(EMB)
    for block in range(4):
        for row in (16 * block, 16 * block + 8):
            unit_grad = unit_grad + found[row : row + 8, lanes(block)]
    unit_grad = jnp.where(inverse_area > 0.0, unit_grad, 0.0) * (1.0 / SOFTMAX_TEMPER)
    embed_grad = scale * unit_grad - embed * (
        scale * scale * scale * jnp.sum(embed * unit_grad, axis=1, keepdims=True)
    )
    grad_high, grad_low = split(embed_grad)
    pooled_grad = across(grad_high, head) + across(grad_low, head)
    pooled_grad = pooled_grad * inverse_area_wide
    for j in range(4):
        k.spread[8 * j : 8 * j + 8, :] = pooled_grad[:, lanes(j)]

    def last_slope(step, carry):
        start = pl.multiple_of(step * part, 16)
        owners = [tab[5, step * per + u] for u in range(per)]
        found, stores = [], []
        for j in range(4):
            upstream = jnp.concatenate(
                [
                    jnp.broadcast_to(k.spread[pl.ds(8 * j + owner, 1), :], (BLOCK, LANES))
                    for owner in owners
                ],
                axis=0,
            )
            upstream = upstream * slope_half(last_half(j, start))
            stores.append((gw, (pl.ds(start, part), lanes(j)), upstream.astype(BF16)))
            found.append(
                (
                    carry[j][0] + folded(upstream),
                    carry[j][1] + folded(upstream * at_block(big0, j, start, part)),
                )
            )
        put_late(stores)
        return tuple(found)

    pair = (zeros(), zeros())
    sums = lax.fori_loop(0, 25, last_slope, (pair,) * 4, unroll=UNROLL)
    bias_grads = [reduced(sums[j][0]) for j in range(4)]
    gain_grads = [normed_sum(L6, bias_grads[j], reduced(sums[j][1]), j) for j in range(4)]
    put_wide(6, 0, bias_grads)
    put_wide(6, 1, gain_grads)
    share(6)
    for j in range(4):
        wst[OUT_GAIN + j : OUT_GAIN + j + 1, :] = gain_grads[j]
        wst[OUT_BIAS + j : OUT_BIAS + j + 1, :] = bias_grads[j]
    wst[AFTER_OUT : AFTER_OUT + COUT, :] = (
        outer(pooled_high, grad_high) + outer(pooled_high, grad_low) + outer(pooled_low, grad_high)
    )
    for j in range(4):
        k.wout2_t[j * LANES : (j + 1) * LANES, :] = turned(k.wout2[:, lanes(j)])
        for r in range(2):
            k.wshort_t[j * LANES : (j + 1) * LANES, lanes(r)] = turned(
                k.wshort[r * LANES : (r + 1) * LANES, lanes(j)]
            )
    def put_turned(source, target, values):
        at = (target // 2) * 4 * MID + source * MID
        k.wmid1_t[at : at + MID, lanes(target % 2)] = values

    for tap in range(9):
        i, j = tap // 3, tap % 3
        source = 2 * (1 if i == 0 else 0) + (1 if j == 0 else 0)
        target = 2 * (0 if i == 1 else 1) + (0 if j == 1 else 1)
        put_turned(source, target, turned(k.wmid1[tap * MID : (tap + 1) * MID, :]))
    for source in range(4):
        for target in range(4):
            if source & target != source:
                put_turned(source, target, jnp.zeros((MID, MID), BF16))
    first_products(3)
    collect(6)
    finish_back(L6, wide(0), wide(1), gain_wide(24), inverse_count)

    def back_value(layer, upstream, values, j=0):
        return (
            upstream * get_coef(layer, GRAD_A, j)
            - values * get_coef(layer, GRAD_E, j)
            - get_coef(layer, GRAD_D, j)
        )

    def back_sixth(start, carry):
        here = pl.ds(start, part)
        stores = []
        for j in range(4):
            values = back_value(
                L6, gw[here, lanes(j)].astype(F32), at_block(big0, j, start, part), j
            )
            stores.append((wide2, (here, lanes(j)), values.astype(BF16)))
        return carry, stores

    each_part(back_sixth)

    def back_rows(values, slope):
        def body(start, carry):
            here = pl.ds(start, part)
            upstream = gn[here, :] * slope[here, :].astype(F32)
            upstream = jnp.where(live_rows(start, part), upstream, 0.0)
            carry = (carry[0] + folded(upstream), carry[1] + folded(upstream * values[here, :]))
            return carry, [(gn, (here, slice(None)), upstream)]

        return each_part(body, (zeros(), zeros()), parts=5)

    def send_back(number, row, layer, sums):
        bias_grad = reduced(sums[0])
        gain_grad = normed_sum(layer, bias_grad, reduced(sums[1]))
        put_narrow(number, 0, bias_grad)
        put_narrow(number, 1, gain_grad)
        share(number)
        put_small(row, gain_grad)
        put_small(row + 1, bias_grad)

    def rounded_product(left, right):
        def body(start, carry):
            here = pl.ds(start, chunk)
            gn[here, :] = dense(left[here, :], right[...]).astype(BF16).astype(F32)
            return carry

        each_chunk(body)

    rounded_product(wide2, k.wout4_t)
    send_back(7, 2, L5, back_rows(k.t5, k.dtn))

    def put_wide_matrix(at, values):
        for r in range(values.shape[0] // LANES):
            for j in range(4):
                wst[pl.ds(at + 4 * LANES * r + j, LANES, stride=4), :] = values[
                    r * LANES : (r + 1) * LANES, lanes(j)
                ]

    def turned_rows(ref, lane=0):
        return turned(ref[:, lane * LANES : (lane + 1) * LANES])

    k.turn[0:LANES, :] = turned_rows(k.h4)
    put_wide_matrix(0, dense(k.turn[0:LANES, :], wide2[0:out_rows, :]))
    stage_piece(LAST)
    keep_narrow_slope(L4, k.t4, k.h4)
    collect(7)
    finish_back(L5, narrow(0), narrow(1), gain_narrow(6), inverse_count)

    def back_close(layer, values):
        def body(start, carry):
            here = pl.ds(start, part)
            found = back_value(layer, gn[here, :], values[here, :])
            found = jnp.where(live_rows(start, part), found, 0.0).astype(BF16)
            return carry, [
                (k.dtn, (here, slice(None)), found),
                (src, (pl.ds(PAD + start, part), slice(None)), found.astype(F32)),
            ]

        each_part(body, parts=5)

    back_close(L5, k.t5)

    def open_back_fourth(step, carry):
        chunk_start = pl.multiple_of(step * chunk, 16)

        def fill(i, inner):
            stores = []
            for u in range(per):
                at = pl.multiple_of((i * per + u) * BLOCK, 16)
                number = step * (chunk // BLOCK) + i * per + u
                stores = stores + near_columns(number, chunk_start + at, k.colt, at)
            put_late(stores)
            return inner

        lax.fori_loop(0, chunk // BLOCK // per, fill, 0, unroll=UNROLL)
        gn[pl.ds(chunk_start, chunk), :] = dense(k.colt[...], k.wmid3_t[...])
        return carry

    lax.fori_loop(0, 5, open_back_fourth, 0, unroll=UNROLL)
    send_back(8, 0, L4, back_rows(k.t4, k.h4))

    def columns_grad(columns, store):
        k.turn[0:LANES, :] = turned_rows(k.dtn)
        for group in range(3):
            found = dense(k.turn[0:LANES, :], columns[:, 3 * group * LANES : 3 * (group + 1) * LANES])
            for j in range(3):
                store(3 * group + j, found[:, lanes(j)].T)

    def store_third(tap, values):
        wst[THIRD_MID + tap * MID : THIRD_MID + (tap + 1) * MID, :] = values

    columns_grad(k.cols2, store_third)
    give_line(LAST)
    keep_narrow_slope(L2, k.t2, k.h4)
    collect(8)
    finish_back(L4, narrow(0), narrow(1), gain_narrow(4), inverse_count)
    back_close(L4, k.t4)

    def back_block(start, carry):
        here = pl.ds(start, part)
        arrived = dense(k.dtn[here, :], k.win3_t[...])
        found, stores = [], []
        for j in range(4):
            upstream = arrived[:, lanes(j)] + gw[here, lanes(j)].astype(F32)
            upstream = upstream.astype(BF16).astype(F32) * second_slope(j, start)
            stores.append((gw, (here, lanes(j)), upstream.astype(BF16)))
            found.append(
                (
                    carry[j][0] + folded(upstream),
                    carry[j][1] + folded(upstream * at_block(big1, j, start, part)),
                    carry[j][2] + folded(upstream * at_block(big2, j, start, part)),
                )
            )
        return tuple(found), stores

    sums = each_part(back_block, ((zeros(), zeros(), zeros()),) * 4)
    bias_grads, gain_grads, short_grads = (
        [reduced(sums[j][which]) for j in range(4)] for which in range(3)
    )
    gain_grads = [normed_sum(L3, bias_grads[j], gain_grads[j], j) for j in range(4)]
    short_grads = [normed_sum(LS, bias_grads[j], short_grads[j], j) for j in range(4)]
    put_wide(9, 0, bias_grads)
    put_wide(9, 1, gain_grads)
    put_wide(9, 2, short_grads)
    share(9)
    k.turn[0:LANES, :] = turned_rows(k.dtn)
    found = dense(k.turn[0:LANES, :], k.y[...])
    for j in range(4):
        wst[j * LANES : (j + 1) * LANES, :] = found[:, lanes(j)].T
    wst[THIRD_GAIN : THIRD_BIAS + 1, :] = k.small[0:2, :]
    wst[THIRD_MID_GAIN : THIRD_MID_BIAS + 1, :] = k.small[2:4, :]
    stage_piece(THIRD)
    give_home(LAST)
    keep_first_slope()
    collect(9)
    finish_back(L3, wide(0), wide(1), gain_wide(8), inverse_count)
    finish_back(LS, wide(0), wide(2), gain_wide(16), inverse_count)

    def back_third(start, carry):
        here = pl.ds(start, part)
        below = pl.ds(out_rows + start, part)
        stores = []
        for j in range(4):
            upstream = gw[here, lanes(j)].astype(F32)
            found = back_value(L3, upstream, at_block(big1, j, start, part), j)
            stores.append((wide2, (here, lanes(j)), found.astype(BF16)))
            found = back_value(LS, upstream, at_block(big2, j, start, part), j)
            stores.append((wide2, (below, lanes(j)), found.astype(BF16)))
        return carry, stores

    each_part(back_third)
    rounded_product(wide2, k.wout2_t)
    send_back(10, 6, L2, back_rows(k.t2, k.h4))
    for j in range(4):
        wst[OUT_GAIN + j : OUT_GAIN + j + 1, :] = gain_grads[j]
        wst[OUT_BIAS + j : OUT_BIAS + j + 1, :] = bias_grads[j]
        wst[SHORT_GAIN + j : SHORT_GAIN + j + 1, :] = short_grads[j]
        wst[SHORT_BIAS + j : SHORT_BIAS + j + 1, :] = bias_grads[j]
    k.turn[0:LANES, :] = turned_rows(k.h2)
    put_wide_matrix(0, dense(k.turn[0:LANES, :], wide2[0:out_rows, :]))
    for half in range(2):
        k.turn[0:LANES, :] = turned_rows(k.xs, half)
        put_wide_matrix(
            AFTER_OUT + half * 4 * LANES, dense(k.turn[0:LANES, :], wide2[out_rows : 2 * out_rows, :])
        )
    stage_piece(SECOND)
    give_line(THIRD)

    def back_picked(start, carry):
        found = dense(wide2[pl.ds(out_rows + start, chunk), :], k.wshort_t[...])
        found = found.astype(BF16).astype(F32)
        for half in range(2):
            big2[pl.ds(half * plane + PAD + start, chunk), :] = found[:, lanes(half)]
        return carry

    each_chunk(back_picked)
    for half in range(2):
        big2[half * plane : half * plane + PAD, :] = jnp.zeros((PAD, LANES), F32)
    collect(10)
    finish_back(L2, narrow(0), narrow(1), gain_narrow(2), inverse_count)
    back_close(L2, k.t2)


    def back_columns(number, start):
        here = pl.ds(start, BLOCK)
        width = tab[0, number]
        bottom, right, live = masks[1, here, :], masks[3, here, :], live_block(width)
        shifts = ((0, live), (1, right), (width, bottom), (width + 1, bottom * right))
        return [
            (
                wide2,
                (here, lanes(which)),
                src[pl.ds(PAD + start + shift, BLOCK), :].astype(BF16) * mask,
            )
            for which, (shift, mask) in enumerate(shifts)
        ]

    each_block(back_columns)

    def back_planes(start, carry):
        here = pl.ds(start, chunk)
        even = dense(wide2[here, 0 : 2 * MID], k.wmid1_t[0 : 2 * MID, :])
        odd = dense(wide2[here, :], k.wmid1_t[4 * MID : 8 * MID, :])
        for number in range(4):
            found = (even, odd)[number // 2][:, lanes(number % 2)]
            big0[pl.ds(number * plane + PAD + start, chunk), :] = found
        return carry

    each_chunk(back_planes)

    in_unroll = 10

    def to_input_order(i, carry):
        stores = []
        for u in range(in_unroll):
            number = i * in_unroll + u
            first, second = tab[7, number], tab[8, number]
            near = near_rows(8, tab[9, number])
            for column in range(2):
                values = jnp.where(
                    near,
                    big0[pl.ds(first + column * plane, 8), :],
                    big0[pl.ds(second + column * plane, 8), :],
                )
                at = pl.ds(number * BLOCK + column, 8, stride=2)
                stores.append((big1, (at, slice(None)), values))
        put_late(stores)
        return carry

    lax.fori_loop(0, in_rows // BLOCK // in_unroll, to_input_order, 0, unroll=UNROLL)

    def back_first(start, carry):
        stores = []
        for block in range(4):
            rows = pl.ds(block * out_rows + start, part)
            upstream = big1[rows, :] * k.cols2[pl.ds(start, part), lanes(block)].astype(F32)
            carry = (carry[0] + folded(upstream), carry[1] + folded(upstream * t1[rows, :]))
            stores.append((big1, (rows, slice(None)), upstream))
        return carry, stores

    sums = each_part(back_first, (zeros(), zeros()))
    send_back(11, 4, L1, sums)
    def store_first(tap, values):
        at = piece_at[FIRST_MID] + tap * MID
        k.gb[at : at + MID, :] = values.astype(BF16)

    columns_grad(k.cols1, store_first)
    if padded[FIRST_MID] > 9 * MID:
        at = piece_at[FIRST_MID]
        k.gb[at + 9 * MID : at + padded[FIRST_MID], :] = jnp.zeros(
            (padded[FIRST_MID] - 9 * MID, LANES), BF16
        )
    give_scatter(FIRST_MID)
    give_line(SECOND)
    give_home(THIRD)

    found = jnp.zeros((MID, CIN), F32)
    for block in range(4):
        rows = slice(block * out_rows, (block + 1) * out_rows)
        k.turn[0:LANES, :] = turned(big1[rows, :])
        found = found + dense(k.turn[0:LANES, :], feat[rows, :])
    first_g = [found[:, lanes(half)].T for half in range(2)]
    for half in range(2):
        k.win1_t[:, lanes(half)] = turned(wts[0, half * LANES : (half + 1) * LANES, :])
    gn[...] = jnp.zeros(gn.shape, F32)
    collect(11)
    finish_back(L1, narrow(0), narrow(1), gain_narrow(0), 0.25 * inverse_count)

    at = piece_at[FIRST_IN]
    for half in range(2):
        rows = slice(half * LANES, (half + 1) * LANES)
        values = first_g[half] * get_coef(L1, GRAD_A) - k.first_t[rows, :] * get_coef(L1, GRAD_E)
        values = values - k.first_s[rows, :] * get_coef(L1, GRAD_D)
        k.gb[at + half * LANES : at + (half + 1) * LANES, :] = values.astype(BF16)
    k.gb[at + CIN : at + CIN + 16, :] = jnp.concatenate(
        [k.small[4:8, :], jnp.zeros((12, LANES), F32)], axis=0
    ).astype(BF16)
    k.gb[at + CIN + 16 : at + padded[FIRST_IN], :] = jnp.zeros(
        (padded[FIRST_IN] - CIN - 16, LANES), BF16
    )
    give_scatter(FIRST_IN)
    give_line(FIRST_MID)
    give_home(SECOND)

    for block in range(4):

        def close_back_first(start, carry, block=block):
            rows = pl.ds(block * out_rows + start, part)
            found = back_value(L1, big1[rows, :], t1[rows, :])
            row = lax.broadcasted_iota(jnp.int32, (part, MID), 0) + (block * out_rows + start)
            found = jnp.where(row < 4 * rows_live, found, 0.0).astype(BF16)
            return carry, [(gw, (pl.ds(start, part), lanes(block)), found)]

        each_part(close_back_first, parts=5)

    give_line(FIRST_IN)
    give_home(FIRST_MID)


    def input_grad(block, carry):
        lane = pl.ds(pl.multiple_of(block * LANES, LANES), LANES)
        for piece in range(5):
            low = (piece % 2) * 2 * chunk
            stores = []
            for u in range(chunk // BLOCK):
                number = (block * 5 + piece) * (chunk // BLOCK) + u
                near = near_rows(8, tab[9, number])
                for half in range(2):
                    values = jnp.where(
                        near,
                        big2[pl.ds(tab[10, number] + half * plane, 8), :],
                        big2[pl.ds(tab[11, number] + half * plane, 8), :],
                    )
                    at = low + half * chunk + u * BLOCK
                    stores.append((gn, (slice(at, at + BLOCK, 2), slice(None)), values))
            put_late(stores)
            found = dense(gw[piece * chunk : (piece + 1) * chunk, lane], k.win1_t[...])
            rows = pl.ds(pl.multiple_of(block * out_rows + piece * chunk, 16), chunk)
            for half in range(2):
                at = low + half * chunk
                feat[rows, lanes(half)] = (found[:, lanes(half)] + gn[at : at + chunk, :]).astype(
                    BF16
                )
        return carry

    lax.fori_loop(0, 2, input_grad, 0)
    give_home(FIRST_IN)
    lax.fori_loop(2, 4, input_grad, 0)
    input_copy = pltpu.make_async_copy(feat, k.input_grad_at, k.out_sem.at[0])
    input_copy.start()

    for number in range(len(PIECES)):
        take_all(number)

    def ordered(target, source, rows):
        def body(i, carry):
            start = pl.multiple_of(i * 32, 32)
            wst[pl.ds(target + start, 32), :] = k.got_all[pl.ds(source + start, 32), :].astype(F32)
            return carry

        lax.fori_loop(0, rows // 32, body, 0)

    def blank(at):
        wst[at:ROWS, :] = jnp.zeros((ROWS - at, LANES), F32)

    for number in (LAST, THIRD, SECOND):

        @pl.when(stage == PIECES[number][0])
        def unused_ordered(number=number):
            rows = min(padded[number], ROWS // 32 * 32)
            if rows < ROWS:
                blank(rows)
            ordered(0, 0, rows)
            if rows < PIECES[number][1]:
                tail = k.got_all[rows : rows + 16, :].astype(F32)
                wst[rows : rows + 16, :] = tail

    @pl.when(stage == 0)
    def unused_first():
        at = section_at[FIRST_IN]
        blank(MID_BIAS + 1)
        ordered(0, at, CIN)
        gains = k.got_all[at + CIN : at + CIN + 16, :].astype(F32)
        wst[IN_GAIN : IN_BIAS + 1, :] = gains[0:2, :]
        wst[MID_GAIN : MID_BIAS + 1, :] = gains[2:4, :]
        ordered(MID_AT, 0, 9 * MID)

    out_copy = pltpu.make_async_copy(wst.at[pl.ds(0, ROWS)], k.weight_grads_at, k.grad_sem)
    out_copy.start()
    input_copy.wait()
    for copy in weight_copies:
        copy.wait_send()
    for number in range(EXCHANGES):
        wait_for(k.stat_send.at[number], incoming(number, pl.ds(0, batches - 1)))
    for number in range(len(PIECES)):
        end_sends(number)
    out_copy.wait()


def write_kernel(weight_rows, input_rows, weight_out, input_out, held_weights, held, sems):
    count = 10
    part = input_rows.shape[0] // count
    pairs = [
        (weight_rows.at[pl.ds(0, ROW)], held_weights, weight_out.reshape(ROW, LANES)),
        *[
            (input_rows.at[rows], held.at[rows], input_out.at[rows])
            for rows in [pl.ds(i * part, part) for i in range(count)]
        ],
    ]
    arriving = [
        pltpu.make_async_copy(source, middle, sems.at[0, i])
        for i, (source, middle, target) in enumerate(pairs)
    ]
    leaving = [
        pltpu.make_async_copy(middle, target, sems.at[1, i])
        for i, (source, middle, target) in enumerate(pairs)
    ]
    for copy in arriving:
        copy.start()
    for i in range(len(pairs)):
        arriving[i].wait()
        leaving[i].start()
    for copy in leaving:
        copy.wait()


def shards(features, weights, crop_kind, positives, negatives, bank, normalizer):
    phases = lax.axis_size("phase")
    batches = lax.axis_size("batch")
    in_rows = features.shape[0] // MICRO
    out_rows = in_rows // 4
    plane = out_rows + 2 * PAD
    slots = crop_kind.shape[2]
    chunk = out_rows // 5
    part = out_rows // 25
    group = 2 * phases
    levels = line_levels(batches // 2)
    padded = [-(-rows // (16 * group)) * 16 * group for unused, rows in PIECES]
    widest = max(*padded[:3], padded[3] + padded[4])
    eighth = sum(padded) // group
    staged = max(ROWS, *padded[:3])
    any_space = pl.BlockSpec(memory_space=pl.ANY)
    smem = pl.BlockSpec(memory_space=pltpu.SMEM)

    def held(*shape, dtype=F32):
        return pltpu.VMEM(shape, dtype)

    def sems(*shape):
        return pltpu.SemaphoreType.DMA(shape)

    def low(*shape):
        return held(*shape, dtype=BF16)

    kept_slopes = {"slope23": low(out_rows, COUT)} if batches <= 8 else {}

    inputs = {
        "features_at": (features, any_space),
        "weights_at": (weights, any_space),
        "negatives_at": (jnp.transpose(negatives, (0, 2, 1, 3)), any_space),
        "bank_at": (bank, any_space),
        "kinds": (jnp.transpose(crop_kind, (2, 1, 0)), smem),
        "positives": (positives, smem),
        "normalizer": (normalizer, smem),
    }
    outputs = {
        "weight_grads_at": jax.ShapeDtypeStruct((ROWS, LANES), F32),
        "input_grad_at": jax.ShapeDtypeStruct((in_rows, CIN), BF16),
    }
    scratch = {
        "feat": low(in_rows, CIN),
        "t1": held(in_rows, MID),
        "big0": held(4 * plane, MID),
        "big1": held(in_rows, MID),
        "big2": held(4 * plane, MID),
        "cols1": low(out_rows, 9 * MID),
        "cols2": low(out_rows, 9 * MID),
        "colt": low(chunk, 9 * MID),
        "src": held(plane, MID),
        "t2": held(out_rows, MID),
        "t4": held(out_rows, MID),
        "t5": held(out_rows, MID),
        "gn": held(out_rows, MID),
        "h2": low(out_rows, MID),
        "h4": low(out_rows, MID),
        "xs": low(out_rows, CIN),
        "y": low(out_rows, COUT),
        "gw": low(out_rows, COUT),
        "wide2": low(BANK // 4, COUT),
        "dtn": low(out_rows, MID),
        "turn": low(LANES + 16, out_rows),
        "first_t": held(CIN, MID),
        "first_s": held(CIN, MID),
        "masks": low(4, out_rows, LANES),
        "raw": low(1, GRAD_LEN),
        "wts": low(phases, ROWS, LANES),
        "wst": held(staged, LANES),
        "wmid1": low(9 * MID, MID),
        "wmid3": low(9 * MID, MID),
        "wout2": low(MID, COUT),
        "wshort": low(CIN, COUT),
        "wout4": low(MID, COUT),
        "wout2_t": low(COUT, MID),
        "wshort_t": low(COUT, CIN),
        "wout4_t": low(COUT, MID),
        "wmid1_t": low(8 * MID, 2 * MID),
        "wmid3_t": low(9 * MID, MID),
        "win1_t": low(MID, CIN),
        "win3_t": low(MID, COUT),
        "gains": held(32, LANES),
        "small": held(8, LANES),
        "coef": held(56, COUT),
        "spread": held(32, LANES),
        "neg": held(slots, MICRO, NEG, dtype=jnp.int32),
        **kept_slopes,
        "tabv": held(16, TABLE, dtype=jnp.int32),
        "tab": pltpu.SMEM((16, TABLE), jnp.int32),
        "send": held(SPAN_ROWS, LANES),
        "send_narrow": held(EXCHANGES, 2, LANES),
        "recv_narrow": held(EXCHANGES, batches, 2, LANES),
        "recv": held(batches, SPAN_ROWS, LANES),
        "total": held(16, LANES),
        "gb": low(sum(padded), LANES),
        "got_scatter": low(group - 1, eighth, LANES),
        "line_sum": low(len(levels), eighth, LANES),
        "got_line": low(sum(levels) - len(levels), eighth, LANES),
        "home": low(eighth, LANES),
        "got_all": low(widest, LANES),
        "raw_sem": pltpu.SemaphoreType.DMA,
        "feat_sem": sems(4),
        "bank_sem": sems(2),
        "neg_sem": pltpu.SemaphoreType.DMA,
        "tab_sem": pltpu.SemaphoreType.DMA,
        "weight_send": sems(2, phases),
        "weight_recv": sems(2, phases),
        "stat_send": sems(EXCHANGES),
        "stat_recv": sems(EXCHANGES),
        "scatter_send": sems(len(PIECES)),
        "scatter_recv": sems(len(PIECES)),
        "line_send": sems(len(levels), len(PIECES)),
        "line_recv": sems(len(levels), len(PIECES)),
        "home_send": sems(len(PIECES)),
        "home_recv": sems(len(PIECES)),
        "out_sem": sems(4),
        "grad_sem": pltpu.SemaphoreType.DMA,
    }
    names = (*inputs, *outputs, *scratch)
    weight_rows, input_rows = pl.pallas_call(
        functools.partial(kernel, names, batches, phases, in_rows, slots),
        out_shape=tuple(outputs.values()),
        in_specs=[spec for unused, spec in inputs.values()],
        out_specs=(any_space,) * len(outputs),
        scratch_shapes=list(scratch.values()),
        compiler_params=pltpu.CompilerParams(
            collective_id=0, has_side_effects=True, vmem_limit_bytes=64 * 1024 * 1024
        ),
    )(*[value for value, unused in inputs.values()])
    weight_grads, input_grad = pl.pallas_call(
        write_kernel,
        out_shape=(
            jax.ShapeDtypeStruct((1, GRAD_LEN), F32),
            jax.ShapeDtypeStruct((in_rows, CIN), BF16),
        ),
        in_specs=[any_space, any_space],
        out_specs=(any_space, any_space),
        scratch_shapes=[held(ROW, LANES), low(in_rows, CIN), sems(2, 11)],
        compiler_params=pltpu.CompilerParams(vmem_limit_bytes=64 * 1024 * 1024),
    )(weight_rows, input_rows)
    return (weight_grads, input_grad)


def solution(mesh):
    placed = (
        P("batch", None),
        P("phase", None),
        P(),
        P("batch", None, None),
        P("batch", None, None, None),
        P(),
        P(),
    )
    return jax.shard_map(
        shards,
        mesh=mesh,
        in_specs=placed,
        out_specs=(P("phase", None), P(("batch", "phase"), None)),
        check_vma=False,
    )
```

```python
import functools
import math
import types

import jax
import jax.numpy as jnp
from jax import lax
from jax.experimental import pallas as pl
from jax.experimental.pallas import tpu as pltpu
from jax.sharding import PartitionSpec as P

CIN = 256
MID = 128
COUT = 512
EMB = 128
SIDE_UNIT = 4
MICRO = 4
NEG = 4096
BANK = 16384
GRAD_LEN = 213504
LANES = 128
SOFTMAX_TEMPER = 0.07
EPSILON = 1e-05

PAD = 48
ROW = GRAD_LEN // LANES
ROWS = -(-ROW // 16) * 16
BLOCK = 16
TABLE = 512
UNROLL = 5
EARLY = 272
AHEAD = 80
MESH = pl.DeviceIdType.MESH
F32 = jnp.float32
BF16 = jnp.bfloat16

IN_GAIN, IN_BIAS, MID_AT = CIN, CIN + 1, CIN + 2
MID_GAIN, MID_BIAS = MID_AT + 9 * MID, MID_AT + 9 * MID + 1
THIRD_GAIN, THIRD_BIAS, THIRD_MID = COUT, COUT + 1, COUT + 2
THIRD_MID_GAIN, THIRD_MID_BIAS = THIRD_MID + 9 * MID, THIRD_MID + 9 * MID + 1
OUT_GAIN, OUT_BIAS, AFTER_OUT = 512, 516, 520
SHORT_GAIN, SHORT_BIAS = AFTER_OUT + 1024, AFTER_OUT + 1028

EXCHANGES = 12
SPANS = {2: 16, 5: 8, 6: 8, 9: 16}
STARTS = {2: 0, 5: 16, 6: 24, 9: 32}
SPAN_ROWS = 48

PIECES = ((3, 1032), (2, 1668), (1, 1552), (0, 9 * MID), (0, 260))
LAST, THIRD, SECOND, FIRST_MID, FIRST_IN = range(5)

L1, L2, L3, LS, L4, L5, L6 = range(7)
HALF_SCALE, HALF_SHIFT, INVERSE, NEG_MEAN, GRAD_A, GRAD_E, GRAD_D = range(7)


def dense(left, right):
    return jnp.dot(left, right, preferred_element_type=F32)


def across(left, right):
    return lax.dot_general(left, right, (((1,), (1,)), ((), ())), preferred_element_type=F32)


def outer(left, right):
    return lax.dot_general(left, right, (((0,), (0,)), ((), ())), preferred_element_type=F32)


def folded(values):
    rows, width = values.shape
    return values.reshape(rows // 8, 8, width).sum(axis=0)


def silu_half(half):
    return half + half * jnp.tanh(half)


def slope_half(half):
    bend = jnp.tanh(half)
    return 0.5 * (1.0 + bend + half * (1.0 - bend * bend))


def split(values):
    high = values.astype(BF16)
    return high, (values - high.astype(F32)).astype(BF16)


def line_levels(lines):
    return [lines] if lines <= 8 else [lines // 8, 8]


def kernel(names, batches, phases, in_rows, slots, *refs):
    k = types.SimpleNamespace(**dict(zip(names, refs, strict=True)))
    out_rows = in_rows // 4
    plane = out_rows + 2 * PAD
    chunk = out_rows // 5
    part = out_rows // 25
    blocks = out_rows // BLOCK
    per = part // BLOCK
    me = lax.axis_index("batch")
    stage = lax.axis_index("phase")
    core = lax.rem(me, 2)
    line = lax.div(me, 2)
    lines = batches // 2
    group = 2 * phases
    mine = 2 * stage + core
    levels = line_levels(lines)
    half_bank = BANK // 2
    quarter = in_rows // 4
    feat, t1, big0, big1, big2, src = k.feat, k.t1, k.big0, k.big1, k.big2, k.src
    tab, masks, wst, wts, gw, wide2, gn = k.tab, k.masks, k.wst, k.wts, k.gw, k.wide2, k.gn

    def batch_peer(i):
        return {"batch": lax.rem(me + i, batches)}

    def phase_peer(i):
        return {"phase": lax.rem(stage + i, phases)}

    def remote(source, target, send_sem, recv_sem, device):
        return pltpu.make_async_remote_copy(
            src_ref=source,
            dst_ref=target,
            send_sem=send_sem,
            recv_sem=recv_sem,
            device_id=device,
            device_id_type=MESH,
        )

    def wait_for(sem, region):
        pltpu.make_async_copy(region, region, sem).wait()

    barrier = pltpu.get_barrier_semaphore()

    def greet(i, carry):
        pl.semaphore_signal(barrier, inc=1, device_id=batch_peer(i), device_id_type=MESH)
        return carry

    lax.fori_loop(1, batches, greet, 0)
    for i in range(1, phases):
        for other in (me, 2 * line + 1 - core):
            pl.semaphore_signal(
                barrier,
                inc=1,
                device_id={"phase": lax.rem(stage + i, phases), "batch": other},
                device_id_type=MESH,
            )

    raw_copy = pltpu.make_async_copy(k.weights_at, k.raw, k.raw_sem)
    raw_copy.start()
    feat_copies = []
    for i in range(4):
        copy = pltpu.make_async_copy(
            k.features_at.at[pl.ds(pl.multiple_of(stage * in_rows + i * quarter, 16), quarter)],
            feat.at[pl.ds(i * quarter, quarter)],
            k.feat_sem.at[i],
        )
        copy.start()
        feat_copies.append(copy)
    neg_copy = pltpu.make_async_copy(k.negatives_at.at[0], k.neg, k.neg_sem)
    neg_copy.start()
    bank_copies = [
        pltpu.make_async_copy(
            k.bank_at.at[pl.ds(i * half_bank, half_bank)],
            big0.at[pl.ds(0, half_bank)],
            k.bank_sem.at[i],
        )
        for i in range(2)
    ]

    def side_of(kind):
        return SIDE_UNIT * jnp.where(
            kind == 1, 5, jnp.where(kind == 2, 7, jnp.where(kind == 3, 9, 0))
        )

    sides = [side_of(k.kinds[slot, stage, me]) for slot in range(slots)]
    ends = []
    for side in sides:
        ends.append(side * side + (ends[-1] if ends else 0))
    starts = [0, *ends[:-1]]
    rows_live = ends[-1]

    def all_areas(i, carry):
        for slot in range(slots):
            side = side_of(k.kinds[slot, stage, i])
            carry = carry + side * side
        return carry

    live_pixels = lax.fori_loop(0, batches, all_areas, 0)
    inverse_count = 1.0 / jnp.full((1, LANES), live_pixels, jnp.int32).astype(F32)[:, 0:1]

    def place(first):
        base = jnp.zeros_like(first)
        width = jnp.zeros_like(first)
        slot = jnp.full_like(first, 7)
        for number in range(slots):
            inside = (first >= starts[number]) & (first < ends[number])
            base = jnp.where(inside, starts[number], base)
            width = jnp.where(inside, sides[number], width)
            slot = jnp.where(inside, number, slot)
        return base, width, slot

    def divided(value, side):
        factor = jnp.zeros_like(side)
        for kind in (5, 7, 9):
            factor = jnp.where(side == SIDE_UNIT * kind, 65536 // (SIDE_UNIT * kind) + 1, factor)
        return lax.shift_right_logical(value * factor, jnp.full_like(value, 16))

    index = lax.broadcasted_iota(jnp.int32, (1, TABLE), 1)
    first = BLOCK * index
    base, width, slot = place(first)
    live = width > 0
    local = jnp.where(live, first - base, 0)
    row = divided(local, width)
    left = jnp.where(live, (row + 1) * width - local, BLOCK)
    begin = jnp.where(live, 4 * base + 2 * (local + row * width), 4 * first)
    jump = jnp.where(left < BLOCK, 2 * width, 0)
    window_at = lax.shift_right_logical(
        index * (65536 // per + 1), jnp.full_like(index, 16)
    ) * (4 * part) - AHEAD
    in_window = begin - jnp.maximum(window_at, 0)
    pixel = BLOCK // 4 * index
    in_base, in_width, unused_slot = place(pixel)
    in_live = in_width > 0
    in_side = jnp.maximum(in_width, 1)
    in_local = 4 * (pixel - in_base)
    in_row = divided(2 * (pixel - in_base), in_width)
    in_left = jnp.where(in_live, (2 * in_side - (in_local - in_row * 2 * in_side)) >> 1, 8)
    upper = in_row >> 1
    odd = in_row - 2 * upper
    lower = (in_row + 1) >> 1
    here = in_base + upper * in_side + (in_side - in_left)
    below = in_base + lower * in_side - in_left
    at_here = jnp.where(in_live, PAD + here + odd * (2 * plane), PAD + out_rows - BLOCK)
    at_below = jnp.where(in_left < 8, PAD + below + (1 - odd) * (2 * plane), at_here)
    even_here = jnp.where(in_live & (odd == 0), PAD + here, 0)
    even_below = jnp.where(in_live & (in_left < 8) & (odd == 1), PAD + below, 0)
    columns = (width, local, begin, left, jump, slot, 2 * width)
    columns = columns + (at_here, at_below, in_left, even_here, even_below, in_window)
    k.tabv[...] = jnp.zeros(k.tabv.shape, jnp.int32)
    for number, column in enumerate(columns):
        k.tabv[number : number + 1, :] = column
    tab_copy = pltpu.make_async_copy(k.tabv, tab, k.tab_sem)
    tab_copy.start()

    raw_copy.wait()

    def to_rows(first, last):
        def body(i, carry):
            found = []
            for u in range(16):
                at = pl.multiple_of((i * 16 + u) * LANES, LANES)
                found.append(k.raw[0:1, pl.ds(at, LANES)].astype(F32))
            for u, values in enumerate(found):
                wst[pl.ds(i * 16 + u, 1), :] = values
            return carry

        lax.fori_loop(first // 16, last // 16, body, 0)
        done = last // 16 * 16
        for at in range(done, last):
            wst[at : at + 1, :] = k.raw[0:1, at * LANES : (at + 1) * LANES].astype(F32)
        if done < last:
            wst[last : done + 16, :] = jnp.zeros((done + 16 - last, LANES), F32)

        def convert(i, carry):
            rows = pl.ds(pl.multiple_of(i * 16, 16), 16)
            wts[stage, rows, :] = wst[rows, :].astype(BF16)
            return carry

        lax.fori_loop(first // 16, -(-last // 16), convert, 0, unroll=2)

    weight_spans = ((0, EARLY), (EARLY, ROWS - EARLY))

    def send_weights(number):
        at, rows = weight_spans[number]
        region = wts.at[stage, pl.ds(at, rows)]
        copies = []
        for i in range(1, phases):
            copy = remote(
                region,
                region,
                k.weight_send.at[number, i],
                k.weight_recv.at[number, stage],
                phase_peer(i),
            )
            copy.start()
            copies.append(copy)
        return copies

    def need_weights(number, section):
        at, rows = weight_spans[number]

        @pl.when(stage != section)
        def unused_wait():
            wait_for(k.weight_recv.at[number, section], wts.at[section, pl.ds(at, rows)])

    to_rows(0, EARLY)
    pl.semaphore_wait(barrier, batches - 1 + 2 * (phases - 1))
    weight_copies = send_weights(0)

    def outgoing(number):
        if number in SPANS:
            return k.send.at[pl.ds(STARTS[number], SPANS[number])]
        return k.send_narrow.at[number]

    def incoming(number, which):
        if number in SPANS:
            return k.recv.at[which, pl.ds(STARTS[number], SPANS[number])]
        return k.recv_narrow.at[number, which]

    def share(number):
        def give(i, carry):
            remote(
                outgoing(number),
                incoming(number, me),
                k.stat_send.at[number],
                k.stat_recv.at[number],
                {"batch": lax.rem(batches - 1 - me + i, batches)},
            ).start()
            return carry

        mirrored = lax.rem(2 * me + 1, batches)

        def skip(i, carry):
            return give(i + jnp.where(i >= mirrored, 1, 0), carry)

        lax.fori_loop(0, batches - 1, skip, 0, unroll=batches <= 8)
        incoming(number, me)[...] = outgoing(number)[...]

    def collect(number):
        wait_for(k.stat_recv.at[number], incoming(number, pl.ds(0, batches - 1)))

        def add(i, carry):
            return carry + incoming(number, i)[...]

        rows = SPANS.get(number, 2)
        k.total[pl.ds(0, rows), :] = lax.fori_loop(
            1, batches, add, incoming(number, 0)[...], unroll=batches <= 8
        )

    padded = [-(-rows // (16 * group)) * 16 * group for unused, rows in PIECES]
    piece_at = [sum(padded[:i]) for i in range(len(padded))]
    section_at = [0, 0, 0, 0, padded[FIRST_MID]]
    part_of = [rows // group for rows in padded]

    def summed(rows, target, *sources):
        total = sources[0](0, rows).astype(F32)
        for source in sources[1:]:
            total = total + source(0, rows).astype(F32)
        target(0, rows, total.astype(BF16))

    def reader(ref, start):
        return lambda at, step: ref[pl.ds(pl.multiple_of(start + at, 16), step), :]

    def writer(ref, start):
        def write(at, step, values):
            ref[pl.ds(pl.multiple_of(start + at, 16), step), :] = values

        return write

    def give_scatter(number):
        rows, at = part_of[number], piece_at[number]

        def give(i, carry):
            other = lax.rem(mine + i, group)
            remote(
                k.gb.at[pl.ds(at + other * rows, rows)],
                k.got_scatter.at[i - 1, pl.ds(at // group, rows)],
                k.scatter_send.at[number],
                k.scatter_recv.at[number],
                {"phase": lax.div(other, 2), "batch": 2 * line + lax.rem(other, 2)},
            ).start()
            return carry

        lax.fori_loop(1, group, give, 0)

    def give_line(number):
        rows, at = part_of[number], piece_at[number]
        within = at // group
        wait_for(k.scatter_recv.at[number], k.got_scatter.at[:, pl.ds(within, rows)])

        def other(i):
            return lambda start, step: k.got_scatter[i, pl.ds(within + start, step), :]

        summed(
            rows,
            writer(k.line_sum.at[0], within),
            reader(k.gb, at + mine * rows),
            *[other(i) for i in range(group - 1)],
        )
        send_level(number, 0)

    def level_of(level):
        size, stride = levels[level], math.prod(levels[:level])
        return size, stride, sum(levels[:level]) - level, lax.rem(lax.div(line, stride), size)

    def send_level(number, level):
        size, stride, slot, digit = level_of(level)
        rows, within = part_of[number], piece_at[number] // group

        def give(i, carry):
            other = line + (lax.rem(digit + i, size) - digit) * stride
            remote(
                k.line_sum.at[level, pl.ds(within, rows)],
                k.got_line.at[slot + i - 1, pl.ds(within, rows)],
                k.line_send.at[level, number],
                k.line_recv.at[level, number],
                {"batch": 2 * other + core},
            ).start()
            return carry

        lax.fori_loop(1, size, give, 0)

    def add_level(number, level, target):
        size, stride, slot, digit = level_of(level)
        rows, within = part_of[number], piece_at[number] // group
        arrived = k.got_line.at[pl.ds(slot, size - 1), pl.ds(within, rows)]
        wait_for(k.line_recv.at[level, number], arrived)

        own = k.line_sum[level, pl.ds(within, rows), :].astype(F32)
        total = jnp.zeros((rows, LANES), F32)
        for which in range(size):
            at = jnp.minimum(lax.rem(digit - which - 1 + size, size), size - 2)
            found = k.got_line[slot + at, pl.ds(within, rows), :].astype(F32)
            total = total + jnp.where(which == digit, own, found)
        target[pl.ds(within, rows), :] = total.astype(BF16)

    def give_home(number):
        section = PIECES[number][0]
        rows, at = part_of[number], piece_at[number]
        within = at // group
        for level in range(len(levels) - 1):
            add_level(number, level, k.line_sum.at[level + 1])
            send_level(number, level + 1)
        add_level(number, len(levels) - 1, k.home)
        target = k.got_all.at[pl.ds(section_at[number] + mine * rows, rows)]

        def give(other):
            remote(
                k.home.at[pl.ds(within, rows)],
                target,
                k.home_send.at[number],
                k.home_recv.at[number],
                {"phase": section, "batch": 2 * line + other},
            ).start()

        @pl.when(stage != section)
        def unused_both():
            give(0)
            give(1)

        @pl.when(stage == section)
        def unused_one():
            give(1 - core)
            target[...] = k.home[pl.ds(within, rows), :]

    def take_all(number):
        rows, within = part_of[number], section_at[number]

        @pl.when(stage == PIECES[number][0])
        def unused_take():
            wait_for(k.home_recv.at[number], k.got_all.at[pl.ds(within, (group - 1) * rows)])

    def end_sends(number):
        rows, at = part_of[number], piece_at[number]
        within = at // group
        wait_for(k.scatter_send.at[number], k.got_scatter.at[:, pl.ds(within, rows)])
        for level in range(len(levels)):
            size, unused_stride, slot, unused_digit = level_of(level)
            sent = k.got_line.at[pl.ds(slot, size - 1), pl.ds(within, rows)]
            wait_for(k.line_send.at[level, number], sent)

        @pl.when(stage != PIECES[number][0])
        def unused_away():
            wait_for(k.home_send.at[number], k.got_all.at[pl.ds(0, 2 * rows)])

        @pl.when(stage == PIECES[number][0])
        def unused_home():
            wait_for(k.home_send.at[number], k.got_all.at[pl.ds(0, rows)])

    def stage_piece(number):
        rows, used, at = padded[number], PIECES[number][1], piece_at[number]
        if used < rows:
            wst[used:rows, :] = jnp.zeros((rows - used, LANES), F32)

        def convert(i, carry):
            start = pl.multiple_of(i * 64, 64)
            k.gb[pl.ds(at + start, 64), :] = wst[pl.ds(start, 64), :].astype(BF16)
            return carry

        lax.fori_loop(0, rows // 64, convert, 0, unroll=2)
        give_scatter(number)

    def put_narrow(number, row, vector):
        k.send_narrow[number, row : row + 1, :] = vector

    def put_wide(number, row, vectors):
        for j, vector in enumerate(vectors):
            at = STARTS[number] + 4 * row + j
            k.send[at : at + 1, :] = vector

    def put_small(row, vector):
        k.small[row : row + 1, :] = vector

    def narrow(row):
        return k.total[row : row + 1, :]

    def wide(row):
        return jnp.concatenate([k.total[4 * row + j : 4 * row + j + 1, :] for j in range(4)], axis=1)

    def reduced(values):
        return jnp.sum(values, axis=0, keepdims=True)

    def gain_narrow(row):
        return k.gains[row : row + 1, :]

    def gain_wide(row):
        return jnp.concatenate([k.gains[row + j : row + j + 1, :] for j in range(4)], axis=1)

    def put_coef(layer, what, vector):
        row = 8 * layer + what
        k.coef[row : row + 1, 0 : vector.shape[1]] = vector

    def lanes(j):
        return slice(j * LANES, (j + 1) * LANES)

    def get_coef(layer, what, j=0):
        row = 8 * layer + what
        return k.coef[row : row + 1, lanes(j)]

    def finish(layer, sums, squares, gain, bias, count_inverse):
        mean = sums * count_inverse
        inverse = lax.rsqrt(squares * count_inverse - mean * mean + EPSILON)
        scale = inverse * gain
        put_coef(layer, INVERSE, inverse)
        put_coef(layer, NEG_MEAN, -mean * inverse)
        put_coef(layer, HALF_SCALE, 0.5 * scale)
        put_coef(layer, HALF_SHIFT, 0.5 * (bias - mean * scale))

    def normed_sum(layer, sums, products, j=0):
        return products * get_coef(layer, INVERSE, j) + sums * get_coef(layer, NEG_MEAN, j)

    def finish_back(layer, sums, dots, gain, count_inverse):
        width = sums.shape[1]
        row = 8 * layer
        inverse = k.coef[row + INVERSE : row + INVERSE + 1, 0:width]
        scale = inverse * gain
        slant = scale * dots * count_inverse
        put_coef(layer, GRAD_A, scale)
        put_coef(layer, GRAD_E, slant * inverse)
        put_coef(
            layer,
            GRAD_D,
            scale * sums * count_inverse
            + slant * k.coef[row + NEG_MEAN : row + NEG_MEAN + 1, 0:width],
        )

    def put_late(stores):
        for ref, at, value in stores:
            ref[at] = value

    def each_part(body, carry=0, parts=1):
        def step(i, inner):
            stores = []
            for u in range(parts):
                inner, found = body(pl.multiple_of((i * parts + u) * part, 16), inner)
                stores = stores + found
            put_late(stores)
            return inner

        return lax.fori_loop(0, 25 // parts, step, carry, unroll=UNROLL if parts == 1 else 1)

    def each_chunk(body, carry=0):
        def step(i, inner):
            return body(pl.multiple_of(i * chunk, 16), inner)

        return lax.fori_loop(0, 5, step, carry, unroll=UNROLL)

    def each_block(body):
        def step(i, carry):
            stores = []
            for u in range(per):
                number = i * per + u
                stores = stores + body(number, pl.multiple_of(number * BLOCK, 16))
            put_late(stores)
            return carry

        lax.fori_loop(0, blocks // per, step, 0, unroll=UNROLL)

    def zeros(width=MID):
        return jnp.zeros((8, width), F32)

    def live_rows(start, rows):
        return lax.broadcasted_iota(jnp.int32, (rows, LANES), 0) + start < rows_live

    def near_rows(rows, number):
        return lax.broadcasted_iota(jnp.int32, (rows, LANES), 0) < number

    def live_block(width):
        return jnp.broadcast_to(jnp.where(width > 0, 1.0, 0.0), (BLOCK, LANES)).astype(BF16)

    def at_block(buffer, j, start, rows):
        return buffer[pl.ds(j * out_rows + start, rows), :]

    def wide_store(buffer, start, values):
        rows = values.shape[0]
        for j in range(4):
            buffer[pl.ds(j * out_rows + start, rows), :] = values[:, lanes(j)]

    def added(carry, values):
        return carry[0] + folded(values), carry[1] + folded(values * values)

    def product_sums(left, right, store, masked=False):
        width = right.shape[1]

        def body(start, carry):
            values = dense(left[pl.ds(start, chunk), :], right[...])
            store(start, values)
            if masked:
                values = jnp.where(live_rows(start, chunk), values, 0.0)
            return added(carry, values)

        return each_chunk(body, (zeros(width), zeros(width)))

    def store_narrow(target):
        def store(start, values):
            target[pl.ds(start, values.shape[0]), :] = values

        return store

    def send_narrow(number, sums):
        put_narrow(number, 0, reduced(sums[0]))
        put_narrow(number, 1, reduced(sums[1]))
        share(number)

    def by_lanes(vector):
        return [vector[:, lanes(j)] for j in range(4)]

    def stage_section(section):
        def step(i, carry):
            start = pl.multiple_of(i * (ROWS // 7), 16)
            wst[pl.ds(start, ROWS // 7), :] = wts[section, pl.ds(start, ROWS // 7), :].astype(F32)
            return carry

        lax.fori_loop(0, 7, step, 0)

    def unpack_wide(at, rows, target):
        for j in range(4):
            for r in range(rows // LANES):
                piece = wst[pl.ds(at + 4 * LANES * r + j, LANES, stride=4), :]
                target[r * LANES : (r + 1) * LANES, lanes(j)] = piece.astype(BF16)

    def take_gain(row, at, rows=1):
        k.gains[row : row + rows, :] = wst[at : at + rows, :]

    def turned(piece):
        return piece.astype(BF16).T

    to_rows(EARLY, ROW)
    weight_copies = weight_copies + send_weights(1)
    for copy in feat_copies:
        copy.wait()

    need_weights(0, 0)
    def open_first(step, carry):
        start = pl.multiple_of(step * chunk, 16)
        values = dense(feat[pl.ds(start, chunk), :], wts[0, 0:CIN, :])
        t1[pl.ds(start, chunk), :] = values
        rows = lax.broadcasted_iota(jnp.int32, values.shape, 0) + start
        return added(carry, jnp.where(rows < 4 * rows_live, values, 0.0))

    sums = lax.fori_loop(0, in_rows // chunk, open_first, (zeros(), zeros()), unroll=UNROLL)
    send_narrow(0, sums)

    tab_copy.wait()
    src[0:PAD, :] = jnp.zeros((PAD, LANES), F32)
    src[PAD + out_rows : plane, :] = jnp.zeros((PAD, LANES), F32)
    for number in range(4):
        big0[number * plane : number * plane + PAD, :] = jnp.zeros((PAD, LANES), F32)

    def make_masks(number, start):
        width, local = tab[0, number], tab[1, number]
        pixel = lax.broadcasted_iota(jnp.int32, (BLOCK, LANES), 0).astype(F32) + local.astype(F32)
        side = jnp.maximum(width, 1).astype(F32)
        row = jnp.floor((pixel + 0.5) / side)
        column = pixel - row * side
        one = jnp.where(width > 0, 1.0, 0.0)
        found = (row > 0.5, row < side - 1.5, column > 0.5, column < side - 1.5)
        return [
            (
                masks,
                (which, pl.ds(start, BLOCK), slice(None)),
                jnp.where(condition, one, 0.0).astype(BF16),
            )
            for which, condition in enumerate(found)
        ]

    each_block(make_masks)
    window_rows = AHEAD + 4 * part

    def shortcut_pixels(i, carry):
        for piece in range(5):
            step = i * 5 + piece
            at = (piece % 2) * 2 * window_rows
            low = pl.multiple_of(jnp.maximum(step * 4 * part - AHEAD, 0), 16)
            for half in range(2):
                gn[at + half * window_rows : at + (half + 1) * window_rows, :] = feat[
                    pl.ds(low, window_rows), lanes(half)
                ].astype(F32)
            stores = []
            for u in range(per):
                number = step * per + u
                start = pl.multiple_of(number * BLOCK, 16)
                first = tab[12, number]
                second = first + tab[4, number]
                near = near_rows(BLOCK, tab[3, number])
                one = jnp.where(tab[0, number] > 0, 1.0, 0.0)
                for half in range(2):
                    base = at + half * window_rows
                    picked = jnp.where(
                        near,
                        gn[pl.ds(base + first, BLOCK, stride=2), :],
                        gn[pl.ds(base + second, BLOCK, stride=2), :],
                    )
                    stores.append(
                        (k.xs, (pl.ds(start, BLOCK), lanes(half)), (picked * one).astype(BF16))
                    )
            put_late(stores)
        return carry

    lax.fori_loop(0, 5, shortcut_pixels, 0)

    need_weights(1, 0)
    stage_section(0)
    take_gain(0, IN_GAIN, 2)
    take_gain(2, MID_GAIN, 2)
    k.wmid1[...] = wst[MID_AT : MID_AT + 9 * MID, :].astype(BF16)

    def first_products(block):
        rows = slice(block * out_rows, (block + 1) * out_rows)
        live = (
            lax.broadcasted_iota(jnp.int32, (out_rows, MID), 0) + block * out_rows < 4 * rows_live
        )
        k.turn[0:LANES, :] = turned(jnp.where(live, t1[rows, :], 0.0))
        live = lax.broadcasted_iota(jnp.int32, (16, out_rows), 1) + block * out_rows < 4 * rows_live
        k.turn[LANES : LANES + 16, :] = jnp.where(live, 1.0, 0.0).astype(BF16)
        found = dense(k.turn[...], feat[rows, :])
        for half in range(2):
            at = slice(half * LANES, (half + 1) * LANES)
            product = found[0:LANES, lanes(half)].T
            total = jnp.broadcast_to(found[LANES : LANES + 1, lanes(half)], (LANES, LANES)).T
            k.first_t[at, :] = product if block == 0 else k.first_t[at, :] + product
            k.first_s[at, :] = total if block == 0 else k.first_s[at, :] + total

    collect(0)
    finish(L1, narrow(0), narrow(1), gain_narrow(0), gain_narrow(1), 0.25 * inverse_count)

    def first_hidden(number, start):
        scale, shift = get_coef(L1, HALF_SCALE), get_coef(L1, HALF_SHIFT)
        near = near_rows(BLOCK, tab[3, number])
        stores = []
        for row in range(2):
            for column in range(2):
                first = tab[2, number] + column + (tab[6, number] if row else 0)
                values = jnp.where(
                    near,
                    t1[pl.ds(first, BLOCK, stride=2), :],
                    t1[pl.ds(first + tab[4, number], BLOCK, stride=2), :],
                )
                at = pl.ds((2 * row + column) * plane + PAD + start, BLOCK)
                stores.append((big0, (at, slice(None)), silu_half(values * scale + shift)))
        return stores

    each_block(first_hidden)

    def wide_columns(number, start):
        width = tab[0, number]
        here = pl.ds(start, BLOCK)
        top, left, live = masks[0, here, :], masks[2, here, :], live_block(width)
        corner = top * left
        stores = []
        for tap in range(9):
            i, j = tap // 3, tap % 3
            at = (2 * (0 if i == 1 else 1) + (0 if j == 1 else 1)) * plane + PAD + start
            at = at - (width if i == 0 else 0) - (1 if j == 0 else 0)
            mask = (corner if j == 0 else top) if i == 0 else (left if j == 0 else live)
            values = big0[pl.ds(at, BLOCK), :].astype(BF16) * mask
            stores.append((k.cols1, (here, lanes(tap)), values))
        return stores

    each_block(wide_columns)
    send_narrow(1, product_sums(k.cols1, k.wmid1, store_narrow(k.t2)))

    bank_copies[0].start()
    need_weights(0, 1)
    need_weights(1, 1)
    stage_section(1)
    take_gain(8, OUT_GAIN, 8)
    take_gain(16, SHORT_GAIN, 8)
    unpack_wide(0, MID, k.wout2)
    unpack_wide(AFTER_OUT, CIN, k.wshort)
    short_sums = product_sums(k.xs, k.wshort, functools.partial(wide_store, big2))
    put_wide(2, 2, by_lanes(reduced(short_sums[0])))
    put_wide(2, 3, by_lanes(reduced(short_sums[1])))

    def close_narrow(layer, source, target):
        def body(start, carry):
            half = source[pl.ds(start, part), :] * get_coef(layer, HALF_SCALE) + get_coef(
                layer, HALF_SHIFT
            )
            values = jnp.where(live_rows(start, part), silu_half(half), 0.0).astype(BF16)
            return carry, [(target, (pl.ds(start, part), slice(None)), values)]

        each_part(body, parts=5)

    first_products(0)
    collect(1)
    finish(L2, narrow(0), narrow(1), gain_narrow(2), gain_narrow(3), inverse_count)
    close_narrow(L2, k.t2, k.h2)

    roomy = hasattr(k, "slope23")

    def worked_slope(layer, values):
        return slope_half(values * get_coef(layer, HALF_SCALE) + get_coef(layer, HALF_SHIFT))

    def keep_narrow_slope(layer, source, target):
        def body(start, carry):
            here = pl.ds(start, part)
            values = worked_slope(layer, source[here, :]).astype(BF16)
            return carry, [(target, (here, slice(None)), values)]

        each_part(body, parts=5)

    def second_slope(j, start):
        if roomy:
            return k.slope23[pl.ds(start, part), lanes(j)].astype(F32)
        return slope_half(second_half(j, start))

    def keep_second_slope():
        def body(start, carry):
            return carry, [
                (
                    k.slope23,
                    (pl.ds(start, part), lanes(j)),
                    slope_half(second_half(j, start)).astype(BF16),
                )
                for j in range(4)
            ]

        if roomy:
            each_part(body)

    def keep_first_slope():
        def body(start, carry):
            return carry, [
                (
                    k.cols2,
                    (pl.ds(start, part), lanes(block)),
                    worked_slope(L1, t1[pl.ds(block * out_rows + start, part), :]).astype(BF16),
                )
                for block in range(4)
            ]

        each_part(body)

    sums = product_sums(k.h2, k.wout2, functools.partial(wide_store, big1))
    put_wide(2, 0, by_lanes(reduced(sums[0])))
    put_wide(2, 1, by_lanes(reduced(sums[1])))
    share(2)

    def bank_to_bf16(half):
        bank_copies[half].wait()

        def body(i, carry):
            start = pl.multiple_of(i * 128, 128)
            for j in range(2):
                wide2[pl.ds(start, 128), lanes(2 * half + j)] = big0[
                    pl.ds(j * (BANK // 4) + start, 128), :
                ].astype(BF16)
            return carry

        lax.fori_loop(0, BANK // 4 // 128, body, 0, unroll=4)

    need_weights(0, 2)
    need_weights(1, 2)
    stage_section(2)
    take_gain(4, THIRD_GAIN, 2)
    take_gain(6, THIRD_MID_GAIN, 2)
    k.wmid3[...] = wst[THIRD_MID : THIRD_MID + 9 * MID, :].astype(BF16)
    bank_to_bf16(0)
    bank_copies[1].start()
    first_products(1)
    collect(2)
    finish(L3, wide(0), wide(1), gain_wide(8), gain_wide(12), inverse_count)
    finish(LS, wide(2), wide(3), gain_wide(16), gain_wide(20), inverse_count)

    def second_half(j, start):
        return (
            at_block(big1, j, start, part) * get_coef(L3, HALF_SCALE, j)
            + at_block(big2, j, start, part) * get_coef(LS, HALF_SCALE, j)
            + (get_coef(L3, HALF_SHIFT, j) + get_coef(LS, HALF_SHIFT, j))
        )

    def close_second(start, carry):
        stores = []
        for j in range(4):
            values = silu_half(second_half(j, start)).astype(BF16)
            stores.append((k.y, (pl.ds(start, part), lanes(j)), values))
        return carry, stores

    each_part(close_second)

    send_narrow(3, product_sums(k.y, wts.at[2, pl.ds(0, COUT)], store_narrow(k.t4), True))
    need_weights(0, 3)
    need_weights(1, 3)
    stage_section(3)
    take_gain(24, OUT_GAIN, 8)
    unpack_wide(0, MID, k.wout4)
    bank_to_bf16(1)
    keep_second_slope()
    collect(3)
    finish(L4, narrow(0), narrow(1), gain_narrow(4), gain_narrow(5), inverse_count)

    def third_hidden(start, carry):
        half = k.t4[pl.ds(start, part), :] * get_coef(L4, HALF_SCALE) + get_coef(L4, HALF_SHIFT)
        return carry, [(src, (pl.ds(PAD + start, part), slice(None)), silu_half(half))]

    each_part(third_hidden, parts=5)

    def near_columns(number, start, target, target_start):
        width = tab[0, number]
        here = pl.ds(start, BLOCK)
        top, bottom, left, right = (masks[which, here, :] for which in range(4))
        live = live_block(width)
        stores = []
        for tap in range(9):
            i, j = tap // 3, tap % 3
            at = PAD + start + (i - 1) * width + (j - 1)
            mask = (top, live, bottom)[i]
            if j != 1:
                beside = left if j == 0 else right
                mask = beside if i == 1 else mask * beside
            values = src[pl.ds(at, BLOCK), :].astype(BF16) * mask
            stores.append((target, (pl.ds(target_start, BLOCK), lanes(tap)), values))
        return stores

    each_block(lambda number, start: near_columns(number, start, k.cols2, start))
    send_narrow(4, product_sums(k.cols2, k.wmid3, store_narrow(k.t5)))

    neg_copy.wait()
    gn[0 : 8 * LANES, :] = jnp.zeros((8 * LANES, LANES), F32)
    neg_piece = 512
    for slot in range(slots):

        def count(i, carry, slot=slot):
            at = pl.multiple_of(i * neg_piece, neg_piece)
            found = k.neg[slot, pl.ds(stage, 1), pl.ds(at, neg_piece)]
            spot = lax.broadcasted_iota(jnp.int32, (LANES, neg_piece), 0)
            upper = lax.shift_right_logical(found, 7)
            high = jnp.where(spot == upper, 1.0, 0.0).astype(BF16)
            low = jnp.where(spot == found - LANES * upper, 1.0, 0.0).astype(BF16)
            return carry + across(high, low)

        found = lax.fori_loop(
            0, NEG // neg_piece, count, jnp.zeros((LANES, LANES), F32), unroll=True
        )
        gn[pl.ds(slot, LANES, stride=8), :] = found
    first_products(2)
    collect(4)
    finish(L5, narrow(0), narrow(1), gain_narrow(6), gain_narrow(7), inverse_count)
    close_narrow(L5, k.t5, k.h4)

    sums = product_sums(k.h4, k.wout4, functools.partial(wide_store, big0))
    put_wide(5, 0, by_lanes(reduced(sums[0])))
    put_wide(5, 1, by_lanes(reduced(sums[1])))
    share(5)
    for j in range(4):
        k.wout4_t[j * LANES : (j + 1) * LANES, :] = turned(k.wout4[:, lanes(j)])
    for tap in range(9):
        k.wmid3_t[(8 - tap) * MID : (9 - tap) * MID, :] = turned(
            k.wmid3[tap * MID : (tap + 1) * MID, :]
        )
    for r in range(4):
        k.win3_t[:, lanes(r)] = turned(wts[2, r * LANES : (r + 1) * LANES, :])
    keep_narrow_slope(L5, k.t5, k.dtn)
    first_products(3)
    collect(5)
    finish(L6, wide(0), wide(1), gain_wide(24), gain_wide(28), inverse_count)

    def last_half(j, start):
        return (
            at_block(big0, j, start, part) * get_coef(L6, HALF_SCALE, j)
            + get_coef(L6, HALF_SHIFT, j)
            + 0.5 * k.y[pl.ds(start, part), lanes(j)].astype(F32)
        )

    def close_last(start, carry):
        return carry, [
            (gw, (pl.ds(start, part), lanes(j)), silu_half(last_half(j, start)).astype(BF16))
            for j in range(4)
        ]

    each_part(close_last)

    def pool(start, carry):
        rows = lax.broadcasted_iota(jnp.int32, (8, chunk), 1) + start
        owner = jnp.zeros((8, chunk), jnp.int32)
        for end in ends:
            owner = owner + jnp.where(rows >= end, 1, 0)
        mine = owner == lax.broadcasted_iota(jnp.int32, (8, chunk), 0)
        mine = jnp.where(mine, 1.0, 0.0).astype(BF16)
        return carry + dense(mine, gw[pl.ds(start, chunk), :])

    slot_row = lax.broadcasted_iota(jnp.int32, (8, LANES), 0)
    area = jnp.zeros((8, LANES), jnp.int32)
    positive = jnp.full((8, LANES), -1, jnp.int32)
    for slot in range(slots):
        area = jnp.where(slot_row == slot, sides[slot] * sides[slot], area)
        positive = jnp.where(slot_row == slot, k.positives[0, stage, slot], positive)
    inverse_area = jnp.where(area > 0, 1.0 / jnp.maximum(area, 1).astype(F32), 0.0)
    inverse_area_wide = jnp.concatenate([inverse_area] * 4, axis=1)
    half_offset = 0.5 * jnp.log(jnp.full((8, LANES), k.normalizer[0] * NEG / BANK))
    pooled = each_chunk(pool, zeros(COUT)) * inverse_area_wide

    head = wst[AFTER_OUT : AFTER_OUT + COUT, :].astype(BF16)
    pooled_high, pooled_low = split(pooled)
    embed = dense(pooled_high, head) + dense(pooled_low, head)
    scale = lax.rsqrt(jnp.sum(embed * embed, axis=1, keepdims=True) + 1e-06)
    unit = embed * scale
    unit_parts = jnp.concatenate(split(unit), axis=0)
    lane = lax.broadcasted_iota(jnp.int32, (8, LANES), 1)
    parts = []
    for block in range(4):
        scores = across(unit_parts, wide2[:, lanes(block)])
        scores = scores[0:8, :] + scores[8:16, :]
        pieces = []
        for j in range(BANK // 4 // LANES):
            high = block * (BANK // 4 // LANES) + j
            half = scores[:, lanes(j)] * (0.5 / SOFTMAX_TEMPER) - half_offset
            sigma = 0.5 + 0.5 * jnp.tanh(half)
            chosen = jnp.where(positive == lane + high * LANES, 1.0, 0.0)
            pieces.append((gn[high * 8 : high * 8 + 8, :] + chosen) * sigma - chosen)
        parts = parts + list(split(jnp.concatenate(pieces, axis=1)))
    found = dense(jnp.concatenate(parts, axis=0), wide2[...])
    unit_grad = zeros(EMB)
    for block in range(4):
        for row in (16 * block, 16 * block + 8):
            unit_grad = unit_grad + found[row : row + 8, lanes(block)]
    unit_grad = jnp.where(inverse_area > 0.0, unit_grad, 0.0) * (1.0 / SOFTMAX_TEMPER)
    embed_grad = scale * unit_grad - embed * (
        scale * scale * scale * jnp.sum(embed * unit_grad, axis=1, keepdims=True)
    )
    grad_high, grad_low = split(embed_grad)
    pooled_grad = across(grad_high, head) + across(grad_low, head)
    pooled_grad = pooled_grad * inverse_area_wide
    for j in range(4):
        k.spread[8 * j : 8 * j + 8, :] = pooled_grad[:, lanes(j)]

    def last_slope(step, carry):
        start = pl.multiple_of(step * part, 16)
        owners = [tab[5, step * per + u] for u in range(per)]
        found, stores = [], []
        for j in range(4):
            upstream = jnp.concatenate(
                [
                    jnp.broadcast_to(k.spread[pl.ds(8 * j + owner, 1), :], (BLOCK, LANES))
                    for owner in owners
                ],
                axis=0,
            )
            upstream = upstream * slope_half(last_half(j, start))
            stores.append((gw, (pl.ds(start, part), lanes(j)), upstream.astype(BF16)))
            found.append(
                (
                    carry[j][0] + folded(upstream),
                    carry[j][1] + folded(upstream * at_block(big0, j, start, part)),
                )
            )
        put_late(stores)
        return tuple(found)

    pair = (zeros(), zeros())
    sums = lax.fori_loop(0, 25, last_slope, (pair,) * 4, unroll=UNROLL)
    bias_grads = [reduced(sums[j][0]) for j in range(4)]
    gain_grads = [normed_sum(L6, bias_grads[j], reduced(sums[j][1]), j) for j in range(4)]
    put_wide(6, 0, bias_grads)
    put_wide(6, 1, gain_grads)
    share(6)
    for j in range(4):
        wst[OUT_GAIN + j : OUT_GAIN + j + 1, :] = gain_grads[j]
        wst[OUT_BIAS + j : OUT_BIAS + j + 1, :] = bias_grads[j]
    wst[AFTER_OUT : AFTER_OUT + COUT, :] = (
        outer(pooled_high, grad_high) + outer(pooled_high, grad_low) + outer(pooled_low, grad_high)
    )
    for j in range(4):
        k.wout2_t[j * LANES : (j + 1) * LANES, :] = turned(k.wout2[:, lanes(j)])
        for r in range(2):
            k.wshort_t[j * LANES : (j + 1) * LANES, lanes(r)] = turned(
                k.wshort[r * LANES : (r + 1) * LANES, lanes(j)]
            )
    def put_turned(source, target, values):
        at = (target // 2) * 4 * MID + source * MID
        k.wmid1_t[at : at + MID, lanes(target % 2)] = values

    for tap in range(9):
        i, j = tap // 3, tap % 3
        source = 2 * (1 if i == 0 else 0) + (1 if j == 0 else 0)
        target = 2 * (0 if i == 1 else 1) + (0 if j == 1 else 1)
        put_turned(source, target, turned(k.wmid1[tap * MID : (tap + 1) * MID, :]))
    for source in range(4):
        for target in range(4):
            if source & target != source:
                put_turned(source, target, jnp.zeros((MID, MID), BF16))
    collect(6)
    finish_back(L6, wide(0), wide(1), gain_wide(24), inverse_count)

    def back_value(layer, upstream, values, j=0):
        return (
            upstream * get_coef(layer, GRAD_A, j)
            - values * get_coef(layer, GRAD_E, j)
            - get_coef(layer, GRAD_D, j)
        )

    def back_sixth(start, carry):
        here = pl.ds(start, part)
        stores = []
        for j in range(4):
            values = back_value(
                L6, gw[here, lanes(j)].astype(F32), at_block(big0, j, start, part), j
            )
            stores.append((wide2, (here, lanes(j)), values.astype(BF16)))
        return carry, stores

    each_part(back_sixth)

    def back_rows(values, slope):
        def body(start, carry):
            here = pl.ds(start, part)
            upstream = gn[here, :] * slope[here, :].astype(F32)
            upstream = jnp.where(live_rows(start, part), upstream, 0.0)
            carry = (carry[0] + folded(upstream), carry[1] + folded(upstream * values[here, :]))
            return carry, [(gn, (here, slice(None)), upstream)]

        return each_part(body, (zeros(), zeros()), parts=5)

    def send_back(number, row, layer, sums):
        bias_grad = reduced(sums[0])
        gain_grad = normed_sum(layer, bias_grad, reduced(sums[1]))
        put_narrow(number, 0, bias_grad)
        put_narrow(number, 1, gain_grad)
        share(number)
        put_small(row, gain_grad)
        put_small(row + 1, bias_grad)

    def rounded_product(left, right):
        def body(start, carry):
            here = pl.ds(start, chunk)
            gn[here, :] = dense(left[here, :], right[...]).astype(BF16).astype(F32)
            return carry

        each_chunk(body)

    rounded_product(wide2, k.wout4_t)
    send_back(7, 2, L5, back_rows(k.t5, k.dtn))

    def put_wide_matrix(at, values):
        for r in range(values.shape[0] // LANES):
            for j in range(4):
                wst[pl.ds(at + 4 * LANES * r + j, LANES, stride=4), :] = values[
                    r * LANES : (r + 1) * LANES, lanes(j)
                ]

    def turned_rows(ref, lane=0):
        return turned(ref[:, lane * LANES : (lane + 1) * LANES])

    k.turn[0:LANES, :] = turned_rows(k.h4)
    put_wide_matrix(0, dense(k.turn[0:LANES, :], wide2[0:out_rows, :]))
    stage_piece(LAST)
    keep_narrow_slope(L4, k.t4, k.h4)
    collect(7)
    finish_back(L5, narrow(0), narrow(1), gain_narrow(6), inverse_count)

    def back_close(layer, values):
        def body(start, carry):
            here = pl.ds(start, part)
            found = back_value(layer, gn[here, :], values[here, :])
            found = jnp.where(live_rows(start, part), found, 0.0).astype(BF16)
            return carry, [
                (k.dtn, (here, slice(None)), found),
                (src, (pl.ds(PAD + start, part), slice(None)), found.astype(F32)),
            ]

        each_part(body, parts=5)

    back_close(L5, k.t5)

    def open_back_fourth(step, carry):
        chunk_start = pl.multiple_of(step * chunk, 16)

        def fill(i, inner):
            stores = []
            for u in range(per):
                at = pl.multiple_of((i * per + u) * BLOCK, 16)
                number = step * (chunk // BLOCK) + i * per + u
                stores = stores + near_columns(number, chunk_start + at, k.colt, at)
            put_late(stores)
            return inner

        lax.fori_loop(0, chunk // BLOCK // per, fill, 0, unroll=UNROLL)
        gn[pl.ds(chunk_start, chunk), :] = dense(k.colt[...], k.wmid3_t[...])
        return carry

    lax.fori_loop(0, 5, open_back_fourth, 0, unroll=UNROLL)
    send_back(8, 0, L4, back_rows(k.t4, k.h4))

    def columns_grad(columns, store):
        k.turn[0:LANES, :] = turned_rows(k.dtn)
        for group in range(3):
            found = dense(k.turn[0:LANES, :], columns[:, 3 * group * LANES : 3 * (group + 1) * LANES])
            for j in range(3):
                store(3 * group + j, found[:, lanes(j)].T)

    def store_third(tap, values):
        wst[THIRD_MID + tap * MID : THIRD_MID + (tap + 1) * MID, :] = values

    columns_grad(k.cols2, store_third)
    give_line(LAST)
    keep_narrow_slope(L2, k.t2, k.h4)
    collect(8)
    finish_back(L4, narrow(0), narrow(1), gain_narrow(4), inverse_count)
    back_close(L4, k.t4)

    def back_block(start, carry):
        here = pl.ds(start, part)
        arrived = dense(k.dtn[here, :], k.win3_t[...])
        found, stores = [], []
        for j in range(4):
            upstream = arrived[:, lanes(j)] + gw[here, lanes(j)].astype(F32)
            upstream = upstream.astype(BF16).astype(F32) * second_slope(j, start)
            stores.append((gw, (here, lanes(j)), upstream.astype(BF16)))
            found.append(
                (
                    carry[j][0] + folded(upstream),
                    carry[j][1] + folded(upstream * at_block(big1, j, start, part)),
                    carry[j][2] + folded(upstream * at_block(big2, j, start, part)),
                )
            )
        return tuple(found), stores

    sums = each_part(back_block, ((zeros(), zeros(), zeros()),) * 4)
    bias_grads, gain_grads, short_grads = (
        [reduced(sums[j][which]) for j in range(4)] for which in range(3)
    )
    gain_grads = [normed_sum(L3, bias_grads[j], gain_grads[j], j) for j in range(4)]
    short_grads = [normed_sum(LS, bias_grads[j], short_grads[j], j) for j in range(4)]
    put_wide(9, 0, bias_grads)
    put_wide(9, 1, gain_grads)
    put_wide(9, 2, short_grads)
    share(9)
    k.turn[0:LANES, :] = turned_rows(k.dtn)
    found = dense(k.turn[0:LANES, :], k.y[...])
    for j in range(4):
        wst[j * LANES : (j + 1) * LANES, :] = found[:, lanes(j)].T
    wst[THIRD_GAIN : THIRD_BIAS + 1, :] = k.small[0:2, :]
    wst[THIRD_MID_GAIN : THIRD_MID_BIAS + 1, :] = k.small[2:4, :]
    stage_piece(THIRD)
    give_home(LAST)
    keep_first_slope()
    collect(9)
    finish_back(L3, wide(0), wide(1), gain_wide(8), inverse_count)
    finish_back(LS, wide(0), wide(2), gain_wide(16), inverse_count)

    def back_third(start, carry):
        here = pl.ds(start, part)
        below = pl.ds(out_rows + start, part)
        stores = []
        for j in range(4):
            upstream = gw[here, lanes(j)].astype(F32)
            found = back_value(L3, upstream, at_block(big1, j, start, part), j)
            stores.append((wide2, (here, lanes(j)), found.astype(BF16)))
            found = back_value(LS, upstream, at_block(big2, j, start, part), j)
            stores.append((wide2, (below, lanes(j)), found.astype(BF16)))
        return carry, stores

    each_part(back_third)
    rounded_product(wide2, k.wout2_t)
    send_back(10, 6, L2, back_rows(k.t2, k.h4))
    for j in range(4):
        wst[OUT_GAIN + j : OUT_GAIN + j + 1, :] = gain_grads[j]
        wst[OUT_BIAS + j : OUT_BIAS + j + 1, :] = bias_grads[j]
        wst[SHORT_GAIN + j : SHORT_GAIN + j + 1, :] = short_grads[j]
        wst[SHORT_BIAS + j : SHORT_BIAS + j + 1, :] = bias_grads[j]
    k.turn[0:LANES, :] = turned_rows(k.h2)
    put_wide_matrix(0, dense(k.turn[0:LANES, :], wide2[0:out_rows, :]))
    for half in range(2):
        k.turn[0:LANES, :] = turned_rows(k.xs, half)
        put_wide_matrix(
            AFTER_OUT + half * 4 * LANES, dense(k.turn[0:LANES, :], wide2[out_rows : 2 * out_rows, :])
        )
    stage_piece(SECOND)
    give_line(THIRD)

    def back_picked(start, carry):
        found = dense(wide2[pl.ds(out_rows + start, chunk), :], k.wshort_t[...])
        found = found.astype(BF16).astype(F32)
        for half in range(2):
            big2[pl.ds(half * plane + PAD + start, chunk), :] = found[:, lanes(half)]
        return carry

    each_chunk(back_picked)
    for half in range(2):
        big2[half * plane : half * plane + PAD, :] = jnp.zeros((PAD, LANES), F32)
    collect(10)
    finish_back(L2, narrow(0), narrow(1), gain_narrow(2), inverse_count)
    back_close(L2, k.t2)


    def back_columns(number, start):
        here = pl.ds(start, BLOCK)
        width = tab[0, number]
        bottom, right, live = masks[1, here, :], masks[3, here, :], live_block(width)
        shifts = ((0, live), (1, right), (width, bottom), (width + 1, bottom * right))
        return [
            (
                wide2,
                (here, lanes(which)),
                src[pl.ds(PAD + start + shift, BLOCK), :].astype(BF16) * mask,
            )
            for which, (shift, mask) in enumerate(shifts)
        ]

    each_block(back_columns)

    def back_planes(start, carry):
        here = pl.ds(start, chunk)
        even = dense(wide2[here, 0 : 2 * MID], k.wmid1_t[0 : 2 * MID, :])
        odd = dense(wide2[here, :], k.wmid1_t[4 * MID : 8 * MID, :])
        for number in range(4):
            found = (even, odd)[number // 2][:, lanes(number % 2)]
            big0[pl.ds(number * plane + PAD + start, chunk), :] = found
        return carry

    each_chunk(back_planes)

    in_unroll = 10

    def to_input_order(i, carry):
        stores = []
        for u in range(in_unroll):
            number = i * in_unroll + u
            first, second = tab[7, number], tab[8, number]
            near = near_rows(8, tab[9, number])
            for column in range(2):
                values = jnp.where(
                    near,
                    big0[pl.ds(first + column * plane, 8), :],
                    big0[pl.ds(second + column * plane, 8), :],
                )
                at = pl.ds(number * BLOCK + column, 8, stride=2)
                stores.append((big1, (at, slice(None)), values))
        put_late(stores)
        return carry

    lax.fori_loop(0, in_rows // BLOCK // in_unroll, to_input_order, 0, unroll=UNROLL)

    def back_first(start, carry):
        stores = []
        for block in range(4):
            rows = pl.ds(block * out_rows + start, part)
            upstream = big1[rows, :] * k.cols2[pl.ds(start, part), lanes(block)].astype(F32)
            carry = (carry[0] + folded(upstream), carry[1] + folded(upstream * t1[rows, :]))
            stores.append((big1, (rows, slice(None)), upstream))
        return carry, stores

    sums = each_part(back_first, (zeros(), zeros()))
    send_back(11, 4, L1, sums)
    def store_first(tap, values):
        at = piece_at[FIRST_MID] + tap * MID
        k.gb[at : at + MID, :] = values.astype(BF16)

    columns_grad(k.cols1, store_first)
    if padded[FIRST_MID] > 9 * MID:
        at = piece_at[FIRST_MID]
        k.gb[at + 9 * MID : at + padded[FIRST_MID], :] = jnp.zeros(
            (padded[FIRST_MID] - 9 * MID, LANES), BF16
        )
    give_scatter(FIRST_MID)
    give_line(SECOND)
    give_home(THIRD)

    found = jnp.zeros((MID, CIN), F32)
    for block in range(4):
        rows = slice(block * out_rows, (block + 1) * out_rows)
        k.turn[0:LANES, :] = turned(big1[rows, :])
        found = found + dense(k.turn[0:LANES, :], feat[rows, :])
    first_g = [found[:, lanes(half)].T for half in range(2)]
    for half in range(2):
        k.win1_t[:, lanes(half)] = turned(wts[0, half * LANES : (half + 1) * LANES, :])
    gn[...] = jnp.zeros(gn.shape, F32)
    collect(11)
    finish_back(L1, narrow(0), narrow(1), gain_narrow(0), 0.25 * inverse_count)

    at = piece_at[FIRST_IN]
    for half in range(2):
        rows = slice(half * LANES, (half + 1) * LANES)
        values = first_g[half] * get_coef(L1, GRAD_A) - k.first_t[rows, :] * get_coef(L1, GRAD_E)
        values = values - k.first_s[rows, :] * get_coef(L1, GRAD_D)
        k.gb[at + half * LANES : at + (half + 1) * LANES, :] = values.astype(BF16)
    k.gb[at + CIN : at + CIN + 16, :] = jnp.concatenate(
        [k.small[4:8, :], jnp.zeros((12, LANES), F32)], axis=0
    ).astype(BF16)
    k.gb[at + CIN + 16 : at + padded[FIRST_IN], :] = jnp.zeros(
        (padded[FIRST_IN] - CIN - 16, LANES), BF16
    )
    give_scatter(FIRST_IN)
    give_line(FIRST_MID)
    give_home(SECOND)

    for block in range(4):

        def close_back_first(start, carry, block=block):
            rows = pl.ds(block * out_rows + start, part)
            found = back_value(L1, big1[rows, :], t1[rows, :])
            row = lax.broadcasted_iota(jnp.int32, (part, MID), 0) + (block * out_rows + start)
            found = jnp.where(row < 4 * rows_live, found, 0.0).astype(BF16)
            return carry, [(gw, (pl.ds(start, part), lanes(block)), found)]

        each_part(close_back_first, parts=5)

    give_line(FIRST_IN)
    give_home(FIRST_MID)


    def ordered(target, source, rows):
        def body(i, carry):
            start = pl.multiple_of(i * 64, 64)
            wst[pl.ds(target + start, 64), :] = k.got_all[pl.ds(source + start, 64), :].astype(F32)
            return carry

        lax.fori_loop(0, rows // 64, body, 0, unroll=2)

    def blank(at):
        wst[at:ROWS, :] = jnp.zeros((ROWS - at, LANES), F32)

    def input_grad(block, carry):
        lane = pl.ds(pl.multiple_of(block * LANES, LANES), LANES)
        for piece in range(5):
            low = (piece % 2) * 2 * chunk
            stores = []
            for u in range(chunk // BLOCK):
                number = (block * 5 + piece) * (chunk // BLOCK) + u
                near = near_rows(8, tab[9, number])
                for half in range(2):
                    values = jnp.where(
                        near,
                        big2[pl.ds(tab[10, number] + half * plane, 8), :],
                        big2[pl.ds(tab[11, number] + half * plane, 8), :],
                    )
                    at = low + half * chunk + u * BLOCK
                    stores.append((gn, (slice(at, at + BLOCK, 2), slice(None)), values))
            put_late(stores)
            found = dense(gw[piece * chunk : (piece + 1) * chunk, lane], k.win1_t[...])
            rows = pl.ds(pl.multiple_of(block * out_rows + piece * chunk, 16), chunk)
            for half in range(2):
                at = low + half * chunk
                feat[rows, lanes(half)] = (found[:, lanes(half)] + gn[at : at + chunk, :]).astype(
                    BF16
                )
        return carry

    lax.fori_loop(0, 2, input_grad, 0)
    give_home(FIRST_IN)
    take_all(FIRST_MID)

    @pl.when(stage == 0)
    def unused_first_mid():
        blank(MID_BIAS + 1)
        ordered(MID_AT, 0, 9 * MID)

    lax.fori_loop(2, 4, input_grad, 0)
    input_copy = pltpu.make_async_copy(feat, k.input_grad_at, k.out_sem.at[0])
    input_copy.start()

    for number in (LAST, THIRD, SECOND, FIRST_IN):
        take_all(number)

    for number in (LAST, THIRD, SECOND):

        @pl.when(stage == PIECES[number][0])
        def unused_ordered(number=number):
            rows = min(padded[number], ROWS // 128 * 128)
            if rows < ROWS:
                blank(rows)
            ordered(0, 0, rows)
            if rows < PIECES[number][1]:
                tail = k.got_all[rows : rows + 16, :].astype(F32)
                wst[rows : rows + 16, :] = tail

    @pl.when(stage == 0)
    def unused_first():
        at = section_at[FIRST_IN]
        ordered(0, at, CIN)
        gains = k.got_all[at + CIN : at + CIN + 16, :].astype(F32)
        wst[IN_GAIN : IN_BIAS + 1, :] = gains[0:2, :]
        wst[MID_GAIN : MID_BIAS + 1, :] = gains[2:4, :]

    out_copy = pltpu.make_async_copy(wst.at[pl.ds(0, ROWS)], k.weight_grads_at, k.grad_sem)
    out_copy.start()
    input_copy.wait()
    for copy in weight_copies:
        copy.wait_send()
    for number in range(EXCHANGES):
        wait_for(k.stat_send.at[number], incoming(number, pl.ds(0, batches - 1)))
    for number in range(len(PIECES)):
        end_sends(number)
    out_copy.wait()


def write_kernel(weight_rows, input_rows, weight_out, input_out, held_weights, held, sems):
    count = 10
    part = input_rows.shape[0] // count
    pairs = [
        (weight_rows.at[pl.ds(0, ROW)], held_weights, weight_out.reshape(ROW, LANES)),
        *[
            (input_rows.at[rows], held.at[rows], input_out.at[rows])
            for rows in [pl.ds(i * part, part) for i in range(count)]
        ],
    ]
    arriving = [
        pltpu.make_async_copy(source, middle, sems.at[0, i])
        for i, (source, middle, target) in enumerate(pairs)
    ]
    leaving = [
        pltpu.make_async_copy(middle, target, sems.at[1, i])
        for i, (source, middle, target) in enumerate(pairs)
    ]
    for copy in arriving:
        copy.start()
    for i in range(len(pairs)):
        arriving[i].wait()
        leaving[i].start()
    for copy in leaving:
        copy.wait()


def shards(features, weights, crop_kind, positives, negatives, bank, normalizer):
    phases = lax.axis_size("phase")
    batches = lax.axis_size("batch")
    in_rows = features.shape[0] // MICRO
    out_rows = in_rows // 4
    plane = out_rows + 2 * PAD
    slots = crop_kind.shape[2]
    chunk = out_rows // 5
    part = out_rows // 25
    group = 2 * phases
    levels = line_levels(batches // 2)
    padded = [-(-rows // (16 * group)) * 16 * group for unused, rows in PIECES]
    widest = max(*padded[:3], padded[3] + padded[4])
    eighth = sum(padded) // group
    staged = max(ROWS, *padded[:3])
    any_space = pl.BlockSpec(memory_space=pl.ANY)
    smem = pl.BlockSpec(memory_space=pltpu.SMEM)

    def held(*shape, dtype=F32):
        return pltpu.VMEM(shape, dtype)

    def sems(*shape):
        return pltpu.SemaphoreType.DMA(shape)

    def low(*shape):
        return held(*shape, dtype=BF16)

    kept_slopes = {"slope23": low(out_rows, COUT)} if batches <= 8 else {}

    inputs = {
        "features_at": (features, any_space),
        "weights_at": (weights, any_space),
        "negatives_at": (jnp.transpose(negatives, (0, 2, 1, 3)), any_space),
        "bank_at": (bank, any_space),
        "kinds": (jnp.transpose(crop_kind, (2, 1, 0)), smem),
        "positives": (positives, smem),
        "normalizer": (normalizer, smem),
    }
    outputs = {
        "weight_grads_at": jax.ShapeDtypeStruct((ROWS, LANES), F32),
        "input_grad_at": jax.ShapeDtypeStruct((in_rows, CIN), BF16),
    }
    scratch = {
        "feat": low(in_rows, CIN),
        "t1": held(in_rows, MID),
        "big0": held(4 * plane, MID),
        "big1": held(in_rows, MID),
        "big2": held(4 * plane, MID),
        "cols1": low(out_rows, 9 * MID),
        "cols2": low(out_rows, 9 * MID),
        "colt": low(chunk, 9 * MID),
        "src": held(plane, MID),
        "t2": held(out_rows, MID),
        "t4": held(out_rows, MID),
        "t5": held(out_rows, MID),
        "gn": held(out_rows, MID),
        "h2": low(out_rows, MID),
        "h4": low(out_rows, MID),
        "xs": low(out_rows, CIN),
        "y": low(out_rows, COUT),
        "gw": low(out_rows, COUT),
        "wide2": low(BANK // 4, COUT),
        "dtn": low(out_rows, MID),
        "turn": low(LANES + 16, out_rows),
        "first_t": held(CIN, MID),
        "first_s": held(CIN, MID),
        "masks": low(4, out_rows, LANES),
        "raw": low(1, GRAD_LEN),
        "wts": low(phases, ROWS, LANES),
        "wst": held(staged, LANES),
        "wmid1": low(9 * MID, MID),
        "wmid3": low(9 * MID, MID),
        "wout2": low(MID, COUT),
        "wshort": low(CIN, COUT),
        "wout4": low(MID, COUT),
        "wout2_t": low(COUT, MID),
        "wshort_t": low(COUT, CIN),
        "wout4_t": low(COUT, MID),
        "wmid1_t": low(8 * MID, 2 * MID),
        "wmid3_t": low(9 * MID, MID),
        "win1_t": low(MID, CIN),
        "win3_t": low(MID, COUT),
        "gains": held(32, LANES),
        "small": held(8, LANES),
        "coef": held(56, COUT),
        "spread": held(32, LANES),
        "neg": held(slots, MICRO, NEG, dtype=jnp.int32),
        **kept_slopes,
        "tabv": held(16, TABLE, dtype=jnp.int32),
        "tab": pltpu.SMEM((16, TABLE), jnp.int32),
        "send": held(SPAN_ROWS, LANES),
        "send_narrow": held(EXCHANGES, 2, LANES),
        "recv_narrow": held(EXCHANGES, batches, 2, LANES),
        "recv": held(batches, SPAN_ROWS, LANES),
        "total": held(16, LANES),
        "gb": low(sum(padded), LANES),
        "got_scatter": low(group - 1, eighth, LANES),
        "line_sum": low(len(levels), eighth, LANES),
        "got_line": low(sum(levels) - len(levels), eighth, LANES),
        "home": low(eighth, LANES),
        "got_all": low(widest, LANES),
        "raw_sem": pltpu.SemaphoreType.DMA,
        "feat_sem": sems(4),
        "bank_sem": sems(2),
        "neg_sem": pltpu.SemaphoreType.DMA,
        "tab_sem": pltpu.SemaphoreType.DMA,
        "weight_send": sems(2, phases),
        "weight_recv": sems(2, phases),
        "stat_send": sems(EXCHANGES),
        "stat_recv": sems(EXCHANGES),
        "scatter_send": sems(len(PIECES)),
        "scatter_recv": sems(len(PIECES)),
        "line_send": sems(len(levels), len(PIECES)),
        "line_recv": sems(len(levels), len(PIECES)),
        "home_send": sems(len(PIECES)),
        "home_recv": sems(len(PIECES)),
        "out_sem": sems(4),
        "grad_sem": pltpu.SemaphoreType.DMA,
    }
    names = (*inputs, *outputs, *scratch)
    weight_rows, input_rows = pl.pallas_call(
        functools.partial(kernel, names, batches, phases, in_rows, slots),
        out_shape=tuple(outputs.values()),
        in_specs=[spec for unused, spec in inputs.values()],
        out_specs=(any_space,) * len(outputs),
        scratch_shapes=list(scratch.values()),
        compiler_params=pltpu.CompilerParams(
            collective_id=0, has_side_effects=True, vmem_limit_bytes=64 * 1024 * 1024
        ),
    )(*[value for value, unused in inputs.values()])
    weight_grads, input_grad = pl.pallas_call(
        write_kernel,
        out_shape=(
            jax.ShapeDtypeStruct((1, GRAD_LEN), F32),
            jax.ShapeDtypeStruct((in_rows, CIN), BF16),
        ),
        in_specs=[any_space, any_space],
        out_specs=(any_space, any_space),
        scratch_shapes=[held(ROW, LANES), low(in_rows, CIN), sems(2, 11)],
        compiler_params=pltpu.CompilerParams(vmem_limit_bytes=64 * 1024 * 1024),
    )(weight_rows, input_rows)
    return (weight_grads, input_grad)


def solution(mesh):
    placed = (
        P("batch", None),
        P("phase", None),
        P(),
        P("batch", None, None),
        P("batch", None, None, None),
        P(),
        P(),
    )
    return jax.shard_map(
        shards,
        mesh=mesh,
        in_specs=placed,
        out_specs=(P("phase", None), P(("batch", "phase"), None)),
        check_vma=False,
    )
```

```python
import functools
import math
import types

import jax
import jax.numpy as jnp
from jax import lax
from jax.experimental import pallas as pl
from jax.experimental.pallas import tpu as pltpu
from jax.sharding import PartitionSpec as P

CIN = 256
MID = 128
COUT = 512
EMB = 128
SIDE_UNIT = 4
MICRO = 4
NEG = 4096
BANK = 16384
GRAD_LEN = 213504
LANES = 128
SOFTMAX_TEMPER = 0.07
EPSILON = 1e-05

PAD = 48
ROW = GRAD_LEN // LANES
ROWS = -(-ROW // 16) * 16
BLOCK = 16
TABLE = 512
UNROLL = 5
EARLY = 272
AHEAD = 80
MESH = pl.DeviceIdType.MESH
F32 = jnp.float32
BF16 = jnp.bfloat16

IN_GAIN, IN_BIAS, MID_AT = CIN, CIN + 1, CIN + 2
MID_GAIN, MID_BIAS = MID_AT + 9 * MID, MID_AT + 9 * MID + 1
THIRD_GAIN, THIRD_BIAS, THIRD_MID = COUT, COUT + 1, COUT + 2
THIRD_MID_GAIN, THIRD_MID_BIAS = THIRD_MID + 9 * MID, THIRD_MID + 9 * MID + 1
OUT_GAIN, OUT_BIAS, AFTER_OUT = 512, 516, 520
SHORT_GAIN, SHORT_BIAS = AFTER_OUT + 1024, AFTER_OUT + 1028

EXCHANGES = 12
SPANS = {2: 16, 5: 8, 6: 8, 9: 16}
STARTS = {2: 0, 5: 16, 6: 24, 9: 32}
SPAN_ROWS = 48

PIECES = ((3, 1032), (2, 1668), (1, 1552), (0, 9 * MID), (0, 260))
LAST, THIRD, SECOND, FIRST_MID, FIRST_IN = range(5)

L1, L2, L3, LS, L4, L5, L6 = range(7)
HALF_SCALE, HALF_SHIFT, INVERSE, NEG_MEAN, GRAD_A, GRAD_E, GRAD_D = range(7)


def dense(left, right):
    return jnp.dot(left, right, preferred_element_type=F32)


def across(left, right):
    return lax.dot_general(left, right, (((1,), (1,)), ((), ())), preferred_element_type=F32)


def outer(left, right):
    return lax.dot_general(left, right, (((0,), (0,)), ((), ())), preferred_element_type=F32)


def folded(values):
    rows, width = values.shape
    return values.reshape(rows // 8, 8, width).sum(axis=0)


def silu_half(half):
    return half + half * jnp.tanh(half)


def slope_half(half):
    bend = jnp.tanh(half)
    return 0.5 * (1.0 + bend + half * (1.0 - bend * bend))


def split(values):
    high = values.astype(BF16)
    return high, (values - high.astype(F32)).astype(BF16)


def line_levels(lines):
    return [lines] if lines <= 8 else [lines // 8, 8]


def kernel(names, batches, phases, in_rows, slots, *refs):
    k = types.SimpleNamespace(**dict(zip(names, refs, strict=True)))
    out_rows = in_rows // 4
    plane = out_rows + 2 * PAD
    chunk = out_rows // 5
    part = out_rows // 25
    blocks = out_rows // BLOCK
    per = part // BLOCK
    me = lax.axis_index("batch")
    stage = lax.axis_index("phase")
    core = lax.rem(me, 2)
    line = lax.div(me, 2)
    lines = batches // 2
    group = 2 * phases
    mine = 2 * stage + core
    levels = line_levels(lines)
    half_bank = BANK // 2
    quarter = in_rows // 4
    feat, t1, big0, big1, big2, src = k.feat, k.t1, k.big0, k.big1, k.big2, k.src
    tab, masks, wst, wts, gw, wide2, gn = k.tab, k.masks, k.wst, k.wts, k.gw, k.wide2, k.gn

    def batch_peer(i):
        return {"batch": lax.rem(me + i, batches)}

    def phase_peer(i):
        return {"phase": lax.rem(stage + i, phases)}

    def remote(source, target, send_sem, recv_sem, device):
        return pltpu.make_async_remote_copy(
            src_ref=source,
            dst_ref=target,
            send_sem=send_sem,
            recv_sem=recv_sem,
            device_id=device,
            device_id_type=MESH,
        )

    def wait_for(sem, region):
        pltpu.make_async_copy(region, region, sem).wait()

    barrier = pltpu.get_barrier_semaphore()

    def greet(i, carry):
        pl.semaphore_signal(barrier, inc=1, device_id=batch_peer(i), device_id_type=MESH)
        return carry

    lax.fori_loop(1, batches, greet, 0)
    for i in range(1, phases):
        for other in (me, 2 * line + 1 - core):
            pl.semaphore_signal(
                barrier,
                inc=1,
                device_id={"phase": lax.rem(stage + i, phases), "batch": other},
                device_id_type=MESH,
            )

    raw_copy = pltpu.make_async_copy(k.weights_at, k.raw, k.raw_sem)
    raw_copy.start()
    feat_copies = []
    for i in range(4):
        copy = pltpu.make_async_copy(
            k.features_at.at[pl.ds(pl.multiple_of(stage * in_rows + i * quarter, 16), quarter)],
            feat.at[pl.ds(i * quarter, quarter)],
            k.feat_sem.at[i],
        )
        copy.start()
        feat_copies.append(copy)
    neg_copy = pltpu.make_async_copy(k.negatives_at.at[0], k.neg, k.neg_sem)
    neg_copy.start()
    bank_copies = [
        pltpu.make_async_copy(
            k.bank_at.at[pl.ds(i * half_bank, half_bank)],
            big0.at[pl.ds(0, half_bank)],
            k.bank_sem.at[i],
        )
        for i in range(2)
    ]

    def side_of(kind):
        return SIDE_UNIT * jnp.where(
            kind == 1, 5, jnp.where(kind == 2, 7, jnp.where(kind == 3, 9, 0))
        )

    sides = [side_of(k.kinds[slot, stage, me]) for slot in range(slots)]
    ends = []
    for side in sides:
        ends.append(side * side + (ends[-1] if ends else 0))
    starts = [0, *ends[:-1]]
    rows_live = ends[-1]

    def all_areas(i, carry):
        for slot in range(slots):
            side = side_of(k.kinds[slot, stage, i])
            carry = carry + side * side
        return carry

    live_pixels = lax.fori_loop(0, batches, all_areas, 0)
    inverse_count = 1.0 / jnp.full((1, LANES), live_pixels, jnp.int32).astype(F32)[:, 0:1]

    def place(first):
        base = jnp.zeros_like(first)
        width = jnp.zeros_like(first)
        slot = jnp.full_like(first, 7)
        for number in range(slots):
            inside = (first >= starts[number]) & (first < ends[number])
            base = jnp.where(inside, starts[number], base)
            width = jnp.where(inside, sides[number], width)
            slot = jnp.where(inside, number, slot)
        return base, width, slot

    def divided(value, side):
        factor = jnp.zeros_like(side)
        for kind in (5, 7, 9):
            factor = jnp.where(side == SIDE_UNIT * kind, 65536 // (SIDE_UNIT * kind) + 1, factor)
        return lax.shift_right_logical(value * factor, jnp.full_like(value, 16))

    index = lax.broadcasted_iota(jnp.int32, (1, TABLE), 1)
    first = BLOCK * index
    base, width, slot = place(first)
    live = width > 0
    local = jnp.where(live, first - base, 0)
    row = divided(local, width)
    left = jnp.where(live, (row + 1) * width - local, BLOCK)
    begin = jnp.where(live, 4 * base + 2 * (local + row * width), 4 * first)
    jump = jnp.where(left < BLOCK, 2 * width, 0)
    window_at = lax.shift_right_logical(
        index * (65536 // per + 1), jnp.full_like(index, 16)
    ) * (4 * part) - AHEAD
    in_window = begin - jnp.maximum(window_at, 0)
    pixel = BLOCK // 4 * index
    in_base, in_width, unused_slot = place(pixel)
    in_live = in_width > 0
    in_side = jnp.maximum(in_width, 1)
    in_local = 4 * (pixel - in_base)
    in_row = divided(2 * (pixel - in_base), in_width)
    in_left = jnp.where(in_live, (2 * in_side - (in_local - in_row * 2 * in_side)) >> 1, 8)
    upper = in_row >> 1
    odd = in_row - 2 * upper
    lower = (in_row + 1) >> 1
    here = in_base + upper * in_side + (in_side - in_left)
    below = in_base + lower * in_side - in_left
    at_here = jnp.where(in_live, PAD + here + odd * (2 * plane), PAD + out_rows - BLOCK)
    at_below = jnp.where(in_left < 8, PAD + below + (1 - odd) * (2 * plane), at_here)
    even_here = jnp.where(in_live & (odd == 0), PAD + here, 0)
    even_below = jnp.where(in_live & (in_left < 8) & (odd == 1), PAD + below, 0)
    columns = (width, local, begin, left, jump, slot, 2 * width)
    columns = columns + (at_here, at_below, in_left, even_here, even_below, in_window)
    k.tabv[...] = jnp.zeros(k.tabv.shape, jnp.int32)
    for number, column in enumerate(columns):
        k.tabv[number : number + 1, :] = column
    tab_copy = pltpu.make_async_copy(k.tabv, tab, k.tab_sem)
    tab_copy.start()

    raw_copy.wait()

    def to_rows(first, last):
        def body(i, carry):
            found = []
            for u in range(16):
                at = pl.multiple_of((i * 16 + u) * LANES, LANES)
                found.append(k.raw[0:1, pl.ds(at, LANES)].astype(F32))
            for u, values in enumerate(found):
                wst[pl.ds(i * 16 + u, 1), :] = values
            return carry

        lax.fori_loop(first // 16, last // 16, body, 0)
        done = last // 16 * 16
        for at in range(done, last):
            wst[at : at + 1, :] = k.raw[0:1, at * LANES : (at + 1) * LANES].astype(F32)
        if done < last:
            wst[last : done + 16, :] = jnp.zeros((done + 16 - last, LANES), F32)

        def convert(i, carry):
            rows = pl.ds(pl.multiple_of(i * 16, 16), 16)
            wts[stage, rows, :] = wst[rows, :].astype(BF16)
            return carry

        lax.fori_loop(first // 16, -(-last // 16), convert, 0, unroll=2)

    weight_spans = ((0, EARLY), (EARLY, ROWS - EARLY))

    def send_weights(number):
        at, rows = weight_spans[number]
        region = wts.at[stage, pl.ds(at, rows)]
        copies = []
        for i in range(1, phases):
            copy = remote(
                region,
                region,
                k.weight_send.at[number, i],
                k.weight_recv.at[number, stage],
                phase_peer(i),
            )
            copy.start()
            copies.append(copy)
        return copies

    def need_weights(number, section):
        at, rows = weight_spans[number]

        @pl.when(stage != section)
        def unused_wait():
            wait_for(k.weight_recv.at[number, section], wts.at[section, pl.ds(at, rows)])

    to_rows(0, EARLY)
    pl.semaphore_wait(barrier, batches - 1 + 2 * (phases - 1))
    weight_copies = send_weights(0)

    def outgoing(number):
        if number in SPANS:
            return k.send.at[pl.ds(STARTS[number], SPANS[number])]
        return k.send_narrow.at[number]

    def incoming(number, which):
        if number in SPANS:
            return k.recv.at[which, pl.ds(STARTS[number], SPANS[number])]
        return k.recv_narrow.at[number, which]

    def share(number):
        def give(i, carry):
            remote(
                outgoing(number),
                incoming(number, me),
                k.stat_send.at[number],
                k.stat_recv.at[number],
                {"batch": lax.rem(batches - 1 - me + i, batches)},
            ).start()
            return carry

        mirrored = lax.rem(2 * me + 1, batches)

        def skip(i, carry):
            return give(i + jnp.where(i >= mirrored, 1, 0), carry)

        lax.fori_loop(0, batches - 1, skip, 0, unroll=batches <= 8)
        incoming(number, me)[...] = outgoing(number)[...]

    def collect(number):
        wait_for(k.stat_recv.at[number], incoming(number, pl.ds(0, batches - 1)))

        def add(i, carry):
            return carry + incoming(number, i)[...]

        rows = SPANS.get(number, 2)
        k.total[pl.ds(0, rows), :] = lax.fori_loop(
            1, batches, add, incoming(number, 0)[...], unroll=batches <= 8
        )

    padded = [-(-rows // (16 * group)) * 16 * group for unused, rows in PIECES]
    piece_at = [sum(padded[:i]) for i in range(len(padded))]
    section_at = [0, 0, 0, 0, padded[FIRST_MID]]
    part_of = [rows // group for rows in padded]

    def summed(rows, target, *sources):
        total = sources[0](0, rows).astype(F32)
        for source in sources[1:]:
            total = total + source(0, rows).astype(F32)
        target(0, rows, total.astype(BF16))

    def reader(ref, start):
        return lambda at, step: ref[pl.ds(pl.multiple_of(start + at, 16), step), :]

    def writer(ref, start):
        def write(at, step, values):
            ref[pl.ds(pl.multiple_of(start + at, 16), step), :] = values

        return write

    def give_scatter(number):
        rows, at = part_of[number], piece_at[number]

        def give(i, carry):
            other = lax.rem(mine + i, group)
            remote(
                k.gb.at[pl.ds(at + other * rows, rows)],
                k.got_scatter.at[i - 1, pl.ds(at // group, rows)],
                k.scatter_send.at[number],
                k.scatter_recv.at[number],
                {"phase": lax.div(other, 2), "batch": 2 * line + lax.rem(other, 2)},
            ).start()
            return carry

        lax.fori_loop(1, group, give, 0)

    def give_line(number):
        rows, at = part_of[number], piece_at[number]
        within = at // group
        wait_for(k.scatter_recv.at[number], k.got_scatter.at[:, pl.ds(within, rows)])

        def other(i):
            return lambda start, step: k.got_scatter[i, pl.ds(within + start, step), :]

        summed(
            rows,
            writer(k.line_sum.at[0], within),
            reader(k.gb, at + mine * rows),
            *[other(i) for i in range(group - 1)],
        )
        send_level(number, 0)

    def level_of(level):
        size, stride = levels[level], math.prod(levels[:level])
        return size, stride, sum(levels[:level]) - level, lax.rem(lax.div(line, stride), size)

    def send_level(number, level):
        size, stride, slot, digit = level_of(level)
        rows, within = part_of[number], piece_at[number] // group

        def give(i, carry):
            other = line + (lax.rem(digit + i, size) - digit) * stride
            remote(
                k.line_sum.at[level, pl.ds(within, rows)],
                k.got_line.at[slot + i - 1, pl.ds(within, rows)],
                k.line_send.at[level, number],
                k.line_recv.at[level, number],
                {"batch": 2 * other + core},
            ).start()
            return carry

        lax.fori_loop(1, size, give, 0)

    def add_level(number, level, target):
        size, stride, slot, digit = level_of(level)
        rows, within = part_of[number], piece_at[number] // group
        arrived = k.got_line.at[pl.ds(slot, size - 1), pl.ds(within, rows)]
        wait_for(k.line_recv.at[level, number], arrived)

        own = k.line_sum[level, pl.ds(within, rows), :].astype(F32)
        total = jnp.zeros((rows, LANES), F32)
        for which in range(size):
            at = jnp.minimum(lax.rem(digit - which - 1 + size, size), size - 2)
            found = k.got_line[slot + at, pl.ds(within, rows), :].astype(F32)
            total = total + jnp.where(which == digit, own, found)
        target[pl.ds(within, rows), :] = total.astype(BF16)

    def give_home(number):
        section = PIECES[number][0]
        rows, at = part_of[number], piece_at[number]
        within = at // group
        for level in range(len(levels) - 1):
            add_level(number, level, k.line_sum.at[level + 1])
            send_level(number, level + 1)
        add_level(number, len(levels) - 1, k.home)
        target = k.got_all.at[pl.ds(section_at[number] + mine * rows, rows)]

        def give(other):
            remote(
                k.home.at[pl.ds(within, rows)],
                target,
                k.home_send.at[number],
                k.home_recv.at[number],
                {"phase": section, "batch": 2 * line + other},
            ).start()

        @pl.when(stage != section)
        def unused_both():
            give(0)
            give(1)

        @pl.when(stage == section)
        def unused_one():
            give(1 - core)
            target[...] = k.home[pl.ds(within, rows), :]

    def take_all(number):
        rows, within = part_of[number], section_at[number]

        @pl.when(stage == PIECES[number][0])
        def unused_take():
            wait_for(k.home_recv.at[number], k.got_all.at[pl.ds(within, (group - 1) * rows)])

    def end_sends(number):
        rows, at = part_of[number], piece_at[number]
        within = at // group
        wait_for(k.scatter_send.at[number], k.got_scatter.at[:, pl.ds(within, rows)])
        for level in range(len(levels)):
            size, unused_stride, slot, unused_digit = level_of(level)
            sent = k.got_line.at[pl.ds(slot, size - 1), pl.ds(within, rows)]
            wait_for(k.line_send.at[level, number], sent)

        @pl.when(stage != PIECES[number][0])
        def unused_away():
            wait_for(k.home_send.at[number], k.got_all.at[pl.ds(0, 2 * rows)])

        @pl.when(stage == PIECES[number][0])
        def unused_home():
            wait_for(k.home_send.at[number], k.got_all.at[pl.ds(0, rows)])

    def stage_piece(number):
        rows, used, at = padded[number], PIECES[number][1], piece_at[number]
        if used < rows:
            wst[used:rows, :] = jnp.zeros((rows - used, LANES), F32)

        def convert(i, carry):
            start = pl.multiple_of(i * 64, 64)
            k.gb[pl.ds(at + start, 64), :] = wst[pl.ds(start, 64), :].astype(BF16)
            return carry

        lax.fori_loop(0, rows // 64, convert, 0, unroll=2)
        give_scatter(number)

    def put_narrow(number, row, vector):
        k.send_narrow[number, row : row + 1, :] = vector

    def put_wide(number, row, vectors):
        for j, vector in enumerate(vectors):
            at = STARTS[number] + 4 * row + j
            k.send[at : at + 1, :] = vector

    def put_small(row, vector):
        k.small[row : row + 1, :] = vector

    def narrow(row):
        return k.total[row : row + 1, :]

    def wide(row):
        return jnp.concatenate([k.total[4 * row + j : 4 * row + j + 1, :] for j in range(4)], axis=1)

    def reduced(values):
        return jnp.sum(values, axis=0, keepdims=True)

    def gain_narrow(row):
        return k.gains[row : row + 1, :]

    def gain_wide(row):
        return jnp.concatenate([k.gains[row + j : row + j + 1, :] for j in range(4)], axis=1)

    def put_coef(layer, what, vector):
        row = 8 * layer + what
        k.coef[row : row + 1, 0 : vector.shape[1]] = vector

    def lanes(j):
        return slice(j * LANES, (j + 1) * LANES)

    def get_coef(layer, what, j=0):
        row = 8 * layer + what
        return k.coef[row : row + 1, lanes(j)]

    def finish(layer, sums, squares, gain, bias, count_inverse):
        mean = sums * count_inverse
        inverse = lax.rsqrt(squares * count_inverse - mean * mean + EPSILON)
        scale = inverse * gain
        put_coef(layer, INVERSE, inverse)
        put_coef(layer, NEG_MEAN, -mean * inverse)
        put_coef(layer, HALF_SCALE, 0.5 * scale)
        put_coef(layer, HALF_SHIFT, 0.5 * (bias - mean * scale))

    def normed_sum(layer, sums, products, j=0):
        return products * get_coef(layer, INVERSE, j) + sums * get_coef(layer, NEG_MEAN, j)

    def finish_back(layer, sums, dots, gain, count_inverse):
        width = sums.shape[1]
        row = 8 * layer
        inverse = k.coef[row + INVERSE : row + INVERSE + 1, 0:width]
        scale = inverse * gain
        slant = scale * dots * count_inverse
        put_coef(layer, GRAD_A, scale)
        put_coef(layer, GRAD_E, slant * inverse)
        put_coef(
            layer,
            GRAD_D,
            scale * sums * count_inverse
            + slant * k.coef[row + NEG_MEAN : row + NEG_MEAN + 1, 0:width],
        )

    def put_late(stores):
        for ref, at, value in stores:
            ref[at] = value

    def each_part(body, carry=0, parts=1):
        def step(i, inner):
            stores = []
            for u in range(parts):
                inner, found = body(pl.multiple_of((i * parts + u) * part, 16), inner)
                stores = stores + found
            put_late(stores)
            return inner

        return lax.fori_loop(0, 25 // parts, step, carry)

    def each_chunk(body, carry=0):
        def step(i, inner):
            return body(pl.multiple_of(i * chunk, 16), inner)

        return lax.fori_loop(0, 5, step, carry, unroll=UNROLL)

    def each_block(body):
        def step(i, carry):
            stores = []
            for u in range(per):
                number = i * per + u
                stores = stores + body(number, pl.multiple_of(number * BLOCK, 16))
            put_late(stores)
            return carry

        lax.fori_loop(0, blocks // per, step, 0, unroll=UNROLL)

    def zeros(width=MID):
        return jnp.zeros((8, width), F32)

    def live_rows(start, rows):
        return lax.broadcasted_iota(jnp.int32, (rows, LANES), 0) + start < rows_live

    def near_rows(rows, number):
        return lax.broadcasted_iota(jnp.int32, (rows, LANES), 0) < number

    def live_block(width):
        return jnp.broadcast_to(jnp.where(width > 0, 1.0, 0.0), (BLOCK, LANES)).astype(BF16)

    def at_block(buffer, j, start, rows):
        return buffer[pl.ds(j * out_rows + start, rows), :]

    def wide_store(buffer, start, values):
        rows = values.shape[0]
        for j in range(4):
            buffer[pl.ds(j * out_rows + start, rows), :] = values[:, lanes(j)]

    def added(carry, values):
        return carry[0] + folded(values), carry[1] + folded(values * values)

    def product_sums(left, right, store, masked=False):
        width = right.shape[1]

        def body(start, carry):
            values = dense(left[pl.ds(start, chunk), :], right[...])
            store(start, values)
            if masked:
                values = jnp.where(live_rows(start, chunk), values, 0.0)
            return added(carry, values)

        return each_chunk(body, (zeros(width), zeros(width)))

    def store_narrow(target):
        def store(start, values):
            target[pl.ds(start, values.shape[0]), :] = values

        return store

    def send_narrow(number, sums):
        put_narrow(number, 0, reduced(sums[0]))
        put_narrow(number, 1, reduced(sums[1]))
        share(number)

    def by_lanes(vector):
        return [vector[:, lanes(j)] for j in range(4)]

    def stage_section(section):
        def step(i, carry):
            start = pl.multiple_of(i * (ROWS // 7), 16)
            wst[pl.ds(start, ROWS // 7), :] = wts[section, pl.ds(start, ROWS // 7), :].astype(F32)
            return carry

        lax.fori_loop(0, 7, step, 0)

    def unpack_wide(at, rows, target):
        for j in range(4):
            for r in range(rows // LANES):
                piece = wst[pl.ds(at + 4 * LANES * r + j, LANES, stride=4), :]
                target[r * LANES : (r + 1) * LANES, lanes(j)] = piece.astype(BF16)

    def take_gain(row, at, rows=1):
        k.gains[row : row + rows, :] = wst[at : at + rows, :]

    def turned(piece):
        return piece.astype(BF16).T

    to_rows(EARLY, ROW)
    weight_copies = weight_copies + send_weights(1)
    for copy in feat_copies:
        copy.wait()

    need_weights(0, 0)
    def open_first(step, carry):
        start = pl.multiple_of(step * chunk, 16)
        values = dense(feat[pl.ds(start, chunk), :], wts[0, 0:CIN, :])
        t1[pl.ds(start, chunk), :] = values
        rows = lax.broadcasted_iota(jnp.int32, values.shape, 0) + start
        return added(carry, jnp.where(rows < 4 * rows_live, values, 0.0))

    sums = lax.fori_loop(0, in_rows // chunk, open_first, (zeros(), zeros()), unroll=UNROLL)
    send_narrow(0, sums)

    tab_copy.wait()
    src[0:PAD, :] = jnp.zeros((PAD, LANES), F32)
    src[PAD + out_rows : plane, :] = jnp.zeros((PAD, LANES), F32)
    for number in range(4):
        big0[number * plane : number * plane + PAD, :] = jnp.zeros((PAD, LANES), F32)

    def make_masks(number, start):
        width, local = tab[0, number], tab[1, number]
        pixel = lax.broadcasted_iota(jnp.int32, (BLOCK, LANES), 0).astype(F32) + local.astype(F32)
        side = jnp.maximum(width, 1).astype(F32)
        row = jnp.floor((pixel + 0.5) / side)
        column = pixel - row * side
        one = jnp.where(width > 0, 1.0, 0.0)
        found = (row > 0.5, row < side - 1.5, column > 0.5, column < side - 1.5)
        return [
            (
                masks,
                (which, pl.ds(start, BLOCK), slice(None)),
                jnp.where(condition, one, 0.0).astype(BF16),
            )
            for which, condition in enumerate(found)
        ]

    each_block(make_masks)
    window_rows = AHEAD + 4 * part

    def shortcut_pixels(i, carry):
        for piece in range(5):
            step = i * 5 + piece
            at = (piece % 2) * 2 * window_rows
            low = pl.multiple_of(jnp.maximum(step * 4 * part - AHEAD, 0), 16)
            for half in range(2):
                gn[at + half * window_rows : at + (half + 1) * window_rows, :] = feat[
                    pl.ds(low, window_rows), lanes(half)
                ].astype(F32)
            stores = []
            for u in range(per):
                number = step * per + u
                start = pl.multiple_of(number * BLOCK, 16)
                first = tab[12, number]
                second = first + tab[4, number]
                near = near_rows(BLOCK, tab[3, number])
                one = jnp.where(tab[0, number] > 0, 1.0, 0.0)
                for half in range(2):
                    base = at + half * window_rows
                    picked = jnp.where(
                        near,
                        gn[pl.ds(base + first, BLOCK, stride=2), :],
                        gn[pl.ds(base + second, BLOCK, stride=2), :],
                    )
                    stores.append(
                        (k.xs, (pl.ds(start, BLOCK), lanes(half)), (picked * one).astype(BF16))
                    )
            put_late(stores)
        return carry

    lax.fori_loop(0, 5, shortcut_pixels, 0)

    need_weights(1, 0)
    stage_section(0)
    take_gain(0, IN_GAIN, 2)
    take_gain(2, MID_GAIN, 2)
    k.wmid1[...] = wst[MID_AT : MID_AT + 9 * MID, :].astype(BF16)

    def first_products(block):
        rows = slice(block * out_rows, (block + 1) * out_rows)
        live = (
            lax.broadcasted_iota(jnp.int32, (out_rows, MID), 0) + block * out_rows < 4 * rows_live
        )
        k.turn[0:LANES, :] = turned(jnp.where(live, t1[rows, :], 0.0))
        live = lax.broadcasted_iota(jnp.int32, (16, out_rows), 1) + block * out_rows < 4 * rows_live
        k.turn[LANES : LANES + 16, :] = jnp.where(live, 1.0, 0.0).astype(BF16)
        found = dense(k.turn[...], feat[rows, :])
        for half in range(2):
            at = slice(half * LANES, (half + 1) * LANES)
            product = found[0:LANES, lanes(half)].T
            total = jnp.broadcast_to(found[LANES : LANES + 1, lanes(half)], (LANES, LANES)).T
            k.first_t[at, :] = product if block == 0 else k.first_t[at, :] + product
            k.first_s[at, :] = total if block == 0 else k.first_s[at, :] + total

    collect(0)
    finish(L1, narrow(0), narrow(1), gain_narrow(0), gain_narrow(1), 0.25 * inverse_count)

    def first_hidden(number, start):
        scale, shift = get_coef(L1, HALF_SCALE), get_coef(L1, HALF_SHIFT)
        near = near_rows(BLOCK, tab[3, number])
        stores = []
        for row in range(2):
            for column in range(2):
                first = tab[2, number] + column + (tab[6, number] if row else 0)
                values = jnp.where(
                    near,
                    t1[pl.ds(first, BLOCK, stride=2), :],
                    t1[pl.ds(first + tab[4, number], BLOCK, stride=2), :],
                )
                at = pl.ds((2 * row + column) * plane + PAD + start, BLOCK)
                stores.append((big0, (at, slice(None)), silu_half(values * scale + shift)))
        return stores

    each_block(first_hidden)

    def wide_columns(number, start):
        width = tab[0, number]
        here = pl.ds(start, BLOCK)
        top, left, live = masks[0, here, :], masks[2, here, :], live_block(width)
        corner = top * left
        stores = []
        for tap in range(9):
            i, j = tap // 3, tap % 3
            at = (2 * (0 if i == 1 else 1) + (0 if j == 1 else 1)) * plane + PAD + start
            at = at - (width if i == 0 else 0) - (1 if j == 0 else 0)
            mask = (corner if j == 0 else top) if i == 0 else (left if j == 0 else live)
            values = big0[pl.ds(at, BLOCK), :].astype(BF16) * mask
            stores.append((k.cols1, (here, lanes(tap)), values))
        return stores

    each_block(wide_columns)
    send_narrow(1, product_sums(k.cols1, k.wmid1, store_narrow(k.t2)))

    bank_copies[0].start()
    need_weights(0, 1)
    need_weights(1, 1)
    stage_section(1)
    take_gain(8, OUT_GAIN, 8)
    take_gain(16, SHORT_GAIN, 8)
    unpack_wide(0, MID, k.wout2)
    unpack_wide(AFTER_OUT, CIN, k.wshort)
    short_sums = product_sums(k.xs, k.wshort, functools.partial(wide_store, big2))
    put_wide(2, 2, by_lanes(reduced(short_sums[0])))
    put_wide(2, 3, by_lanes(reduced(short_sums[1])))

    def close_narrow(layer, source, target):
        def body(start, carry):
            half = source[pl.ds(start, part), :] * get_coef(layer, HALF_SCALE) + get_coef(
                layer, HALF_SHIFT
            )
            values = jnp.where(live_rows(start, part), silu_half(half), 0.0).astype(BF16)
            return carry, [(target, (pl.ds(start, part), slice(None)), values)]

        each_part(body, parts=5)

    first_products(0)
    collect(1)
    finish(L2, narrow(0), narrow(1), gain_narrow(2), gain_narrow(3), inverse_count)
    close_narrow(L2, k.t2, k.h2)

    roomy = hasattr(k, "slope23")

    def worked_slope(layer, values):
        return slope_half(values * get_coef(layer, HALF_SCALE) + get_coef(layer, HALF_SHIFT))

    def keep_narrow_slope(layer, source, target):
        def body(start, carry):
            here = pl.ds(start, part)
            values = worked_slope(layer, source[here, :]).astype(BF16)
            return carry, [(target, (here, slice(None)), values)]

        each_part(body, parts=5)

    def second_slope(j, start):
        if roomy:
            return k.slope23[pl.ds(start, part), lanes(j)].astype(F32)
        return slope_half(second_half(j, start))

    def keep_second_slope():
        def body(start, carry):
            return carry, [
                (
                    k.slope23,
                    (pl.ds(start, part), lanes(j)),
                    slope_half(second_half(j, start)).astype(BF16),
                )
                for j in range(4)
            ]

        if roomy:
            each_part(body)

    def keep_first_slope():
        def body(start, carry):
            return carry, [
                (
                    k.cols2,
                    (pl.ds(start, part), lanes(block)),
                    worked_slope(L1, t1[pl.ds(block * out_rows + start, part), :]).astype(BF16),
                )
                for block in range(4)
            ]

        each_part(body)

    sums = product_sums(k.h2, k.wout2, functools.partial(wide_store, big1))
    put_wide(2, 0, by_lanes(reduced(sums[0])))
    put_wide(2, 1, by_lanes(reduced(sums[1])))
    share(2)

    def bank_to_bf16(half):
        bank_copies[half].wait()

        def body(i, carry):
            start = pl.multiple_of(i * 128, 128)
            for j in range(2):
                wide2[pl.ds(start, 128), lanes(2 * half + j)] = big0[
                    pl.ds(j * (BANK // 4) + start, 128), :
                ].astype(BF16)
            return carry

        lax.fori_loop(0, BANK // 4 // 128, body, 0, unroll=4)

    need_weights(0, 2)
    need_weights(1, 2)
    stage_section(2)
    take_gain(4, THIRD_GAIN, 2)
    take_gain(6, THIRD_MID_GAIN, 2)
    k.wmid3[...] = wst[THIRD_MID : THIRD_MID + 9 * MID, :].astype(BF16)
    bank_to_bf16(0)
    bank_copies[1].start()
    first_products(1)
    collect(2)
    finish(L3, wide(0), wide(1), gain_wide(8), gain_wide(12), inverse_count)
    finish(LS, wide(2), wide(3), gain_wide(16), gain_wide(20), inverse_count)

    def second_half(j, start):
        return (
            at_block(big1, j, start, part) * get_coef(L3, HALF_SCALE, j)
            + at_block(big2, j, start, part) * get_coef(LS, HALF_SCALE, j)
            + (get_coef(L3, HALF_SHIFT, j) + get_coef(LS, HALF_SHIFT, j))
        )

    def close_second(start, carry):
        stores = []
        for j in range(4):
            values = silu_half(second_half(j, start)).astype(BF16)
            stores.append((k.y, (pl.ds(start, part), lanes(j)), values))
        return carry, stores

    each_part(close_second)

    send_narrow(3, product_sums(k.y, wts.at[2, pl.ds(0, COUT)], store_narrow(k.t4), True))
    need_weights(0, 3)
    need_weights(1, 3)
    stage_section(3)
    take_gain(24, OUT_GAIN, 8)
    unpack_wide(0, MID, k.wout4)
    bank_to_bf16(1)
    keep_second_slope()
    collect(3)
    finish(L4, narrow(0), narrow(1), gain_narrow(4), gain_narrow(5), inverse_count)

    def third_hidden(start, carry):
        half = k.t4[pl.ds(start, part), :] * get_coef(L4, HALF_SCALE) + get_coef(L4, HALF_SHIFT)
        return carry, [(src, (pl.ds(PAD + start, part), slice(None)), silu_half(half))]

    each_part(third_hidden, parts=5)

    def near_columns(number, start, target, target_start):
        width = tab[0, number]
        here = pl.ds(start, BLOCK)
        top, bottom, left, right = (masks[which, here, :] for which in range(4))
        live = live_block(width)
        stores = []
        for tap in range(9):
            i, j = tap // 3, tap % 3
            at = PAD + start + (i - 1) * width + (j - 1)
            mask = (top, live, bottom)[i]
            if j != 1:
                beside = left if j == 0 else right
                mask = beside if i == 1 else mask * beside
            values = src[pl.ds(at, BLOCK), :].astype(BF16) * mask
            stores.append((target, (pl.ds(target_start, BLOCK), lanes(tap)), values))
        return stores

    each_block(lambda number, start: near_columns(number, start, k.cols2, start))
    send_narrow(4, product_sums(k.cols2, k.wmid3, store_narrow(k.t5)))

    neg_copy.wait()
    gn[0 : 8 * LANES, :] = jnp.zeros((8 * LANES, LANES), F32)
    neg_piece = 512
    for slot in range(slots):

        def count(i, carry, slot=slot):
            at = pl.multiple_of(i * neg_piece, neg_piece)
            found = k.neg[slot, pl.ds(stage, 1), pl.ds(at, neg_piece)]
            spot = lax.broadcasted_iota(jnp.int32, (LANES, neg_piece), 0)
            upper = lax.shift_right_logical(found, 7)
            high = jnp.where(spot == upper, 1.0, 0.0).astype(BF16)
            low = jnp.where(spot == found - LANES * upper, 1.0, 0.0).astype(BF16)
            return carry + across(high, low)

        found = lax.fori_loop(
            0, NEG // neg_piece, count, jnp.zeros((LANES, LANES), F32), unroll=True
        )
        gn[pl.ds(slot, LANES, stride=8), :] = found
    first_products(2)
    collect(4)
    finish(L5, narrow(0), narrow(1), gain_narrow(6), gain_narrow(7), inverse_count)
    close_narrow(L5, k.t5, k.h4)

    sums = product_sums(k.h4, k.wout4, functools.partial(wide_store, big0))
    put_wide(5, 0, by_lanes(reduced(sums[0])))
    put_wide(5, 1, by_lanes(reduced(sums[1])))
    share(5)
    for j in range(4):
        k.wout4_t[j * LANES : (j + 1) * LANES, :] = turned(k.wout4[:, lanes(j)])
    for tap in range(9):
        k.wmid3_t[(8 - tap) * MID : (9 - tap) * MID, :] = turned(
            k.wmid3[tap * MID : (tap + 1) * MID, :]
        )
    for r in range(4):
        k.win3_t[:, lanes(r)] = turned(wts[2, r * LANES : (r + 1) * LANES, :])
    keep_narrow_slope(L5, k.t5, k.dtn)
    first_products(3)
    collect(5)
    finish(L6, wide(0), wide(1), gain_wide(24), gain_wide(28), inverse_count)

    def last_half(j, start):
        return (
            at_block(big0, j, start, part) * get_coef(L6, HALF_SCALE, j)
            + get_coef(L6, HALF_SHIFT, j)
            + 0.5 * k.y[pl.ds(start, part), lanes(j)].astype(F32)
        )

    def close_last(start, carry):
        return carry, [
            (gw, (pl.ds(start, part), lanes(j)), silu_half(last_half(j, start)).astype(BF16))
            for j in range(4)
        ]

    each_part(close_last)

    def pool(start, carry):
        rows = lax.broadcasted_iota(jnp.int32, (8, chunk), 1) + start
        owner = jnp.zeros((8, chunk), jnp.int32)
        for end in ends:
            owner = owner + jnp.where(rows >= end, 1, 0)
        mine = owner == lax.broadcasted_iota(jnp.int32, (8, chunk), 0)
        mine = jnp.where(mine, 1.0, 0.0).astype(BF16)
        return carry + dense(mine, gw[pl.ds(start, chunk), :])

    slot_row = lax.broadcasted_iota(jnp.int32, (8, LANES), 0)
    area = jnp.zeros((8, LANES), jnp.int32)
    positive = jnp.full((8, LANES), -1, jnp.int32)
    for slot in range(slots):
        area = jnp.where(slot_row == slot, sides[slot] * sides[slot], area)
        positive = jnp.where(slot_row == slot, k.positives[0, stage, slot], positive)
    inverse_area = jnp.where(area > 0, 1.0 / jnp.maximum(area, 1).astype(F32), 0.0)
    inverse_area_wide = jnp.concatenate([inverse_area] * 4, axis=1)
    half_offset = 0.5 * jnp.log(jnp.full((8, LANES), k.normalizer[0] * NEG / BANK))
    pooled = each_chunk(pool, zeros(COUT)) * inverse_area_wide

    head = wst[AFTER_OUT : AFTER_OUT + COUT, :].astype(BF16)
    pooled_high, pooled_low = split(pooled)
    embed = dense(pooled_high, head) + dense(pooled_low, head)
    scale = lax.rsqrt(jnp.sum(embed * embed, axis=1, keepdims=True) + 1e-06)
    unit = embed * scale
    unit_parts = jnp.concatenate(split(unit), axis=0)
    lane = lax.broadcasted_iota(jnp.int32, (8, LANES), 1)
    parts = []
    for block in range(4):
        scores = across(unit_parts, wide2[:, lanes(block)])
        scores = scores[0:8, :] + scores[8:16, :]
        pieces = []
        for j in range(BANK // 4 // LANES):
            high = block * (BANK // 4 // LANES) + j
            half = scores[:, lanes(j)] * (0.5 / SOFTMAX_TEMPER) - half_offset
            sigma = 0.5 + 0.5 * jnp.tanh(half)
            chosen = jnp.where(positive == lane + high * LANES, 1.0, 0.0)
            pieces.append((gn[high * 8 : high * 8 + 8, :] + chosen) * sigma - chosen)
        parts = parts + list(split(jnp.concatenate(pieces, axis=1)))
    found = dense(jnp.concatenate(parts, axis=0), wide2[...])
    unit_grad = zeros(EMB)
    for block in range(4):
        for row in (16 * block, 16 * block + 8):
            unit_grad = unit_grad + found[row : row + 8, lanes(block)]
    unit_grad = jnp.where(inverse_area > 0.0, unit_grad, 0.0) * (1.0 / SOFTMAX_TEMPER)
    embed_grad = scale * unit_grad - embed * (
        scale * scale * scale * jnp.sum(embed * unit_grad, axis=1, keepdims=True)
    )
    grad_high, grad_low = split(embed_grad)
    pooled_grad = across(grad_high, head) + across(grad_low, head)
    pooled_grad = pooled_grad * inverse_area_wide
    for j in range(4):
        k.spread[8 * j : 8 * j + 8, :] = pooled_grad[:, lanes(j)]

    def last_slope(step, carry):
        start = pl.multiple_of(step * part, 16)
        owners = [tab[5, step * per + u] for u in range(per)]
        found, stores = [], []
        for j in range(4):
            upstream = jnp.concatenate(
                [
                    jnp.broadcast_to(k.spread[pl.ds(8 * j + owner, 1), :], (BLOCK, LANES))
                    for owner in owners
                ],
                axis=0,
            )
            upstream = upstream * slope_half(last_half(j, start))
            stores.append((gw, (pl.ds(start, part), lanes(j)), upstream.astype(BF16)))
            found.append(
                (
                    carry[j][0] + folded(upstream),
                    carry[j][1] + folded(upstream * at_block(big0, j, start, part)),
                )
            )
        put_late(stores)
        return tuple(found)

    pair = (zeros(), zeros())
    sums = lax.fori_loop(0, 25, last_slope, (pair,) * 4)
    bias_grads = [reduced(sums[j][0]) for j in range(4)]
    gain_grads = [normed_sum(L6, bias_grads[j], reduced(sums[j][1]), j) for j in range(4)]
    put_wide(6, 0, bias_grads)
    put_wide(6, 1, gain_grads)
    share(6)
    for j in range(4):
        wst[OUT_GAIN + j : OUT_GAIN + j + 1, :] = gain_grads[j]
        wst[OUT_BIAS + j : OUT_BIAS + j + 1, :] = bias_grads[j]
    wst[AFTER_OUT : AFTER_OUT + COUT, :] = (
        outer(pooled_high, grad_high) + outer(pooled_high, grad_low) + outer(pooled_low, grad_high)
    )
    for j in range(4):
        k.wout2_t[j * LANES : (j + 1) * LANES, :] = turned(k.wout2[:, lanes(j)])
        for r in range(2):
            k.wshort_t[j * LANES : (j + 1) * LANES, lanes(r)] = turned(
                k.wshort[r * LANES : (r + 1) * LANES, lanes(j)]
            )
    def put_turned(source, target, values):
        at = (target // 2) * 4 * MID + source * MID
        k.wmid1_t[at : at + MID, lanes(target % 2)] = values

    for tap in range(9):
        i, j = tap // 3, tap % 3
        source = 2 * (1 if i == 0 else 0) + (1 if j == 0 else 0)
        target = 2 * (0 if i == 1 else 1) + (0 if j == 1 else 1)
        put_turned(source, target, turned(k.wmid1[tap * MID : (tap + 1) * MID, :]))
    for source in range(4):
        for target in range(4):
            if source & target != source:
                put_turned(source, target, jnp.zeros((MID, MID), BF16))
    collect(6)
    finish_back(L6, wide(0), wide(1), gain_wide(24), inverse_count)

    def back_value(layer, upstream, values, j=0):
        return (
            upstream * get_coef(layer, GRAD_A, j)
            - values * get_coef(layer, GRAD_E, j)
            - get_coef(layer, GRAD_D, j)
        )

    def back_sixth(start, carry):
        here = pl.ds(start, part)
        stores = []
        for j in range(4):
            values = back_value(
                L6, gw[here, lanes(j)].astype(F32), at_block(big0, j, start, part), j
            )
            stores.append((wide2, (here, lanes(j)), values.astype(BF16)))
        return carry, stores

    each_part(back_sixth)

    def back_rows(values, slope):
        def body(start, carry):
            here = pl.ds(start, part)
            upstream = gn[here, :] * slope[here, :].astype(F32)
            upstream = jnp.where(live_rows(start, part), upstream, 0.0)
            carry = (carry[0] + folded(upstream), carry[1] + folded(upstream * values[here, :]))
            return carry, [(gn, (here, slice(None)), upstream)]

        return each_part(body, (zeros(), zeros()), parts=5)

    def send_back(number, row, layer, sums):
        bias_grad = reduced(sums[0])
        gain_grad = normed_sum(layer, bias_grad, reduced(sums[1]))
        put_narrow(number, 0, bias_grad)
        put_narrow(number, 1, gain_grad)
        share(number)
        put_small(row, gain_grad)
        put_small(row + 1, bias_grad)

    def rounded_product(left, right):
        def body(start, carry):
            here = pl.ds(start, chunk)
            gn[here, :] = dense(left[here, :], right[...]).astype(BF16).astype(F32)
            return carry

        each_chunk(body)

    rounded_product(wide2, k.wout4_t)
    send_back(7, 2, L5, back_rows(k.t5, k.dtn))

    def put_wide_matrix(at, values):
        for r in range(values.shape[0] // LANES):
            for j in range(4):
                wst[pl.ds(at + 4 * LANES * r + j, LANES, stride=4), :] = values[
                    r * LANES : (r + 1) * LANES, lanes(j)
                ]

    def turned_rows(ref, lane=0):
        return turned(ref[:, lane * LANES : (lane + 1) * LANES])

    k.turn[0:LANES, :] = turned_rows(k.h4)
    put_wide_matrix(0, dense(k.turn[0:LANES, :], wide2[0:out_rows, :]))
    stage_piece(LAST)
    keep_narrow_slope(L4, k.t4, k.h4)
    collect(7)
    finish_back(L5, narrow(0), narrow(1), gain_narrow(6), inverse_count)

    def back_close(layer, values):
        def body(start, carry):
            here = pl.ds(start, part)
            found = back_value(layer, gn[here, :], values[here, :])
            found = jnp.where(live_rows(start, part), found, 0.0).astype(BF16)
            return carry, [
                (k.dtn, (here, slice(None)), found),
                (src, (pl.ds(PAD + start, part), slice(None)), found.astype(F32)),
            ]

        each_part(body, parts=5)

    back_close(L5, k.t5)

    def open_back_fourth(step, carry):
        chunk_start = pl.multiple_of(step * chunk, 16)

        def fill(i, inner):
            stores = []
            for u in range(per):
                at = pl.multiple_of((i * per + u) * BLOCK, 16)
                number = step * (chunk // BLOCK) + i * per + u
                stores = stores + near_columns(number, chunk_start + at, k.colt, at)
            put_late(stores)
            return inner

        lax.fori_loop(0, chunk // BLOCK // per, fill, 0, unroll=UNROLL)
        gn[pl.ds(chunk_start, chunk), :] = dense(k.colt[...], k.wmid3_t[...])
        return carry

    lax.fori_loop(0, 5, open_back_fourth, 0, unroll=UNROLL)
    send_back(8, 0, L4, back_rows(k.t4, k.h4))

    def columns_grad(columns, store):
        k.turn[0:LANES, :] = turned_rows(k.dtn)
        for group in range(3):
            found = dense(k.turn[0:LANES, :], columns[:, 3 * group * LANES : 3 * (group + 1) * LANES])
            for j in range(3):
                store(3 * group + j, found[:, lanes(j)].T)

    def store_third(tap, values):
        wst[THIRD_MID + tap * MID : THIRD_MID + (tap + 1) * MID, :] = values

    columns_grad(k.cols2, store_third)
    give_line(LAST)
    keep_narrow_slope(L2, k.t2, k.h4)
    collect(8)
    finish_back(L4, narrow(0), narrow(1), gain_narrow(4), inverse_count)
    back_close(L4, k.t4)

    def back_block(start, carry):
        here = pl.ds(start, part)
        arrived = dense(k.dtn[here, :], k.win3_t[...])
        found, stores = [], []
        for j in range(4):
            upstream = arrived[:, lanes(j)] + gw[here, lanes(j)].astype(F32)
            upstream = upstream.astype(BF16).astype(F32) * second_slope(j, start)
            stores.append((gw, (here, lanes(j)), upstream.astype(BF16)))
            found.append(
                (
                    carry[j][0] + folded(upstream),
                    carry[j][1] + folded(upstream * at_block(big1, j, start, part)),
                    carry[j][2] + folded(upstream * at_block(big2, j, start, part)),
                )
            )
        return tuple(found), stores

    sums = each_part(back_block, ((zeros(), zeros(), zeros()),) * 4)
    bias_grads, gain_grads, short_grads = (
        [reduced(sums[j][which]) for j in range(4)] for which in range(3)
    )
    gain_grads = [normed_sum(L3, bias_grads[j], gain_grads[j], j) for j in range(4)]
    short_grads = [normed_sum(LS, bias_grads[j], short_grads[j], j) for j in range(4)]
    put_wide(9, 0, bias_grads)
    put_wide(9, 1, gain_grads)
    put_wide(9, 2, short_grads)
    share(9)
    k.turn[0:LANES, :] = turned_rows(k.dtn)
    found = dense(k.turn[0:LANES, :], k.y[...])
    for j in range(4):
        wst[j * LANES : (j + 1) * LANES, :] = found[:, lanes(j)].T
    wst[THIRD_GAIN : THIRD_BIAS + 1, :] = k.small[0:2, :]
    wst[THIRD_MID_GAIN : THIRD_MID_BIAS + 1, :] = k.small[2:4, :]
    stage_piece(THIRD)
    give_home(LAST)
    keep_first_slope()
    collect(9)
    finish_back(L3, wide(0), wide(1), gain_wide(8), inverse_count)
    finish_back(LS, wide(0), wide(2), gain_wide(16), inverse_count)

    def back_third(start, carry):
        here = pl.ds(start, part)
        below = pl.ds(out_rows + start, part)
        stores = []
        for j in range(4):
            upstream = gw[here, lanes(j)].astype(F32)
            found = back_value(L3, upstream, at_block(big1, j, start, part), j)
            stores.append((wide2, (here, lanes(j)), found.astype(BF16)))
            found = back_value(LS, upstream, at_block(big2, j, start, part), j)
            stores.append((wide2, (below, lanes(j)), found.astype(BF16)))
        return carry, stores

    each_part(back_third)
    rounded_product(wide2, k.wout2_t)
    send_back(10, 6, L2, back_rows(k.t2, k.h4))
    for j in range(4):
        wst[OUT_GAIN + j : OUT_GAIN + j + 1, :] = gain_grads[j]
        wst[OUT_BIAS + j : OUT_BIAS + j + 1, :] = bias_grads[j]
        wst[SHORT_GAIN + j : SHORT_GAIN + j + 1, :] = short_grads[j]
        wst[SHORT_BIAS + j : SHORT_BIAS + j + 1, :] = bias_grads[j]
    k.turn[0:LANES, :] = turned_rows(k.h2)
    put_wide_matrix(0, dense(k.turn[0:LANES, :], wide2[0:out_rows, :]))
    for half in range(2):
        k.turn[0:LANES, :] = turned_rows(k.xs, half)
        put_wide_matrix(
            AFTER_OUT + half * 4 * LANES, dense(k.turn[0:LANES, :], wide2[out_rows : 2 * out_rows, :])
        )
    stage_piece(SECOND)
    give_line(THIRD)

    collect(10)
    finish_back(L2, narrow(0), narrow(1), gain_narrow(2), inverse_count)
    back_close(L2, k.t2)


    def back_columns(number, start):
        here = pl.ds(start, BLOCK)
        width = tab[0, number]
        bottom, right, live = masks[1, here, :], masks[3, here, :], live_block(width)
        shifts = ((0, live), (1, right), (width, bottom), (width + 1, bottom * right))
        return [
            (
                wide2,
                (here, lanes(which)),
                src[pl.ds(PAD + start + shift, BLOCK), :].astype(BF16) * mask,
            )
            for which, (shift, mask) in enumerate(shifts)
        ]

    each_block(back_columns)

    def back_planes(start, carry):
        here = pl.ds(start, chunk)
        even = dense(wide2[here, 0 : 2 * MID], k.wmid1_t[0 : 2 * MID, :])
        odd = dense(wide2[here, :], k.wmid1_t[4 * MID : 8 * MID, :])
        for number in range(4):
            found = (even, odd)[number // 2][:, lanes(number % 2)]
            big0[pl.ds(number * plane + PAD + start, chunk), :] = found
        return carry

    each_chunk(back_planes)

    in_unroll = 10

    def to_input_order(i, carry):
        stores = []
        for u in range(in_unroll):
            number = i * in_unroll + u
            first, second = tab[7, number], tab[8, number]
            near = near_rows(8, tab[9, number])
            for column in range(2):
                values = jnp.where(
                    near,
                    big0[pl.ds(first + column * plane, 8), :],
                    big0[pl.ds(second + column * plane, 8), :],
                )
                at = pl.ds(number * BLOCK + column, 8, stride=2)
                stores.append((big1, (at, slice(None)), values))
        put_late(stores)
        return carry

    lax.fori_loop(0, in_rows // BLOCK // in_unroll, to_input_order, 0, unroll=UNROLL)

    def back_first(start, carry):
        stores = []
        for block in range(4):
            rows = pl.ds(block * out_rows + start, part)
            upstream = big1[rows, :] * k.cols2[pl.ds(start, part), lanes(block)].astype(F32)
            carry = (carry[0] + folded(upstream), carry[1] + folded(upstream * t1[rows, :]))
            stores.append((big1, (rows, slice(None)), upstream))
        return carry, stores

    sums = each_part(back_first, (zeros(), zeros()))
    send_back(11, 4, L1, sums)
    def store_first(tap, values):
        at = piece_at[FIRST_MID] + tap * MID
        k.gb[at : at + MID, :] = values.astype(BF16)

    columns_grad(k.cols1, store_first)
    if padded[FIRST_MID] > 9 * MID:
        at = piece_at[FIRST_MID]
        k.gb[at + 9 * MID : at + padded[FIRST_MID], :] = jnp.zeros(
            (padded[FIRST_MID] - 9 * MID, LANES), BF16
        )
    give_scatter(FIRST_MID)
    give_line(SECOND)
    give_home(THIRD)

    found = jnp.zeros((MID, CIN), F32)
    for block in range(4):
        rows = slice(block * out_rows, (block + 1) * out_rows)
        k.turn[0:LANES, :] = turned(big1[rows, :])
        found = found + dense(k.turn[0:LANES, :], feat[rows, :])
    first_g = [found[:, lanes(half)].T for half in range(2)]
    for half in range(2):
        k.win1_t[:, lanes(half)] = turned(wts[0, half * LANES : (half + 1) * LANES, :])
    gn[...] = jnp.zeros(gn.shape, F32)
    collect(11)
    finish_back(L1, narrow(0), narrow(1), gain_narrow(0), 0.25 * inverse_count)

    at = piece_at[FIRST_IN]
    for half in range(2):
        rows = slice(half * LANES, (half + 1) * LANES)
        values = first_g[half] * get_coef(L1, GRAD_A) - k.first_t[rows, :] * get_coef(L1, GRAD_E)
        values = values - k.first_s[rows, :] * get_coef(L1, GRAD_D)
        k.gb[at + half * LANES : at + (half + 1) * LANES, :] = values.astype(BF16)
    k.gb[at + CIN : at + CIN + 16, :] = jnp.concatenate(
        [k.small[4:8, :], jnp.zeros((12, LANES), F32)], axis=0
    ).astype(BF16)
    k.gb[at + CIN + 16 : at + padded[FIRST_IN], :] = jnp.zeros(
        (padded[FIRST_IN] - CIN - 16, LANES), BF16
    )
    give_scatter(FIRST_IN)
    give_line(FIRST_MID)
    give_home(SECOND)

    for block in range(4):

        def close_back_first(start, carry, block=block):
            rows = pl.ds(block * out_rows + start, part)
            found = back_value(L1, big1[rows, :], t1[rows, :])
            row = lax.broadcasted_iota(jnp.int32, (part, MID), 0) + (block * out_rows + start)
            found = jnp.where(row < 4 * rows_live, found, 0.0).astype(BF16)
            return carry, [(gw, (pl.ds(start, part), lanes(block)), found)]

        each_part(close_back_first, parts=5)

    def back_picked(start, carry):
        found = dense(wide2[pl.ds(out_rows + start, chunk), :], k.wshort_t[...])
        found = found.astype(BF16).astype(F32)
        for half in range(2):
            big2[pl.ds(half * plane + PAD + start, chunk), :] = found[:, lanes(half)]
        return carry

    each_chunk(back_picked)
    for half in range(2):
        big2[half * plane : half * plane + PAD, :] = jnp.zeros((PAD, LANES), F32)
    give_line(FIRST_IN)
    give_home(FIRST_MID)


    def ordered(target, source, rows):
        def body(i, carry):
            start = pl.multiple_of(i * 64, 64)
            wst[pl.ds(target + start, 64), :] = k.got_all[pl.ds(source + start, 64), :].astype(F32)
            return carry

        lax.fori_loop(0, rows // 64, body, 0, unroll=2)

    def blank(at):
        wst[at:ROWS, :] = jnp.zeros((ROWS - at, LANES), F32)

    def input_grad(block, carry):
        lane = pl.ds(pl.multiple_of(block * LANES, LANES), LANES)
        for piece in range(5):
            low = (piece % 2) * 2 * chunk
            stores = []
            for u in range(chunk // BLOCK):
                number = (block * 5 + piece) * (chunk // BLOCK) + u
                near = near_rows(8, tab[9, number])
                for half in range(2):
                    values = jnp.where(
                        near,
                        big2[pl.ds(tab[10, number] + half * plane, 8), :],
                        big2[pl.ds(tab[11, number] + half * plane, 8), :],
                    )
                    at = low + half * chunk + u * BLOCK
                    stores.append((gn, (slice(at, at + BLOCK, 2), slice(None)), values))
            put_late(stores)
            found = dense(gw[piece * chunk : (piece + 1) * chunk, lane], k.win1_t[...])
            rows = pl.ds(pl.multiple_of(block * out_rows + piece * chunk, 16), chunk)
            for half in range(2):
                at = low + half * chunk
                feat[rows, lanes(half)] = (found[:, lanes(half)] + gn[at : at + chunk, :]).astype(
                    BF16
                )
        return carry

    lax.fori_loop(0, 2, input_grad, 0)
    give_home(FIRST_IN)
    take_all(FIRST_MID)

    @pl.when(stage == 0)
    def unused_first_mid():
        blank(MID_BIAS + 1)
        ordered(MID_AT, 0, 9 * MID)

    lax.fori_loop(2, 4, input_grad, 0)
    input_copy = pltpu.make_async_copy(feat, k.input_grad_at, k.out_sem.at[0])
    input_copy.start()

    for number in (LAST, THIRD, SECOND, FIRST_IN):
        take_all(number)

    for number in (LAST, THIRD, SECOND):

        @pl.when(stage == PIECES[number][0])
        def unused_ordered(number=number):
            rows = min(padded[number], ROWS // 128 * 128)
            if rows < ROWS:
                blank(rows)
            ordered(0, 0, rows)
            if rows < PIECES[number][1]:
                tail = k.got_all[rows : rows + 16, :].astype(F32)
                wst[rows : rows + 16, :] = tail

    @pl.when(stage == 0)
    def unused_first():
        at = section_at[FIRST_IN]
        ordered(0, at, CIN)
        gains = k.got_all[at + CIN : at + CIN + 16, :].astype(F32)
        wst[IN_GAIN : IN_BIAS + 1, :] = gains[0:2, :]
        wst[MID_GAIN : MID_BIAS + 1, :] = gains[2:4, :]

    out_copy = pltpu.make_async_copy(wst.at[pl.ds(0, ROWS)], k.weight_grads_at, k.grad_sem)
    out_copy.start()
    input_copy.wait()
    for copy in weight_copies:
        copy.wait_send()
    for number in range(EXCHANGES):
        wait_for(k.stat_send.at[number], incoming(number, pl.ds(0, batches - 1)))
    for number in range(len(PIECES)):
        end_sends(number)
    out_copy.wait()


def write_kernel(weight_rows, input_rows, weight_out, input_out, held_weights, held, sems):
    count = 10
    part = input_rows.shape[0] // count
    pairs = [
        (weight_rows.at[pl.ds(0, ROW)], held_weights, weight_out.reshape(ROW, LANES)),
        *[
            (input_rows.at[rows], held.at[rows], input_out.at[rows])
            for rows in [pl.ds(i * part, part) for i in range(count)]
        ],
    ]
    arriving = [
        pltpu.make_async_copy(source, middle, sems.at[0, i])
        for i, (source, middle, target) in enumerate(pairs)
    ]
    leaving = [
        pltpu.make_async_copy(middle, target, sems.at[1, i])
        for i, (source, middle, target) in enumerate(pairs)
    ]
    for copy in arriving:
        copy.start()
    for i in range(len(pairs)):
        arriving[i].wait()
        leaving[i].start()
    for copy in leaving:
        copy.wait()


def shards(features, weights, crop_kind, positives, negatives, bank, normalizer):
    phases = lax.axis_size("phase")
    batches = lax.axis_size("batch")
    in_rows = features.shape[0] // MICRO
    out_rows = in_rows // 4
    plane = out_rows + 2 * PAD
    slots = crop_kind.shape[2]
    chunk = out_rows // 5
    part = out_rows // 25
    group = 2 * phases
    levels = line_levels(batches // 2)
    padded = [-(-rows // (16 * group)) * 16 * group for unused, rows in PIECES]
    widest = max(*padded[:3], padded[3] + padded[4])
    eighth = sum(padded) // group
    staged = max(ROWS, *padded[:3])
    any_space = pl.BlockSpec(memory_space=pl.ANY)
    smem = pl.BlockSpec(memory_space=pltpu.SMEM)

    def held(*shape, dtype=F32):
        return pltpu.VMEM(shape, dtype)

    def sems(*shape):
        return pltpu.SemaphoreType.DMA(shape)

    def low(*shape):
        return held(*shape, dtype=BF16)

    kept_slopes = {"slope23": low(out_rows, COUT)} if batches <= 8 else {}

    inputs = {
        "features_at": (features, any_space),
        "weights_at": (weights, any_space),
        "negatives_at": (jnp.transpose(negatives, (0, 2, 1, 3)), any_space),
        "bank_at": (bank, any_space),
        "kinds": (jnp.transpose(crop_kind, (2, 1, 0)), smem),
        "positives": (positives, smem),
        "normalizer": (normalizer, smem),
    }
    outputs = {
        "weight_grads_at": jax.ShapeDtypeStruct((ROWS, LANES), F32),
        "input_grad_at": jax.ShapeDtypeStruct((in_rows, CIN), BF16),
    }
    scratch = {
        "feat": low(in_rows, CIN),
        "t1": held(in_rows, MID),
        "big0": held(4 * plane, MID),
        "big1": held(in_rows, MID),
        "big2": held(4 * plane, MID),
        "cols1": low(out_rows, 9 * MID),
        "cols2": low(out_rows, 9 * MID),
        "colt": low(chunk, 9 * MID),
        "src": held(plane, MID),
        "t2": held(out_rows, MID),
        "t4": held(out_rows, MID),
        "t5": held(out_rows, MID),
        "gn": held(out_rows, MID),
        "h2": low(out_rows, MID),
        "h4": low(out_rows, MID),
        "xs": low(out_rows, CIN),
        "y": low(out_rows, COUT),
        "gw": low(out_rows, COUT),
        "wide2": low(BANK // 4, COUT),
        "dtn": low(out_rows, MID),
        "turn": low(LANES + 16, out_rows),
        "first_t": held(CIN, MID),
        "first_s": held(CIN, MID),
        "masks": low(4, out_rows, LANES),
        "raw": low(1, GRAD_LEN),
        "wts": low(phases, ROWS, LANES),
        "wst": held(staged, LANES),
        "wmid1": low(9 * MID, MID),
        "wmid3": low(9 * MID, MID),
        "wout2": low(MID, COUT),
        "wshort": low(CIN, COUT),
        "wout4": low(MID, COUT),
        "wout2_t": low(COUT, MID),
        "wshort_t": low(COUT, CIN),
        "wout4_t": low(COUT, MID),
        "wmid1_t": low(8 * MID, 2 * MID),
        "wmid3_t": low(9 * MID, MID),
        "win1_t": low(MID, CIN),
        "win3_t": low(MID, COUT),
        "gains": held(32, LANES),
        "small": held(8, LANES),
        "coef": held(56, COUT),
        "spread": held(32, LANES),
        "neg": held(slots, MICRO, NEG, dtype=jnp.int32),
        **kept_slopes,
        "tabv": held(16, TABLE, dtype=jnp.int32),
        "tab": pltpu.SMEM((16, TABLE), jnp.int32),
        "send": held(SPAN_ROWS, LANES),
        "send_narrow": held(EXCHANGES, 2, LANES),
        "recv_narrow": held(EXCHANGES, batches, 2, LANES),
        "recv": held(batches, SPAN_ROWS, LANES),
        "total": held(16, LANES),
        "gb": low(sum(padded), LANES),
        "got_scatter": low(group - 1, eighth, LANES),
        "line_sum": low(len(levels), eighth, LANES),
        "got_line": low(sum(levels) - len(levels), eighth, LANES),
        "home": low(eighth, LANES),
        "got_all": low(widest, LANES),
        "raw_sem": pltpu.SemaphoreType.DMA,
        "feat_sem": sems(4),
        "bank_sem": sems(2),
        "neg_sem": pltpu.SemaphoreType.DMA,
        "tab_sem": pltpu.SemaphoreType.DMA,
        "weight_send": sems(2, phases),
        "weight_recv": sems(2, phases),
        "stat_send": sems(EXCHANGES),
        "stat_recv": sems(EXCHANGES),
        "scatter_send": sems(len(PIECES)),
        "scatter_recv": sems(len(PIECES)),
        "line_send": sems(len(levels), len(PIECES)),
        "line_recv": sems(len(levels), len(PIECES)),
        "home_send": sems(len(PIECES)),
        "home_recv": sems(len(PIECES)),
        "out_sem": sems(4),
        "grad_sem": pltpu.SemaphoreType.DMA,
    }
    names = (*inputs, *outputs, *scratch)
    weight_rows, input_rows = pl.pallas_call(
        functools.partial(kernel, names, batches, phases, in_rows, slots),
        out_shape=tuple(outputs.values()),
        in_specs=[spec for unused, spec in inputs.values()],
        out_specs=(any_space,) * len(outputs),
        scratch_shapes=list(scratch.values()),
        compiler_params=pltpu.CompilerParams(
            collective_id=0, has_side_effects=True, vmem_limit_bytes=64 * 1024 * 1024
        ),
    )(*[value for value, unused in inputs.values()])
    weight_grads, input_grad = pl.pallas_call(
        write_kernel,
        out_shape=(
            jax.ShapeDtypeStruct((1, GRAD_LEN), F32),
            jax.ShapeDtypeStruct((in_rows, CIN), BF16),
        ),
        in_specs=[any_space, any_space],
        out_specs=(any_space, any_space),
        scratch_shapes=[held(ROW, LANES), low(in_rows, CIN), sems(2, 11)],
        compiler_params=pltpu.CompilerParams(vmem_limit_bytes=64 * 1024 * 1024),
    )(weight_rows, input_rows)
    return (weight_grads, input_grad)


def solution(mesh):
    placed = (
        P("batch", None),
        P("phase", None),
        P(),
        P("batch", None, None),
        P("batch", None, None, None),
        P(),
        P(),
    )
    return jax.shard_map(
        shards,
        mesh=mesh,
        in_specs=placed,
        out_specs=(P("phase", None), P(("batch", "phase"), None)),
        check_vma=False,
    )
```

```python
import functools
import math
import types

import jax
import jax.numpy as jnp
from jax import lax
from jax.experimental import pallas as pl
from jax.experimental.pallas import tpu as pltpu
from jax.sharding import PartitionSpec as P

CIN = 256
MID = 128
COUT = 512
EMB = 128
SIDE_UNIT = 4
MICRO = 4
NEG = 4096
BANK = 16384
GRAD_LEN = 213504
LANES = 128
SOFTMAX_TEMPER = 0.07
EPSILON = 1e-05

PAD = 40
ROW = GRAD_LEN // LANES
ROWS = -(-ROW // 16) * 16
BLOCK = 16
TABLE = 512
UNROLL = 5
EARLY = 272
AHEAD = 80
MESH = pl.DeviceIdType.MESH
F32 = jnp.float32
BF16 = jnp.bfloat16

IN_GAIN, IN_BIAS, MID_AT = CIN, CIN + 1, CIN + 2
MID_GAIN, MID_BIAS = MID_AT + 9 * MID, MID_AT + 9 * MID + 1
THIRD_GAIN, THIRD_BIAS, THIRD_MID = COUT, COUT + 1, COUT + 2
THIRD_MID_GAIN, THIRD_MID_BIAS = THIRD_MID + 9 * MID, THIRD_MID + 9 * MID + 1
OUT_GAIN, OUT_BIAS, AFTER_OUT = 512, 516, 520
SHORT_GAIN, SHORT_BIAS = AFTER_OUT + 1024, AFTER_OUT + 1028

EXCHANGES = 12
SPANS = {2: 16, 5: 8, 6: 8, 9: 16}
STARTS = {2: 0, 5: 16, 6: 24, 9: 32}
SPAN_ROWS = 48
NARROW = [number for number in range(EXCHANGES) if number not in SPANS]

PIECES = ((3, 1032), (2, 1668), (1, 1552), (0, 9 * MID), (0, 260))
LAST, THIRD, SECOND, FIRST_MID, FIRST_IN = range(5)

L1, L2, L3, LS, L4, L5, L6 = range(7)
HALF_SCALE, HALF_SHIFT, INVERSE, NEG_MEAN, GRAD_A, GRAD_E, GRAD_D = range(7)


def dense(left, right):
    return jnp.dot(left, right, preferred_element_type=F32)


def across(left, right):
    return lax.dot_general(left, right, (((1,), (1,)), ((), ())), preferred_element_type=F32)


def outer(left, right):
    return lax.dot_general(left, right, (((0,), (0,)), ((), ())), preferred_element_type=F32)


def folded(values):
    rows, width = values.shape
    return values.reshape(rows // 8, 8, width).sum(axis=0)


def silu_half(half):
    return half + half * jnp.tanh(half)


def slope_half(half):
    bend = jnp.tanh(half)
    return 0.5 * (1.0 + bend + half * (1.0 - bend * bend))


def split(values):
    high = values.astype(BF16)
    return high, (values - high.astype(F32)).astype(BF16)


def line_levels(lines):
    return [lines] if lines <= 8 else [lines // 8, 8]


def kernel(names, batches, phases, in_rows, slots, *refs):
    k = types.SimpleNamespace(**dict(zip(names, refs, strict=True)))
    out_rows = in_rows // 4
    plane = out_rows + 2 * PAD
    chunk = out_rows // 5
    part = out_rows // 25
    blocks = out_rows // BLOCK
    per = part // BLOCK
    me = lax.axis_index("batch")
    stage = lax.axis_index("phase")
    core = lax.rem(me, 2)
    line = lax.div(me, 2)
    lines = batches // 2
    group = 2 * phases
    mine = 2 * stage + core
    levels = line_levels(lines)
    half_bank = BANK // 2
    quarter = in_rows // 4
    feat, t1, big0, big1, big2, src = k.feat, k.t1, k.big0, k.big1, k.big2, k.src
    tab, masks, wst, wts, gw, wide2, gn = k.tab, k.masks, k.wst, k.wts, k.gw, k.wide2, k.gn

    def batch_peer(i):
        return {"batch": lax.rem(me + i, batches)}

    def phase_peer(i):
        return {"phase": lax.rem(stage + i, phases)}

    def remote(source, target, send_sem, recv_sem, device):
        return pltpu.make_async_remote_copy(
            src_ref=source,
            dst_ref=target,
            send_sem=send_sem,
            recv_sem=recv_sem,
            device_id=device,
            device_id_type=MESH,
        )

    def wait_for(sem, region):
        pltpu.make_async_copy(region, region, sem).wait()

    barrier = pltpu.get_barrier_semaphore()

    def greet(i, carry):
        pl.semaphore_signal(barrier, inc=1, device_id=batch_peer(i), device_id_type=MESH)
        return carry

    lax.fori_loop(1, batches, greet, 0)
    for i in range(1, phases):
        for other in (me, 2 * line + 1 - core):
            pl.semaphore_signal(
                barrier,
                inc=1,
                device_id={"phase": lax.rem(stage + i, phases), "batch": other},
                device_id_type=MESH,
            )

    raw_copy = pltpu.make_async_copy(k.weights_at, k.raw, k.raw_sem)
    raw_copy.start()
    feat_copies = []
    for i in range(4):
        copy = pltpu.make_async_copy(
            k.features_at.at[pl.ds(pl.multiple_of(stage * in_rows + i * quarter, 16), quarter)],
            feat.at[pl.ds(i * quarter, quarter)],
            k.feat_sem.at[i],
        )
        copy.start()
        feat_copies.append(copy)
    neg_copy = pltpu.make_async_copy(k.negatives_at.at[0], k.neg, k.neg_sem)
    neg_copy.start()
    bank_copies = [
        pltpu.make_async_copy(
            k.bank_at.at[pl.ds(i * half_bank, half_bank)],
            big0.at[pl.ds(0, half_bank)],
            k.bank_sem.at[i],
        )
        for i in range(2)
    ]

    def side_of(kind):
        return SIDE_UNIT * jnp.where(
            kind == 1, 5, jnp.where(kind == 2, 7, jnp.where(kind == 3, 9, 0))
        )

    sides = [side_of(k.kinds[slot, stage, me]) for slot in range(slots)]
    ends = []
    for side in sides:
        ends.append(side * side + (ends[-1] if ends else 0))
    starts = [0, *ends[:-1]]
    rows_live = ends[-1]

    def all_areas(i, carry):
        for slot in range(slots):
            side = side_of(k.kinds[slot, stage, i])
            carry = carry + side * side
        return carry

    live_pixels = lax.fori_loop(0, batches, all_areas, 0)
    inverse_count = 1.0 / jnp.full((1, LANES), live_pixels, jnp.int32).astype(F32)[:, 0:1]

    def place(first):
        base = jnp.zeros_like(first)
        width = jnp.zeros_like(first)
        slot = jnp.full_like(first, 7)
        for number in range(slots):
            inside = (first >= starts[number]) & (first < ends[number])
            base = jnp.where(inside, starts[number], base)
            width = jnp.where(inside, sides[number], width)
            slot = jnp.where(inside, number, slot)
        return base, width, slot

    def divided(value, side):
        factor = jnp.zeros_like(side)
        for kind in (5, 7, 9):
            factor = jnp.where(side == SIDE_UNIT * kind, 65536 // (SIDE_UNIT * kind) + 1, factor)
        return lax.shift_right_logical(value * factor, jnp.full_like(value, 16))

    index = lax.broadcasted_iota(jnp.int32, (1, TABLE), 1)
    first = BLOCK * index
    base, width, slot = place(first)
    live = width > 0
    local = jnp.where(live, first - base, 0)
    row = divided(local, width)
    left = jnp.where(live, (row + 1) * width - local, BLOCK)
    begin = jnp.where(live, 4 * base + 2 * (local + row * width), 4 * first)
    jump = jnp.where(left < BLOCK, 2 * width, 0)
    window_at = lax.shift_right_logical(
        index * (65536 // per + 1), jnp.full_like(index, 16)
    ) * (4 * part) - AHEAD
    in_window = begin - jnp.maximum(window_at, 0)
    pixel = BLOCK // 4 * index
    in_base, in_width, unused_slot = place(pixel)
    in_live = in_width > 0
    in_side = jnp.maximum(in_width, 1)
    in_local = 4 * (pixel - in_base)
    in_row = divided(2 * (pixel - in_base), in_width)
    in_left = jnp.where(in_live, (2 * in_side - (in_local - in_row * 2 * in_side)) >> 1, 8)
    upper = in_row >> 1
    odd = in_row - 2 * upper
    lower = (in_row + 1) >> 1
    here = in_base + upper * in_side + (in_side - in_left)
    below = in_base + lower * in_side - in_left
    at_here = jnp.where(in_live, PAD + here + odd * (2 * plane), PAD + out_rows - BLOCK)
    at_below = jnp.where(in_left < 8, PAD + below + (1 - odd) * (2 * plane), at_here)
    even_here = jnp.where(in_live & (odd == 0), PAD + here, 0)
    even_below = jnp.where(in_live & (in_left < 8) & (odd == 1), PAD + below, 0)
    columns = (width, local, begin, left, jump, slot, 2 * width)
    columns = columns + (at_here, at_below, in_left, even_here, even_below, in_window)
    k.tabv[...] = jnp.zeros(k.tabv.shape, jnp.int32)
    for number, column in enumerate(columns):
        k.tabv[number : number + 1, :] = column
    tab_copy = pltpu.make_async_copy(k.tabv, tab, k.tab_sem)
    tab_copy.start()

    raw_copy.wait()

    def to_rows(first, last):
        def body(i, carry):
            found = []
            for u in range(16):
                at = pl.multiple_of((i * 16 + u) * LANES, LANES)
                found.append(k.raw[0:1, pl.ds(at, LANES)].astype(F32))
            for u, values in enumerate(found):
                wst[pl.ds(i * 16 + u, 1), :] = values
            return carry

        lax.fori_loop(first // 16, last // 16, body, 0)
        done = last // 16 * 16
        for at in range(done, last):
            wst[at : at + 1, :] = k.raw[0:1, at * LANES : (at + 1) * LANES].astype(F32)
        if done < last:
            wst[last : done + 16, :] = jnp.zeros((done + 16 - last, LANES), F32)

        def convert(i, carry):
            rows = pl.ds(pl.multiple_of(i * 16, 16), 16)
            wts[stage, rows, :] = wst[rows, :].astype(BF16)
            return carry

        lax.fori_loop(first // 16, -(-last // 16), convert, 0, unroll=2)

    weight_spans = ((0, EARLY), (EARLY, ROWS - EARLY))

    def send_weights(number):
        at, rows = weight_spans[number]
        region = wts.at[stage, pl.ds(at, rows)]
        copies = []
        for i in range(1, phases):
            copy = remote(
                region,
                region,
                k.weight_send.at[number, i],
                k.weight_recv.at[number, stage],
                phase_peer(i),
            )
            copy.start()
            copies.append(copy)
        return copies

    def need_weights(number, section):
        at, rows = weight_spans[number]

        @pl.when(stage != section)
        def unused_wait():
            wait_for(k.weight_recv.at[number, section], wts.at[section, pl.ds(at, rows)])

    to_rows(0, EARLY)
    pl.semaphore_wait(barrier, batches - 1 + 2 * (phases - 1))
    weight_copies = send_weights(0)

    def outgoing(number):
        if number in SPANS:
            return k.send.at[pl.ds(STARTS[number], SPANS[number])]
        return k.send_narrow.at[NARROW.index(number)]

    def incoming(number, which):
        if number in SPANS:
            return k.recv.at[which, pl.ds(STARTS[number], SPANS[number])]
        return k.recv_narrow.at[NARROW.index(number), which]

    def share(number):
        def give(i, carry):
            remote(
                outgoing(number),
                incoming(number, me),
                k.stat_send.at[number],
                k.stat_recv.at[number],
                {"batch": lax.rem(batches - 1 - me + i, batches)},
            ).start()
            return carry

        mirrored = lax.rem(2 * me + 1, batches)

        def skip(i, carry):
            return give(i + jnp.where(i >= mirrored, 1, 0), carry)

        lax.fori_loop(0, batches - 1, skip, 0, unroll=batches <= 8)
        incoming(number, me)[...] = outgoing(number)[...]

    def collect(number):
        wait_for(k.stat_recv.at[number], incoming(number, pl.ds(0, batches - 1)))

        def add(i, carry):
            return carry + incoming(number, i)[...]

        rows = SPANS.get(number, 2)
        k.total[pl.ds(0, rows), :] = lax.fori_loop(
            1, batches, add, incoming(number, 0)[...], unroll=batches <= 8
        )

    padded = [-(-rows // (16 * group)) * 16 * group for unused, rows in PIECES]
    piece_at = [sum(padded[:i]) for i in range(len(padded))]
    section_at = [0, 0, 0, 0, padded[FIRST_MID]]
    part_of = [rows // group for rows in padded]

    def summed(rows, target, *sources):
        total = sources[0](0, rows).astype(F32)
        for source in sources[1:]:
            total = total + source(0, rows).astype(F32)
        target(0, rows, total.astype(BF16))

    def reader(ref, start):
        return lambda at, step: ref[pl.ds(pl.multiple_of(start + at, 16), step), :]

    def writer(ref, start):
        def write(at, step, values):
            ref[pl.ds(pl.multiple_of(start + at, 16), step), :] = values

        return write

    def give_scatter(number):
        rows, at = part_of[number], piece_at[number]

        def give(i, carry):
            other = lax.rem(mine + i, group)
            remote(
                k.gb.at[pl.ds(at + other * rows, rows)],
                k.got_scatter.at[i - 1, pl.ds(at // group, rows)],
                k.scatter_send.at[number],
                k.scatter_recv.at[number],
                {"phase": lax.div(other, 2), "batch": 2 * line + lax.rem(other, 2)},
            ).start()
            return carry

        lax.fori_loop(1, group, give, 0)

    def give_line(number):
        rows, at = part_of[number], piece_at[number]
        within = at // group
        wait_for(k.scatter_recv.at[number], k.got_scatter.at[:, pl.ds(within, rows)])

        def other(i):
            return lambda start, step: k.got_scatter[i, pl.ds(within + start, step), :]

        summed(
            rows,
            writer(k.line_sum.at[0], within),
            reader(k.gb, at + mine * rows),
            *[other(i) for i in range(group - 1)],
        )
        send_level(number, 0)

    def level_of(level):
        size, stride = levels[level], math.prod(levels[:level])
        return size, stride, sum(levels[:level]) - level, lax.rem(lax.div(line, stride), size)

    def send_level(number, level):
        size, stride, slot, digit = level_of(level)
        rows, within = part_of[number], piece_at[number] // group

        def give(i, carry):
            other = line + (lax.rem(digit + i, size) - digit) * stride
            remote(
                k.line_sum.at[level, pl.ds(within, rows)],
                k.got_line.at[slot + i - 1, pl.ds(within, rows)],
                k.line_send.at[level, number],
                k.line_recv.at[level, number],
                {"batch": 2 * other + core},
            ).start()
            return carry

        lax.fori_loop(1, size, give, 0)

    def add_level(number, level, target):
        size, stride, slot, digit = level_of(level)
        rows, within = part_of[number], piece_at[number] // group
        arrived = k.got_line.at[pl.ds(slot, size - 1), pl.ds(within, rows)]
        wait_for(k.line_recv.at[level, number], arrived)

        own = k.line_sum[level, pl.ds(within, rows), :].astype(F32)
        total = jnp.zeros((rows, LANES), F32)
        for which in range(size):
            at = jnp.minimum(lax.rem(digit - which - 1 + size, size), size - 2)
            found = k.got_line[slot + at, pl.ds(within, rows), :].astype(F32)
            total = total + jnp.where(which == digit, own, found)
        target[pl.ds(within, rows), :] = total.astype(BF16)

    def give_home(number):
        section = PIECES[number][0]
        rows, at = part_of[number], piece_at[number]
        within = at // group
        for level in range(len(levels) - 1):
            add_level(number, level, k.line_sum.at[level + 1])
            send_level(number, level + 1)
        add_level(number, len(levels) - 1, k.home)
        target = k.got_all.at[pl.ds(section_at[number] + mine * rows, rows)]

        def give(other):
            remote(
                k.home.at[pl.ds(within, rows)],
                target,
                k.home_send.at[number],
                k.home_recv.at[number],
                {"phase": section, "batch": 2 * line + other},
            ).start()

        @pl.when(stage != section)
        def unused_both():
            give(0)
            give(1)

        @pl.when(stage == section)
        def unused_one():
            give(1 - core)
            target[...] = k.home[pl.ds(within, rows), :]

    def take_all(number):
        rows, within = part_of[number], section_at[number]

        @pl.when(stage == PIECES[number][0])
        def unused_take():
            wait_for(k.home_recv.at[number], k.got_all.at[pl.ds(within, (group - 1) * rows)])

    def end_sends(number):
        rows, at = part_of[number], piece_at[number]
        within = at // group
        wait_for(k.scatter_send.at[number], k.got_scatter.at[:, pl.ds(within, rows)])
        for level in range(len(levels)):
            size, unused_stride, slot, unused_digit = level_of(level)
            sent = k.got_line.at[pl.ds(slot, size - 1), pl.ds(within, rows)]
            wait_for(k.line_send.at[level, number], sent)

        @pl.when(stage != PIECES[number][0])
        def unused_away():
            wait_for(k.home_send.at[number], k.got_all.at[pl.ds(0, 2 * rows)])

        @pl.when(stage == PIECES[number][0])
        def unused_home():
            wait_for(k.home_send.at[number], k.got_all.at[pl.ds(0, rows)])

    def stage_piece(number):
        rows, used, at = padded[number], PIECES[number][1], piece_at[number]
        if used < rows:
            wst[used:rows, :] = jnp.zeros((rows - used, LANES), F32)

        def convert(i, carry):
            start = pl.multiple_of(i * 64, 64)
            k.gb[pl.ds(at + start, 64), :] = wst[pl.ds(start, 64), :].astype(BF16)
            return carry

        lax.fori_loop(0, rows // 64, convert, 0, unroll=2)
        give_scatter(number)

    def put_narrow(number, row, vector):
        k.send_narrow[NARROW.index(number), row : row + 1, :] = vector

    def put_wide(number, row, vectors):
        for j, vector in enumerate(vectors):
            at = STARTS[number] + 4 * row + j
            k.send[at : at + 1, :] = vector

    def put_small(row, vector):
        k.small[row : row + 1, :] = vector

    def narrow(row):
        return k.total[row : row + 1, :]

    def wide(row):
        return jnp.concatenate([k.total[4 * row + j : 4 * row + j + 1, :] for j in range(4)], axis=1)

    def reduced(values):
        return jnp.sum(values, axis=0, keepdims=True)

    def gain_narrow(row):
        return k.gains[row : row + 1, :]

    def gain_wide(row):
        return jnp.concatenate([k.gains[row + j : row + j + 1, :] for j in range(4)], axis=1)

    def put_coef(layer, what, vector):
        row = 8 * layer + what
        k.coef[row : row + 1, 0 : vector.shape[1]] = vector

    def lanes(j):
        return slice(j * LANES, (j + 1) * LANES)

    def get_coef(layer, what, j=0):
        row = 8 * layer + what
        return k.coef[row : row + 1, lanes(j)]

    def finish(layer, sums, squares, gain, bias, count_inverse):
        mean = sums * count_inverse
        inverse = lax.rsqrt(squares * count_inverse - mean * mean + EPSILON)
        scale = inverse * gain
        put_coef(layer, INVERSE, inverse)
        put_coef(layer, NEG_MEAN, -mean * inverse)
        put_coef(layer, HALF_SCALE, 0.5 * scale)
        put_coef(layer, HALF_SHIFT, 0.5 * (bias - mean * scale))

    def normed_sum(layer, sums, products, j=0):
        return products * get_coef(layer, INVERSE, j) + sums * get_coef(layer, NEG_MEAN, j)

    def finish_back(layer, sums, dots, gain, count_inverse):
        width = sums.shape[1]
        row = 8 * layer
        inverse = k.coef[row + INVERSE : row + INVERSE + 1, 0:width]
        scale = inverse * gain
        slant = scale * dots * count_inverse
        put_coef(layer, GRAD_A, scale)
        put_coef(layer, GRAD_E, slant * inverse)
        put_coef(
            layer,
            GRAD_D,
            scale * sums * count_inverse
            + slant * k.coef[row + NEG_MEAN : row + NEG_MEAN + 1, 0:width],
        )

    def put_late(stores):
        for ref, at, value in stores:
            ref[at] = value

    def each_part(body, carry=0, parts=1):
        def step(i, inner):
            stores = []
            for u in range(parts):
                inner, found = body(pl.multiple_of((i * parts + u) * part, 16), inner)
                stores = stores + found
            put_late(stores)
            return inner

        return lax.fori_loop(0, 25 // parts, step, carry, unroll=UNROLL if parts == 1 else 1)

    def each_chunk(body, carry=0):
        def step(i, inner):
            return body(pl.multiple_of(i * chunk, 16), inner)

        return lax.fori_loop(0, 5, step, carry, unroll=UNROLL)

    def each_block(body):
        def step(i, carry):
            stores = []
            for u in range(per):
                number = i * per + u
                stores = stores + body(number, pl.multiple_of(number * BLOCK, 16))
            put_late(stores)
            return carry

        lax.fori_loop(0, blocks // per, step, 0, unroll=UNROLL)

    def zeros(width=MID):
        return jnp.zeros((8, width), F32)

    def live_rows(start, rows):
        return lax.broadcasted_iota(jnp.int32, (rows, LANES), 0) + start < rows_live

    def near_rows(rows, number):
        return lax.broadcasted_iota(jnp.int32, (rows, LANES), 0) < number

    def live_block(width):
        return jnp.broadcast_to(jnp.where(width > 0, 1.0, 0.0), (BLOCK, LANES)).astype(BF16)

    def at_block(buffer, j, start, rows):
        return buffer[pl.ds(j * out_rows + start, rows), :]

    def wide_store(buffer, start, values):
        rows = values.shape[0]
        for j in range(4):
            buffer[pl.ds(j * out_rows + start, rows), :] = values[:, lanes(j)]

    def added(carry, values):
        return carry[0] + folded(values), carry[1] + folded(values * values)

    def product_sums(left, right, store, masked=False):
        width = right.shape[1]

        def body(start, carry):
            values = dense(left[pl.ds(start, chunk), :], right[...])
            store(start, values)
            if masked:
                values = jnp.where(live_rows(start, chunk), values, 0.0)
            return added(carry, values)

        return each_chunk(body, (zeros(width), zeros(width)))

    def store_narrow(target):
        def store(start, values):
            target[pl.ds(start, values.shape[0]), :] = values

        return store

    def send_narrow(number, sums):
        put_narrow(number, 0, reduced(sums[0]))
        put_narrow(number, 1, reduced(sums[1]))
        share(number)

    def by_lanes(vector):
        return [vector[:, lanes(j)] for j in range(4)]

    def stage_section(section):
        def step(i, carry):
            start = pl.multiple_of(i * (ROWS // 7), 16)
            wst[pl.ds(start, ROWS // 7), :] = wts[section, pl.ds(start, ROWS // 7), :].astype(F32)
            return carry

        lax.fori_loop(0, 7, step, 0)

    def unpack_wide(at, rows, target):
        for j in range(4):
            for r in range(rows // LANES):
                piece = wst[pl.ds(at + 4 * LANES * r + j, LANES, stride=4), :]
                target[r * LANES : (r + 1) * LANES, lanes(j)] = piece.astype(BF16)

    def take_gain(row, at, rows=1):
        k.gains[row : row + rows, :] = wst[at : at + rows, :]

    def turned(piece):
        return piece.astype(BF16).T

    def turned_rows(ref, lane=0):
        return turned(ref[:, lane * LANES : (lane + 1) * LANES])

    to_rows(EARLY, ROW)
    weight_copies = weight_copies + send_weights(1)
    for copy in feat_copies:
        copy.wait()

    need_weights(0, 0)
    def open_first(step, carry):
        start = pl.multiple_of(step * chunk, 16)
        values = dense(feat[pl.ds(start, chunk), :], wts[0, 0:CIN, :])
        t1[pl.ds(start, chunk), :] = values
        rows = lax.broadcasted_iota(jnp.int32, values.shape, 0) + start
        return added(carry, jnp.where(rows < 4 * rows_live, values, 0.0))

    sums = lax.fori_loop(0, in_rows // chunk, open_first, (zeros(), zeros()), unroll=UNROLL)
    send_narrow(0, sums)

    tab_copy.wait()
    src[0:PAD, :] = jnp.zeros((PAD, LANES), F32)
    src[PAD + out_rows : plane, :] = jnp.zeros((PAD, LANES), F32)
    for number in range(4):
        big0[number * plane : number * plane + PAD, :] = jnp.zeros((PAD, LANES), F32)

    def make_masks(number, start):
        width, local = tab[0, number], tab[1, number]
        pixel = lax.broadcasted_iota(jnp.int32, (BLOCK, LANES), 0).astype(F32) + local.astype(F32)
        side = jnp.maximum(width, 1).astype(F32)
        row = jnp.floor((pixel + 0.5) / side)
        column = pixel - row * side
        one = jnp.where(width > 0, 1.0, 0.0)
        found = (row > 0.5, row < side - 1.5, column > 0.5, column < side - 1.5)
        return [
            (
                masks,
                (which, pl.ds(start, BLOCK), slice(None)),
                jnp.where(condition, one, 0.0).astype(BF16),
            )
            for which, condition in enumerate(found)
        ]

    each_block(make_masks)
    window_rows = AHEAD + 4 * part

    def shortcut_pixels(i, carry):
        for piece in range(5):
            step = i * 5 + piece
            at = (piece % 2) * 2 * window_rows
            low = pl.multiple_of(jnp.maximum(step * 4 * part - AHEAD, 0), 16)
            for half in range(2):
                gn[at + half * window_rows : at + (half + 1) * window_rows, :] = feat[
                    pl.ds(low, window_rows), lanes(half)
                ].astype(F32)
            stores = []
            for u in range(per):
                number = step * per + u
                start = pl.multiple_of(number * BLOCK, 16)
                first = tab[12, number]
                second = first + tab[4, number]
                near = near_rows(BLOCK, tab[3, number])
                one = jnp.where(tab[0, number] > 0, 1.0, 0.0)
                for half in range(2):
                    base = at + half * window_rows
                    picked = jnp.where(
                        near,
                        gn[pl.ds(base + first, BLOCK, stride=2), :],
                        gn[pl.ds(base + second, BLOCK, stride=2), :],
                    )
                    stores.append(
                        (k.xs, (pl.ds(start, BLOCK), lanes(half)), (picked * one).astype(BF16))
                    )
            put_late(stores)
        return carry

    lax.fori_loop(0, 5, shortcut_pixels, 0)

    need_weights(1, 0)
    stage_section(0)
    take_gain(0, IN_GAIN, 2)
    take_gain(2, MID_GAIN, 2)
    k.wmid1[...] = wst[MID_AT : MID_AT + 9 * MID, :].astype(BF16)

    def first_products(block):
        rows = slice(block * out_rows, (block + 1) * out_rows)
        live = (
            lax.broadcasted_iota(jnp.int32, (out_rows, MID), 0) + block * out_rows < 4 * rows_live
        )
        k.turn[0:LANES, :] = turned(jnp.where(live, t1[rows, :], 0.0))
        live = lax.broadcasted_iota(jnp.int32, (16, out_rows), 1) + block * out_rows < 4 * rows_live
        k.turn[LANES : LANES + 16, :] = jnp.where(live, 1.0, 0.0).astype(BF16)
        found = dense(k.turn[0 : LANES + 16, :], feat[rows, :])
        for half in range(2):
            at = slice(half * LANES, (half + 1) * LANES)
            product = found[0:LANES, lanes(half)].T
            total = jnp.broadcast_to(found[LANES : LANES + 1, lanes(half)], (LANES, LANES)).T
            k.first_t[at, :] = product if block == 0 else k.first_t[at, :] + product
            k.first_s[at, :] = total if block == 0 else k.first_s[at, :] + total

    collect(0)
    finish(L1, narrow(0), narrow(1), gain_narrow(0), gain_narrow(1), 0.25 * inverse_count)

    def first_hidden(number, start):
        scale, shift = get_coef(L1, HALF_SCALE), get_coef(L1, HALF_SHIFT)
        near = near_rows(BLOCK, tab[3, number])
        stores = []
        for row in range(2):
            for column in range(2):
                first = tab[2, number] + column + (tab[6, number] if row else 0)
                values = jnp.where(
                    near,
                    t1[pl.ds(first, BLOCK, stride=2), :],
                    t1[pl.ds(first + tab[4, number], BLOCK, stride=2), :],
                )
                at = pl.ds((2 * row + column) * plane + PAD + start, BLOCK)
                stores.append((big0, (at, slice(None)), silu_half(values * scale + shift)))
        return stores

    each_block(first_hidden)

    def wide_columns(number, start):
        width = tab[0, number]
        here = pl.ds(start, BLOCK)
        top, left, live = masks[0, here, :], masks[2, here, :], live_block(width)
        corner = top * left
        stores = []
        for tap in range(9):
            i, j = tap // 3, tap % 3
            at = (2 * (0 if i == 1 else 1) + (0 if j == 1 else 1)) * plane + PAD + start
            at = at - (width if i == 0 else 0) - (1 if j == 0 else 0)
            mask = (corner if j == 0 else top) if i == 0 else (left if j == 0 else live)
            values = big0[pl.ds(at, BLOCK), :].astype(BF16) * mask
            stores.append((k.cols1, (here, lanes(tap)), values))
        return stores

    each_block(wide_columns)
    send_narrow(1, product_sums(k.cols1, k.wmid1, store_narrow(k.t2)))

    bank_copies[0].start()
    need_weights(0, 1)
    need_weights(1, 1)
    stage_section(1)
    take_gain(8, OUT_GAIN, 8)
    take_gain(16, SHORT_GAIN, 8)
    unpack_wide(0, MID, k.wout2)
    unpack_wide(AFTER_OUT, CIN, k.wshort)
    short_sums = product_sums(k.xs, k.wshort, functools.partial(wide_store, big2))
    put_wide(2, 2, by_lanes(reduced(short_sums[0])))
    put_wide(2, 3, by_lanes(reduced(short_sums[1])))

    def close_narrow(layer, source, target):
        def body(start, carry):
            half = source[pl.ds(start, part), :] * get_coef(layer, HALF_SCALE) + get_coef(
                layer, HALF_SHIFT
            )
            values = jnp.where(live_rows(start, part), silu_half(half), 0.0).astype(BF16)
            return carry, [(target, (pl.ds(start, part), slice(None)), values)]

        each_part(body, parts=5)

    first_products(0)
    collect(1)
    finish(L2, narrow(0), narrow(1), gain_narrow(2), gain_narrow(3), inverse_count)
    close_narrow(L2, k.t2, k.h2)

    roomy = hasattr(k, "slope23")

    def worked_slope(layer, values):
        return slope_half(values * get_coef(layer, HALF_SCALE) + get_coef(layer, HALF_SHIFT))

    def keep_narrow_slope(layer, source, target):
        def body(start, carry):
            here = pl.ds(start, part)
            values = worked_slope(layer, source[here, :]).astype(BF16)
            return carry, [(target, (here, slice(None)), values)]

        each_part(body, parts=5)

    def second_slope(j, start):
        if roomy:
            return k.slope23[pl.ds(start, part), lanes(j)].astype(F32)
        return slope_half(second_half(j, start))

    def keep_second_slope():
        def body(start, carry):
            return carry, [
                (
                    k.slope23,
                    (pl.ds(start, part), lanes(j)),
                    slope_half(second_half(j, start)).astype(BF16),
                )
                for j in range(4)
            ]

        if roomy:
            each_part(body)

    def keep_first_slope():
        def body(start, carry):
            return carry, [
                (
                    k.cols2,
                    (pl.ds(start, part), lanes(block)),
                    worked_slope(L1, t1[pl.ds(block * out_rows + start, part), :]).astype(BF16),
                )
                for block in range(4)
            ]

        each_part(body)

    sums = product_sums(k.h2, k.wout2, functools.partial(wide_store, big1))
    put_wide(2, 0, by_lanes(reduced(sums[0])))
    put_wide(2, 1, by_lanes(reduced(sums[1])))
    share(2)

    def bank_to_bf16(half):
        bank_copies[half].wait()

        def body(i, carry):
            start = pl.multiple_of(i * 128, 128)
            for j in range(2):
                wide2[pl.ds(start, 128), lanes(2 * half + j)] = big0[
                    pl.ds(j * (BANK // 4) + start, 128), :
                ].astype(BF16)
            return carry

        lax.fori_loop(0, BANK // 4 // 128, body, 0, unroll=4)

    need_weights(0, 2)
    need_weights(1, 2)
    stage_section(2)
    take_gain(4, THIRD_GAIN, 2)
    take_gain(6, THIRD_MID_GAIN, 2)
    k.wmid3[...] = wst[THIRD_MID : THIRD_MID + 9 * MID, :].astype(BF16)
    bank_to_bf16(0)
    bank_copies[1].start()
    first_products(1)
    collect(2)
    finish(L3, wide(0), wide(1), gain_wide(8), gain_wide(12), inverse_count)
    finish(LS, wide(2), wide(3), gain_wide(16), gain_wide(20), inverse_count)

    def second_half(j, start):
        return (
            at_block(big1, j, start, part) * get_coef(L3, HALF_SCALE, j)
            + at_block(big2, j, start, part) * get_coef(LS, HALF_SCALE, j)
            + (get_coef(L3, HALF_SHIFT, j) + get_coef(LS, HALF_SHIFT, j))
        )

    def close_second(start, carry):
        stores = []
        for j in range(4):
            values = silu_half(second_half(j, start)).astype(BF16)
            stores.append((k.y, (pl.ds(start, part), lanes(j)), values))
        return carry, stores

    each_part(close_second)

    send_narrow(3, product_sums(k.y, wts.at[2, pl.ds(0, COUT)], store_narrow(k.t4), True))
    need_weights(0, 3)
    need_weights(1, 3)
    stage_section(3)
    take_gain(24, OUT_GAIN, 8)
    unpack_wide(0, MID, k.wout4)
    bank_to_bf16(1)
    keep_second_slope()
    ones = jnp.ones((out_rows, LANES), BF16)
    for half in range(2):
        k.turn[half * LANES : (half + 1) * LANES, :] = turned_rows(k.xs, half)
    k.gram_s[...] = dense(k.turn[0:CIN, :], k.xs[...])
    k.sum_s[...] = dense(k.turn[0:CIN, :], ones)
    collect(3)
    finish(L4, narrow(0), narrow(1), gain_narrow(4), gain_narrow(5), inverse_count)

    def third_hidden(start, carry):
        half = k.t4[pl.ds(start, part), :] * get_coef(L4, HALF_SCALE) + get_coef(L4, HALF_SHIFT)
        return carry, [(src, (pl.ds(PAD + start, part), slice(None)), silu_half(half))]

    each_part(third_hidden, parts=5)

    def near_columns(number, start, target, target_start):
        width = tab[0, number]
        here = pl.ds(start, BLOCK)
        top, bottom, left, right = (masks[which, here, :] for which in range(4))
        live = live_block(width)
        stores = []
        for tap in range(9):
            i, j = tap // 3, tap % 3
            at = PAD + start + (i - 1) * width + (j - 1)
            mask = (top, live, bottom)[i]
            if j != 1:
                beside = left if j == 0 else right
                mask = beside if i == 1 else mask * beside
            values = src[pl.ds(at, BLOCK), :].astype(BF16) * mask
            stores.append((target, (pl.ds(target_start, BLOCK), lanes(tap)), values))
        return stores

    each_block(lambda number, start: near_columns(number, start, k.cols2, start))
    send_narrow(4, product_sums(k.cols2, k.wmid3, store_narrow(k.t5)))

    neg_copy.wait()
    gn[0 : 8 * LANES, :] = jnp.zeros((8 * LANES, LANES), F32)
    neg_piece = 512
    for slot in range(slots):

        def count(i, carry, slot=slot):
            at = pl.multiple_of(i * neg_piece, neg_piece)
            found = k.neg[slot, pl.ds(stage, 1), pl.ds(at, neg_piece)]
            spot = lax.broadcasted_iota(jnp.int32, (LANES, neg_piece), 0)
            upper = lax.shift_right_logical(found, 7)
            high = jnp.where(spot == upper, 1.0, 0.0).astype(BF16)
            low = jnp.where(spot == found - LANES * upper, 1.0, 0.0).astype(BF16)
            return carry + across(high, low)

        found = lax.fori_loop(
            0, NEG // neg_piece, count, jnp.zeros((LANES, LANES), F32), unroll=True
        )
        gn[pl.ds(slot, LANES, stride=8), :] = found
    first_products(2)
    k.turn[0:MID, :] = turned_rows(k.h2)
    k.gram2[...] = dense(k.turn[0:MID, :], k.h2[...])
    k.sum2[...] = dense(k.turn[0:MID, :], ones)
    collect(4)
    finish(L5, narrow(0), narrow(1), gain_narrow(6), gain_narrow(7), inverse_count)
    close_narrow(L5, k.t5, k.h4)

    sums = product_sums(k.h4, k.wout4, functools.partial(wide_store, big0))
    put_wide(5, 0, by_lanes(reduced(sums[0])))
    put_wide(5, 1, by_lanes(reduced(sums[1])))
    share(5)
    for j in range(4):
        k.wout4_t[j * LANES : (j + 1) * LANES, :] = turned(k.wout4[:, lanes(j)])
    for tap in range(9):
        k.wmid3_t[(8 - tap) * MID : (9 - tap) * MID, :] = turned(
            k.wmid3[tap * MID : (tap + 1) * MID, :]
        )
    for r in range(4):
        k.win3_t[:, lanes(r)] = turned(wts[2, r * LANES : (r + 1) * LANES, :])
    keep_narrow_slope(L5, k.t5, k.dtn)
    first_products(3)
    collect(5)
    finish(L6, wide(0), wide(1), gain_wide(24), gain_wide(28), inverse_count)

    def last_half(j, start):
        return (
            at_block(big0, j, start, part) * get_coef(L6, HALF_SCALE, j)
            + get_coef(L6, HALF_SHIFT, j)
            + 0.5 * k.y[pl.ds(start, part), lanes(j)].astype(F32)
        )

    def close_last(start, carry):
        return carry, [
            (gw, (pl.ds(start, part), lanes(j)), silu_half(last_half(j, start)).astype(BF16))
            for j in range(4)
        ]

    each_part(close_last)

    def pool(start, carry):
        rows = lax.broadcasted_iota(jnp.int32, (8, chunk), 1) + start
        owner = jnp.zeros((8, chunk), jnp.int32)
        for end in ends:
            owner = owner + jnp.where(rows >= end, 1, 0)
        mine = owner == lax.broadcasted_iota(jnp.int32, (8, chunk), 0)
        mine = jnp.where(mine, 1.0, 0.0).astype(BF16)
        return carry + dense(mine, gw[pl.ds(start, chunk), :])

    slot_row = lax.broadcasted_iota(jnp.int32, (8, LANES), 0)
    area = jnp.zeros((8, LANES), jnp.int32)
    positive = jnp.full((8, LANES), -1, jnp.int32)
    for slot in range(slots):
        area = jnp.where(slot_row == slot, sides[slot] * sides[slot], area)
        positive = jnp.where(slot_row == slot, k.positives[0, stage, slot], positive)
    inverse_area = jnp.where(area > 0, 1.0 / jnp.maximum(area, 1).astype(F32), 0.0)
    inverse_area_wide = jnp.concatenate([inverse_area] * 4, axis=1)
    half_offset = 0.5 * jnp.log(jnp.full((8, LANES), k.normalizer[0] * NEG / BANK))
    pooled = each_chunk(pool, zeros(COUT)) * inverse_area_wide

    head = wst[AFTER_OUT : AFTER_OUT + COUT, :].astype(BF16)
    pooled_high, pooled_low = split(pooled)
    embed = dense(pooled_high, head) + dense(pooled_low, head)
    scale = lax.rsqrt(jnp.sum(embed * embed, axis=1, keepdims=True) + 1e-06)
    unit = embed * scale
    unit_parts = jnp.concatenate(split(unit), axis=0)
    lane = lax.broadcasted_iota(jnp.int32, (8, LANES), 1)
    parts = []
    for block in range(4):
        scores = across(unit_parts, wide2[:, lanes(block)])
        scores = scores[0:8, :] + scores[8:16, :]
        pieces = []
        for j in range(BANK // 4 // LANES):
            high = block * (BANK // 4 // LANES) + j
            half = scores[:, lanes(j)] * (0.5 / SOFTMAX_TEMPER) - half_offset
            sigma = 0.5 + 0.5 * jnp.tanh(half)
            chosen = jnp.where(positive == lane + high * LANES, 1.0, 0.0)
            pieces.append((gn[high * 8 : high * 8 + 8, :] + chosen) * sigma - chosen)
        parts = parts + list(split(jnp.concatenate(pieces, axis=1)))
    found = dense(jnp.concatenate(parts, axis=0), wide2[...])
    unit_grad = zeros(EMB)
    for block in range(4):
        for row in (16 * block, 16 * block + 8):
            unit_grad = unit_grad + found[row : row + 8, lanes(block)]
    unit_grad = jnp.where(inverse_area > 0.0, unit_grad, 0.0) * (1.0 / SOFTMAX_TEMPER)
    embed_grad = scale * unit_grad - embed * (
        scale * scale * scale * jnp.sum(embed * unit_grad, axis=1, keepdims=True)
    )
    grad_high, grad_low = split(embed_grad)
    pooled_grad = across(grad_high, head) + across(grad_low, head)
    pooled_grad = pooled_grad * inverse_area_wide
    for j in range(4):
        k.spread[8 * j : 8 * j + 8, :] = pooled_grad[:, lanes(j)]

    def last_slope(step, carry):
        start = pl.multiple_of(step * part, 16)
        owners = [tab[5, step * per + u] for u in range(per)]
        found, stores = [], []
        for j in range(4):
            upstream = jnp.concatenate(
                [
                    jnp.broadcast_to(k.spread[pl.ds(8 * j + owner, 1), :], (BLOCK, LANES))
                    for owner in owners
                ],
                axis=0,
            )
            upstream = upstream * slope_half(last_half(j, start))
            stores.append((gw, (pl.ds(start, part), lanes(j)), upstream.astype(BF16)))
            found.append(
                (
                    carry[j][0] + folded(upstream),
                    carry[j][1] + folded(upstream * at_block(big0, j, start, part)),
                )
            )
        put_late(stores)
        return tuple(found)

    pair = (zeros(), zeros())
    sums = lax.fori_loop(0, 25, last_slope, (pair,) * 4, unroll=UNROLL)
    bias_grads = [reduced(sums[j][0]) for j in range(4)]
    gain_grads = [normed_sum(L6, bias_grads[j], reduced(sums[j][1]), j) for j in range(4)]
    put_wide(6, 0, bias_grads)
    put_wide(6, 1, gain_grads)
    share(6)
    for j in range(4):
        wst[OUT_GAIN + j : OUT_GAIN + j + 1, :] = gain_grads[j]
        wst[OUT_BIAS + j : OUT_BIAS + j + 1, :] = bias_grads[j]
    wst[AFTER_OUT : AFTER_OUT + COUT, :] = (
        outer(pooled_high, grad_high) + outer(pooled_high, grad_low) + outer(pooled_low, grad_high)
    )
    for j in range(4):
        k.wout2_t[j * LANES : (j + 1) * LANES, :] = turned(k.wout2[:, lanes(j)])
        for r in range(2):
            k.wshort_t[j * LANES : (j + 1) * LANES, lanes(r)] = turned(
                k.wshort[r * LANES : (r + 1) * LANES, lanes(j)]
            )
    def put_turned(source, target, values):
        at = (target // 2) * 4 * MID + source * MID
        k.wmid1_t[at : at + MID, lanes(target % 2)] = values

    for tap in range(9):
        i, j = tap // 3, tap % 3
        source = 2 * (1 if i == 0 else 0) + (1 if j == 0 else 0)
        target = 2 * (0 if i == 1 else 1) + (0 if j == 1 else 1)
        put_turned(source, target, turned(k.wmid1[tap * MID : (tap + 1) * MID, :]))
    for source in range(4):
        for target in range(4):
            if source & target != source:
                put_turned(source, target, jnp.zeros((MID, MID), BF16))
    collect(6)
    finish_back(L6, wide(0), wide(1), gain_wide(24), inverse_count)

    def back_value(layer, upstream, values, j=0):
        return (
            upstream * get_coef(layer, GRAD_A, j)
            - values * get_coef(layer, GRAD_E, j)
            - get_coef(layer, GRAD_D, j)
        )

    def back_sixth(start, carry):
        here = pl.ds(start, part)
        stores = []
        for j in range(4):
            values = back_value(
                L6, gw[here, lanes(j)].astype(F32), at_block(big0, j, start, part), j
            )
            stores.append((wide2, (here, lanes(j)), values.astype(BF16)))
        return carry, stores

    each_part(back_sixth)

    def back_rows(values, slope):
        def body(start, carry):
            here = pl.ds(start, part)
            upstream = gn[here, :] * slope[here, :].astype(F32)
            upstream = jnp.where(live_rows(start, part), upstream, 0.0)
            carry = (carry[0] + folded(upstream), carry[1] + folded(upstream * values[here, :]))
            return carry, [(gn, (here, slice(None)), upstream)]

        return each_part(body, (zeros(), zeros()), parts=5)

    def send_back(number, row, layer, sums):
        bias_grad = reduced(sums[0])
        gain_grad = normed_sum(layer, bias_grad, reduced(sums[1]))
        put_narrow(number, 0, bias_grad)
        put_narrow(number, 1, gain_grad)
        share(number)
        put_small(row, gain_grad)
        put_small(row + 1, bias_grad)

    def rounded_product(left, right):
        def body(start, carry):
            here = pl.ds(start, chunk)
            gn[here, :] = dense(left[here, :], right[...]).astype(BF16).astype(F32)
            return carry

        each_chunk(body)

    rounded_product(wide2, k.wout4_t)
    send_back(7, 2, L5, back_rows(k.t5, k.dtn))

    def put_wide_matrix(at, values):
        for r in range(values.shape[0] // LANES):
            for j in range(4):
                wst[pl.ds(at + 4 * LANES * r + j, LANES, stride=4), :] = values[
                    r * LANES : (r + 1) * LANES, lanes(j)
                ]

    k.turn[0:LANES, :] = turned_rows(k.h4)
    put_wide_matrix(0, dense(k.turn[0:LANES, :], wide2[0:out_rows, :]))
    stage_piece(LAST)
    keep_narrow_slope(L4, k.t4, k.h4)
    collect(7)
    finish_back(L5, narrow(0), narrow(1), gain_narrow(6), inverse_count)

    def back_close(layer, values):
        def body(start, carry):
            here = pl.ds(start, part)
            found = back_value(layer, gn[here, :], values[here, :])
            found = jnp.where(live_rows(start, part), found, 0.0).astype(BF16)
            return carry, [
                (k.dtn, (here, slice(None)), found),
                (src, (pl.ds(PAD + start, part), slice(None)), found.astype(F32)),
            ]

        each_part(body, parts=5)

    back_close(L5, k.t5)

    def open_back_fourth(step, carry):
        chunk_start = pl.multiple_of(step * chunk, 16)

        def fill(i, inner):
            stores = []
            for u in range(per):
                at = pl.multiple_of((i * per + u) * BLOCK, 16)
                number = step * (chunk // BLOCK) + i * per + u
                stores = stores + near_columns(number, chunk_start + at, k.colt, at)
            put_late(stores)
            return inner

        lax.fori_loop(0, chunk // BLOCK // per, fill, 0, unroll=UNROLL)
        gn[pl.ds(chunk_start, chunk), :] = dense(k.colt[...], k.wmid3_t[...])
        return carry

    lax.fori_loop(0, 5, open_back_fourth, 0, unroll=UNROLL)
    send_back(8, 0, L4, back_rows(k.t4, k.h4))

    def columns_grad(columns, store):
        k.turn[0:LANES, :] = turned_rows(k.dtn)
        for group in range(3):
            found = dense(k.turn[0:LANES, :], columns[:, 3 * group * LANES : 3 * (group + 1) * LANES])
            for j in range(3):
                store(3 * group + j, found[:, lanes(j)].T)

    def store_third(tap, values):
        wst[THIRD_MID + tap * MID : THIRD_MID + (tap + 1) * MID, :] = values

    columns_grad(k.cols2, store_third)
    give_line(LAST)
    keep_narrow_slope(L2, k.t2, k.h4)
    collect(8)
    finish_back(L4, narrow(0), narrow(1), gain_narrow(4), inverse_count)
    back_close(L4, k.t4)

    def back_block(start, carry):
        here = pl.ds(start, part)
        arrived = dense(k.dtn[here, :], k.win3_t[...])
        found, stores = [], []
        for j in range(4):
            upstream = arrived[:, lanes(j)] + gw[here, lanes(j)].astype(F32)
            upstream = upstream.astype(BF16).astype(F32) * second_slope(j, start)
            stores.append((gw, (here, lanes(j)), upstream.astype(BF16)))
            found.append(
                (
                    carry[j][0] + folded(upstream),
                    carry[j][1] + folded(upstream * at_block(big1, j, start, part)),
                    carry[j][2] + folded(upstream * at_block(big2, j, start, part)),
                )
            )
        return tuple(found), stores

    sums = each_part(back_block, ((zeros(), zeros(), zeros()),) * 4)
    bias_grads, gain_grads, short_grads = (
        [reduced(sums[j][which]) for j in range(4)] for which in range(3)
    )
    gain_grads = [normed_sum(L3, bias_grads[j], gain_grads[j], j) for j in range(4)]
    short_grads = [normed_sum(LS, bias_grads[j], short_grads[j], j) for j in range(4)]
    put_wide(9, 0, bias_grads)
    put_wide(9, 1, gain_grads)
    put_wide(9, 2, short_grads)
    share(9)
    k.turn[0:LANES, :] = turned_rows(k.dtn)
    found = dense(k.turn[0:LANES, :], k.y[...])
    for j in range(4):
        wst[j * LANES : (j + 1) * LANES, :] = found[:, lanes(j)].T
    wst[THIRD_GAIN : THIRD_BIAS + 1, :] = k.small[0:2, :]
    wst[THIRD_MID_GAIN : THIRD_MID_BIAS + 1, :] = k.small[2:4, :]
    stage_piece(THIRD)
    k.turn[0:MID, :] = turned_rows(k.h2)
    for half in range(2):
        k.turn[MID + half * LANES : MID + (half + 1) * LANES, :] = turned_rows(k.xs, half)
    for pair in range(2):
        found = dense(k.turn[0 : MID + CIN, :], gw[:, 2 * pair * LANES : 2 * (pair + 1) * LANES])
        for r, at in enumerate((0, AFTER_OUT, AFTER_OUT + 4 * LANES)):
            for j in range(2):
                wst[pl.ds(at + 2 * pair + j, LANES, stride=4), :] = found[
                    r * LANES : (r + 1) * LANES, lanes(j)
                ]
    give_home(LAST)
    collect(9)
    finish_back(L3, wide(0), wide(1), gain_wide(8), inverse_count)
    finish_back(LS, wide(0), wide(2), gain_wide(16), inverse_count)

    def back_third(start, carry):
        here = pl.ds(start, part)
        below = pl.ds(out_rows + start, part)
        stores = []
        for j in range(4):
            upstream = gw[here, lanes(j)].astype(F32)
            found = back_value(L3, upstream, at_block(big1, j, start, part), j)
            stores.append((wide2, (here, lanes(j)), found.astype(BF16)))
            found = back_value(LS, upstream, at_block(big2, j, start, part), j)
            stores.append((wide2, (below, lanes(j)), found.astype(BF16)))
        return carry, stores

    each_part(back_third)
    rounded_product(wide2, k.wout2_t)
    send_back(10, 6, L2, back_rows(k.t2, k.h4))
    for j in range(4):
        wst[OUT_GAIN + j : OUT_GAIN + j + 1, :] = gain_grads[j]
        wst[OUT_BIAS + j : OUT_BIAS + j + 1, :] = bias_grads[j]
        wst[SHORT_GAIN + j : SHORT_GAIN + j + 1, :] = short_grads[j]
        wst[SHORT_BIAS + j : SHORT_BIAS + j + 1, :] = bias_grads[j]

    def by_linearity(at, layer, products, sums):
        for j in range(4):
            rows = pl.ds(at + j, LANES, stride=4)
            wst[rows, :] = (
                wst[rows, :] * get_coef(layer, GRAD_A, j)
                - products[:, lanes(j)] * get_coef(layer, GRAD_E, j)
                - sums * get_coef(layer, GRAD_D, j)
            )

    high, low = split(k.gram2[...])
    by_linearity(0, L3, dense(high, k.wout2[...]) + dense(low, k.wout2[...]), k.sum2[...])
    high, low = split(k.gram_s[...])
    products = dense(high, k.wshort[...]) + dense(low, k.wshort[...])
    for half in range(2):
        rows = slice(half * LANES, (half + 1) * LANES)
        by_linearity(AFTER_OUT + half * 4 * LANES, LS, products[rows, :], k.sum_s[rows, :])
    stage_piece(SECOND)
    give_line(THIRD)

    def back_picked(start, carry):
        found = dense(wide2[pl.ds(out_rows + start, chunk), :], k.wshort_t[...])
        found = found.astype(BF16).astype(F32)
        for half in range(2):
            big2[pl.ds(half * plane + PAD + start, chunk), :] = found[:, lanes(half)]
        return carry

    each_chunk(back_picked)
    for half in range(2):
        big2[half * plane : half * plane + PAD, :] = jnp.zeros((PAD, LANES), F32)
    keep_first_slope()
    collect(10)
    finish_back(L2, narrow(0), narrow(1), gain_narrow(2), inverse_count)
    back_close(L2, k.t2)


    def back_columns(number, start):
        here = pl.ds(start, BLOCK)
        width = tab[0, number]
        bottom, right, live = masks[1, here, :], masks[3, here, :], live_block(width)
        shifts = ((0, live), (1, right), (width, bottom), (width + 1, bottom * right))
        return [
            (
                wide2,
                (here, lanes(which)),
                src[pl.ds(PAD + start + shift, BLOCK), :].astype(BF16) * mask,
            )
            for which, (shift, mask) in enumerate(shifts)
        ]

    each_block(back_columns)

    def back_planes(start, carry):
        here = pl.ds(start, chunk)
        even = dense(wide2[here, 0 : 2 * MID], k.wmid1_t[0 : 2 * MID, :])
        odd = dense(wide2[here, :], k.wmid1_t[4 * MID : 8 * MID, :])
        for number in range(4):
            found = (even, odd)[number // 2][:, lanes(number % 2)]
            big0[pl.ds(number * plane + PAD + start, chunk), :] = found
        return carry

    each_chunk(back_planes)

    in_unroll = 10

    def to_input_order(i, carry):
        stores = []
        for u in range(in_unroll):
            number = i * in_unroll + u
            first, second = tab[7, number], tab[8, number]
            near = near_rows(8, tab[9, number])
            for column in range(2):
                values = jnp.where(
                    near,
                    big0[pl.ds(first + column * plane, 8), :],
                    big0[pl.ds(second + column * plane, 8), :],
                )
                at = pl.ds(number * BLOCK + column, 8, stride=2)
                stores.append((big1, (at, slice(None)), values))
        put_late(stores)
        return carry

    lax.fori_loop(0, in_rows // BLOCK // in_unroll, to_input_order, 0, unroll=UNROLL)

    def back_first(start, carry):
        stores = []
        for block in range(4):
            rows = pl.ds(block * out_rows + start, part)
            upstream = big1[rows, :] * k.cols2[pl.ds(start, part), lanes(block)].astype(F32)
            carry = (carry[0] + folded(upstream), carry[1] + folded(upstream * t1[rows, :]))
            stores.append((big1, (rows, slice(None)), upstream))
        return carry, stores

    sums = each_part(back_first, (zeros(), zeros()))
    send_back(11, 4, L1, sums)
    def store_first(tap, values):
        at = piece_at[FIRST_MID] + tap * MID
        k.gb[at : at + MID, :] = values.astype(BF16)

    columns_grad(k.cols1, store_first)
    if padded[FIRST_MID] > 9 * MID:
        at = piece_at[FIRST_MID]
        k.gb[at + 9 * MID : at + padded[FIRST_MID], :] = jnp.zeros(
            (padded[FIRST_MID] - 9 * MID, LANES), BF16
        )
    give_scatter(FIRST_MID)
    give_line(SECOND)
    give_home(THIRD)

    found = jnp.zeros((MID, CIN), F32)
    for block in range(4):
        rows = slice(block * out_rows, (block + 1) * out_rows)
        k.turn[0:LANES, :] = turned(big1[rows, :])
        found = found + dense(k.turn[0:LANES, :], feat[rows, :])
    first_g = [found[:, lanes(half)].T for half in range(2)]
    for half in range(2):
        k.win1_t[:, lanes(half)] = turned(wts[0, half * LANES : (half + 1) * LANES, :])
    gn[...] = jnp.zeros(gn.shape, F32)
    collect(11)
    finish_back(L1, narrow(0), narrow(1), gain_narrow(0), 0.25 * inverse_count)

    at = piece_at[FIRST_IN]
    for half in range(2):
        rows = slice(half * LANES, (half + 1) * LANES)
        values = first_g[half] * get_coef(L1, GRAD_A) - k.first_t[rows, :] * get_coef(L1, GRAD_E)
        values = values - k.first_s[rows, :] * get_coef(L1, GRAD_D)
        k.gb[at + half * LANES : at + (half + 1) * LANES, :] = values.astype(BF16)
    k.gb[at + CIN : at + CIN + 16, :] = jnp.concatenate(
        [k.small[4:8, :], jnp.zeros((12, LANES), F32)], axis=0
    ).astype(BF16)
    k.gb[at + CIN + 16 : at + padded[FIRST_IN], :] = jnp.zeros(
        (padded[FIRST_IN] - CIN - 16, LANES), BF16
    )
    give_scatter(FIRST_IN)
    give_line(FIRST_MID)
    give_home(SECOND)

    for block in range(4):

        def close_back_first(start, carry, block=block):
            rows = pl.ds(block * out_rows + start, part)
            found = back_value(L1, big1[rows, :], t1[rows, :])
            row = lax.broadcasted_iota(jnp.int32, (part, MID), 0) + (block * out_rows + start)
            found = jnp.where(row < 4 * rows_live, found, 0.0).astype(BF16)
            return carry, [(gw, (pl.ds(start, part), lanes(block)), found)]

        each_part(close_back_first, parts=5)

    give_line(FIRST_IN)
    give_home(FIRST_MID)


    def ordered(target, source, rows):
        def body(i, carry):
            start = pl.multiple_of(i * 64, 64)
            wst[pl.ds(target + start, 64), :] = k.got_all[pl.ds(source + start, 64), :].astype(F32)
            return carry

        lax.fori_loop(0, rows // 64, body, 0, unroll=2)

    def blank(at):
        wst[at:ROWS, :] = jnp.zeros((ROWS - at, LANES), F32)

    def input_grad(block, carry):
        lane = pl.ds(pl.multiple_of(block * LANES, LANES), LANES)
        for piece in range(5):
            low = (piece % 2) * 2 * chunk
            stores = []
            for u in range(chunk // BLOCK):
                number = (block * 5 + piece) * (chunk // BLOCK) + u
                near = near_rows(8, tab[9, number])
                for half in range(2):
                    values = jnp.where(
                        near,
                        big2[pl.ds(tab[10, number] + half * plane, 8), :],
                        big2[pl.ds(tab[11, number] + half * plane, 8), :],
                    )
                    at = low + half * chunk + u * BLOCK
                    stores.append((gn, (slice(at, at + BLOCK, 2), slice(None)), values))
            put_late(stores)
            found = dense(gw[piece * chunk : (piece + 1) * chunk, lane], k.win1_t[...])
            rows = pl.ds(pl.multiple_of(block * out_rows + piece * chunk, 16), chunk)
            for half in range(2):
                at = low + half * chunk
                feat[rows, lanes(half)] = (found[:, lanes(half)] + gn[at : at + chunk, :]).astype(
                    BF16
                )
        return carry

    lax.fori_loop(0, 2, input_grad, 0)
    give_home(FIRST_IN)
    take_all(FIRST_MID)

    @pl.when(stage == 0)
    def unused_first_mid():
        blank(MID_BIAS + 1)
        ordered(MID_AT, 0, 9 * MID)

    lax.fori_loop(2, 4, input_grad, 0)
    input_copy = pltpu.make_async_copy(feat, k.input_grad_at, k.out_sem.at[0])
    input_copy.start()

    for number in (LAST, THIRD, SECOND, FIRST_IN):
        take_all(number)

    for number in (LAST, THIRD, SECOND):

        @pl.when(stage == PIECES[number][0])
        def unused_ordered(number=number):
            rows = min(padded[number], ROWS // 128 * 128)
            if rows < ROWS:
                blank(rows)
            ordered(0, 0, rows)
            if rows < PIECES[number][1]:
                tail = k.got_all[rows : rows + 16, :].astype(F32)
                wst[rows : rows + 16, :] = tail

    @pl.when(stage == 0)
    def unused_first():
        at = section_at[FIRST_IN]
        ordered(0, at, CIN)
        gains = k.got_all[at + CIN : at + CIN + 16, :].astype(F32)
        wst[IN_GAIN : IN_BIAS + 1, :] = gains[0:2, :]
        wst[MID_GAIN : MID_BIAS + 1, :] = gains[2:4, :]

    out_copy = pltpu.make_async_copy(wst.at[pl.ds(0, ROWS)], k.weight_grads_at, k.grad_sem)
    out_copy.start()
    input_copy.wait()
    for copy in weight_copies:
        copy.wait_send()
    for number in range(EXCHANGES):
        wait_for(k.stat_send.at[number], incoming(number, pl.ds(0, batches - 1)))
    for number in range(len(PIECES)):
        end_sends(number)
    out_copy.wait()


def write_kernel(weight_rows, input_rows, weight_out, input_out, held_weights, held, sems):
    count = 10
    part = input_rows.shape[0] // count
    pairs = [
        (weight_rows.at[pl.ds(0, ROW)], held_weights, weight_out.reshape(ROW, LANES)),
        *[
            (input_rows.at[rows], held.at[rows], input_out.at[rows])
            for rows in [pl.ds(i * part, part) for i in range(count)]
        ],
    ]
    arriving = [
        pltpu.make_async_copy(source, middle, sems.at[0, i])
        for i, (source, middle, target) in enumerate(pairs)
    ]
    leaving = [
        pltpu.make_async_copy(middle, target, sems.at[1, i])
        for i, (source, middle, target) in enumerate(pairs)
    ]
    for copy in arriving:
        copy.start()
    for i in range(len(pairs)):
        arriving[i].wait()
        leaving[i].start()
    for copy in leaving:
        copy.wait()


def shards(features, weights, crop_kind, positives, negatives, bank, normalizer):
    phases = lax.axis_size("phase")
    batches = lax.axis_size("batch")
    in_rows = features.shape[0] // MICRO
    out_rows = in_rows // 4
    plane = out_rows + 2 * PAD
    slots = crop_kind.shape[2]
    chunk = out_rows // 5
    part = out_rows // 25
    group = 2 * phases
    levels = line_levels(batches // 2)
    padded = [-(-rows // (16 * group)) * 16 * group for unused, rows in PIECES]
    widest = max(*padded[:3], padded[3] + padded[4])
    eighth = sum(padded) // group
    staged = max(ROWS, *padded[:3])
    any_space = pl.BlockSpec(memory_space=pl.ANY)
    smem = pl.BlockSpec(memory_space=pltpu.SMEM)

    def held(*shape, dtype=F32):
        return pltpu.VMEM(shape, dtype)

    def sems(*shape):
        return pltpu.SemaphoreType.DMA(shape)

    def low(*shape):
        return held(*shape, dtype=BF16)

    kept_slopes = {"slope23": low(out_rows, COUT)} if batches <= 8 else {}

    inputs = {
        "features_at": (features, any_space),
        "weights_at": (weights, any_space),
        "negatives_at": (jnp.transpose(negatives, (0, 2, 1, 3)), any_space),
        "bank_at": (bank, any_space),
        "kinds": (jnp.transpose(crop_kind, (2, 1, 0)), smem),
        "positives": (positives, smem),
        "normalizer": (normalizer, smem),
    }
    outputs = {
        "weight_grads_at": jax.ShapeDtypeStruct((ROWS, LANES), F32),
        "input_grad_at": jax.ShapeDtypeStruct((in_rows, CIN), BF16),
    }
    scratch = {
        "feat": low(in_rows, CIN),
        "t1": held(in_rows, MID),
        "big0": held(4 * plane, MID),
        "big1": held(in_rows, MID),
        "big2": held(4 * plane, MID),
        "cols1": low(out_rows, 9 * MID),
        "cols2": low(out_rows, 9 * MID),
        "colt": low(chunk, 9 * MID),
        "src": held(plane, MID),
        "t2": held(out_rows, MID),
        "t4": held(out_rows, MID),
        "t5": held(out_rows, MID),
        "gn": held(out_rows, MID),
        "h2": low(out_rows, MID),
        "h4": low(out_rows, MID),
        "xs": low(out_rows, CIN),
        "y": low(out_rows, COUT),
        "gw": low(out_rows, COUT),
        "wide2": low(BANK // 4, COUT),
        "dtn": low(out_rows, MID),
        "turn": low(MID + CIN, out_rows),
        "gram2": held(MID, MID),
        "gram_s": held(CIN, CIN),
        "sum2": held(MID, LANES),
        "sum_s": held(CIN, LANES),
        "first_t": held(CIN, MID),
        "first_s": held(CIN, MID),
        "masks": low(4, out_rows, LANES),
        "raw": low(1, GRAD_LEN),
        "wts": low(phases, ROWS, LANES),
        "wst": held(staged, LANES),
        "wmid1": low(9 * MID, MID),
        "wmid3": low(9 * MID, MID),
        "wout2": low(MID, COUT),
        "wshort": low(CIN, COUT),
        "wout4": low(MID, COUT),
        "wout2_t": low(COUT, MID),
        "wshort_t": low(COUT, CIN),
        "wout4_t": low(COUT, MID),
        "wmid1_t": low(8 * MID, 2 * MID),
        "wmid3_t": low(9 * MID, MID),
        "win1_t": low(MID, CIN),
        "win3_t": low(MID, COUT),
        "gains": held(32, LANES),
        "small": held(8, LANES),
        "coef": held(56, COUT),
        "spread": held(32, LANES),
        "neg": held(slots, MICRO, NEG, dtype=jnp.int32),
        **kept_slopes,
        "tabv": held(16, TABLE, dtype=jnp.int32),
        "tab": pltpu.SMEM((16, TABLE), jnp.int32),
        "send": held(SPAN_ROWS, LANES),
        "send_narrow": held(len(NARROW), 2, LANES),
        "recv_narrow": held(len(NARROW), batches, 2, LANES),
        "recv": held(batches, SPAN_ROWS, LANES),
        "total": held(16, LANES),
        "gb": low(sum(padded), LANES),
        "got_scatter": low(group - 1, eighth, LANES),
        "line_sum": low(len(levels), eighth, LANES),
        "got_line": low(sum(levels) - len(levels), eighth, LANES),
        "home": low(eighth, LANES),
        "got_all": low(widest, LANES),
        "raw_sem": pltpu.SemaphoreType.DMA,
        "feat_sem": sems(4),
        "bank_sem": sems(2),
        "neg_sem": pltpu.SemaphoreType.DMA,
        "tab_sem": pltpu.SemaphoreType.DMA,
        "weight_send": sems(2, phases),
        "weight_recv": sems(2, phases),
        "stat_send": sems(EXCHANGES),
        "stat_recv": sems(EXCHANGES),
        "scatter_send": sems(len(PIECES)),
        "scatter_recv": sems(len(PIECES)),
        "line_send": sems(len(levels), len(PIECES)),
        "line_recv": sems(len(levels), len(PIECES)),
        "home_send": sems(len(PIECES)),
        "home_recv": sems(len(PIECES)),
        "out_sem": sems(4),
        "grad_sem": pltpu.SemaphoreType.DMA,
    }
    names = (*inputs, *outputs, *scratch)
    weight_rows, input_rows = pl.pallas_call(
        functools.partial(kernel, names, batches, phases, in_rows, slots),
        out_shape=tuple(outputs.values()),
        in_specs=[spec for unused, spec in inputs.values()],
        out_specs=(any_space,) * len(outputs),
        scratch_shapes=list(scratch.values()),
        compiler_params=pltpu.CompilerParams(
            collective_id=0, has_side_effects=True, vmem_limit_bytes=64 * 1024 * 1024
        ),
    )(*[value for value, unused in inputs.values()])
    weight_grads, input_grad = pl.pallas_call(
        write_kernel,
        out_shape=(
            jax.ShapeDtypeStruct((1, GRAD_LEN), F32),
            jax.ShapeDtypeStruct((in_rows, CIN), BF16),
        ),
        in_specs=[any_space, any_space],
        out_specs=(any_space, any_space),
        scratch_shapes=[held(ROW, LANES), low(in_rows, CIN), sems(2, 11)],
        compiler_params=pltpu.CompilerParams(vmem_limit_bytes=64 * 1024 * 1024),
    )(weight_rows, input_rows)
    return (weight_grads, input_grad)


def solution(mesh):
    placed = (
        P("batch", None),
        P("phase", None),
        P(),
        P("batch", None, None),
        P("batch", None, None, None),
        P(),
        P(),
    )
    return jax.shard_map(
        shards,
        mesh=mesh,
        in_specs=placed,
        out_specs=(P("phase", None), P(("batch", "phase"), None)),
        check_vma=False,
    )
```
